32 devices in a mesh: seq: 16 (over z, x, core), head: 2 (over y).
Axes of the slice: x: 2, y: 2, z: 4, core: 2. Of those that a mesh axis runs over, the one named last changes fastest.
Arguments:
- tokens: bfloat16 [2048, 4096], P('seq', 'head')
- gain: float32 [4096], replicated, may hold values from 0.25 to 1.75
- w_query: bfloat16 [4096, 2048], P('seq', 'head'), may hold values from -0.09375 to 0.09375
- w_key: bfloat16 [4096, 2048], P('seq', 'head'), may hold values from -0.09375 to 0.09375
- w_value: bfloat16 [4096, 2048], P('seq', 'head'), may hold values from -0.09375 to 0.09375
- w_out: bfloat16 [2048, 4096], P('head', 'seq'), may hold values from -0.125 to 0.125
- mem_query: bfloat16 [128, 2048], P(None, 'head'), may hold values from -12 to 12
- score_scale: float32 [16], P('head'), may hold values from 1.5 to 4
- decay: float32 [16, 16], P('seq', 'head'), may hold values from 0 to 1, as said below
- seg_len: int32 [16], P('seq'), may hold values from 32 to 128, as said below
Outputs:
- branch: bfloat16 [2048, 4096], P('seq', 'head')
The draws below stay inside these ranges and needn't reach their ends.
Inputs may be any that keep to these rules, and one draw needn't show every extreme that they name: `decay`: retention lies strictly between 0 and 1. `seg_len`: at least one segment is full and at least one holds exactly 32 valid tokens.
All inputs are finite; a program needn't handle non-finite values.
Results may differ from the reference program's by a relative error of at most 0.015.
Values may be sent and summed in bfloat16 or wider, within the bound.
No kernel may reach another device: no remote copies, remote signals or barrier semaphores. Data moves between devices by JAX's collectives and lax.ppermute only.
A program may use at most 64 MiB of HBM per device.

```python
import math
import jax
import jax.numpy as jnp
from jax import lax

D = 4096
HEADS = 16
DH = 128
MEMORY_ROWS = 128
SEG = 128
LOG_PART_TOTAL = 16
TOKENS = 2048
HD = 2048
N_HEAD = 2


def draw_tokens(key, part):
    key_base, key_rows, key_cols = jax.random.split(key, 3)
    row_scale = jnp.exp(jax.random.uniform(key_rows, (TOKENS, 1), jnp.float32) * math.log(10.0))
    ramp = 1.0 + 2.0 * jnp.arange(D, dtype=jnp.float32)[None, :] / D
    col_scale = jnp.exp(jax.random.uniform(key_cols, (1, D), jnp.float32) * math.log(10.0)) * ramp
    base = jax.random.normal(key_base, (TOKENS, D), jnp.float32)
    return (base * row_scale * col_scale / 5.0).astype(jnp.bfloat16)


def draw_decay(key, part):
    selection_seed_stream, gradual_seed_stream, quick_seed_stream, multiplier_seed_stream, spike_seed_stream, threshold_seed_stream = jax.random.split(key, 6)
    share = 0.5
    gradual_sample = jax.random.uniform(selection_seed_stream, (HEADS,), jnp.float32) < share
    slow_rate = jnp.exp(jax.random.uniform(gradual_seed_stream, (HEADS,), jnp.float32, math.log(0.05), math.log(0.5))) / LOG_PART_TOTAL
    fast_rate = jnp.exp(jax.random.uniform(quick_seed_stream, (HEADS,), jnp.float32, math.log(1.5), math.log(4.0)))
    rate = jnp.where(gradual_sample, slow_rate, fast_rate)
    factor = jnp.exp(jax.random.uniform(multiplier_seed_stream, (LOG_PART_TOTAL, HEADS), jnp.float32, math.log(0.5), math.log(2.0)))
    selected_places = jax.random.randint(spike_seed_stream, (2,), 0, LOG_PART_TOTAL)
    spike_sample = jnp.zeros((LOG_PART_TOTAL,), jnp.float32).at[selected_places].set(1.0)
    cut = jax.random.uniform(threshold_seed_stream, (LOG_PART_TOTAL, HEADS), jnp.float32, 0.6, 0.8)
    match_indicator = (spike_sample[:, None] > 0.5) & gradual_sample[None, :]
    retain = jnp.exp(-rate[None, :] * factor) * jnp.where(match_indicator, cut, 1.0)
    return retain.astype(jnp.float32)


def draw_seg_len(key, part):
    key_len, key_first, key_second = jax.random.split(key, 3)
    lens = jax.random.randint(key_len, (LOG_PART_TOTAL,), SEG // 4, SEG + 1)
    first = jax.random.randint(key_first, (), 0, LOG_PART_TOTAL)
    second = (first + 1 + jax.random.randint(key_second, (), 0, LOG_PART_TOTAL - 1)) % LOG_PART_TOTAL
    lens = lens.at[first].set(SEG)
    lens = lens.at[second].set(SEG // 4)
    return lens.astype(jnp.int32)


def steps_of(stream_key, dims, shards, low, high):
    factor_of = 1.0
    for dim, blocks in shards:
        draws = jax.random.uniform(jax.random.fold_in(jax.random.fold_in(stream_key, 6), dim), (blocks,), jnp.float32, low / len(shards), high / len(shards))
        factor_of = factor_of * jnp.repeat(jnp.exp(draws), dims[dim] // blocks).reshape((-1,) + (1,) * (len(dims) - 1 - dim))
    return factor_of


def centred(own_key, dims, deviation, limit, cuts=(), held_as=jnp.bfloat16):
    values = deviation * jax.random.normal(own_key, dims, jnp.float32)
    if cuts:
        values = values * steps_of(own_key, dims, cuts, -0.22, 0.18)
    return jnp.clip(values, -limit, limit).astype(held_as)


def setup_inputs(seed: int = 0) -> dict:
    key_list = jax.random.split(jax.random.key(seed), 11)
    return {
        "tokens": draw_tokens(jax.random.fold_in(key_list[10], 71), 0),
        "gain": jnp.clip(1.0 + 0.15 * jax.random.normal(key_list[1], (D,), jnp.float32), 0.25, 1.75),
        "w_query": centred(key_list[2], (D, HD), D ** -0.5, 0.09375, ((0, 16), (1, 2))),
        "w_key": centred(key_list[3], (D, HD), D ** -0.5, 0.09375, ((0, 16), (1, 2))),
        "w_value": centred(key_list[4], (D, HD), D ** -0.5, 0.09375, ((0, 16), (1, 2))),
        "w_out": centred(key_list[5], (HD, D), HD ** -0.5, 0.125, ((0, 2), (1, 16))),
        "mem_query": centred(key_list[6], (MEMORY_ROWS, HD), 2.5, 12.0, ((1, 2),)),
        "score_scale": jnp.clip(jnp.exp(math.log(4.0) - 0.98082925 * jax.random.uniform(key_list[7], (HEADS,), jnp.float32) ** steps_of(key_list[7], (HEADS,), ((0, 2),), -0.2, 0.2)), 1.5, 4.0),
        "decay": draw_decay(jax.random.fold_in(key_list[10], 71), 0),
        "seg_len": draw_seg_len(jax.random.fold_in(key_list[10], 71), 0),
    }


def unit_rows(field):
    return field * lax.rsqrt(lax.optimization_barrier(jnp.mean(jnp.square(field), axis=-1, keepdims=True)) + 1e-06)

def rounded(field):
    return lax.optimization_barrier(field.astype(jnp.bfloat16)).astype(jnp.float32)

def reference(tokens, gain, w_query, w_key, w_value, w_out, mem_query, score_scale, decay, seg_len):
    head_columns = HEADS * DH
    group_cols = head_columns // N_HEAD
    inverse_root_scale = 1.0 / math.sqrt(DH)
    score_bias = math.log(MEMORY_ROWS + SEG)
    positions = jnp.arange(SEG, dtype=jnp.int32)
    causal = (positions[None, :] <= positions[:, None]).astype(jnp.float32)
    memory_head_split = mem_query.astype(jnp.float32).reshape(MEMORY_ROWS, HEADS, DH)
    head_scale_factors = (score_scale * inverse_root_scale)[:, None, None]
    out_groups = w_out.astype(jnp.float32).reshape(N_HEAD, group_cols, D)

    def segment(memory, inputs):
        block, retain, valid_len = inputs
        wide = block.astype(jnp.float32)
        normed = (wide * lax.rsqrt(lax.optimization_barrier(jnp.mean(wide * wide, axis=1, keepdims=True)) + 1e-05) * gain).astype(jnp.bfloat16)
        query = jnp.dot(normed, w_query, preferred_element_type=jnp.float32).astype(jnp.bfloat16)
        keys = jnp.dot(normed, w_key, preferred_element_type=jnp.float32).astype(jnp.bfloat16)
        values = jnp.dot(normed, w_value, preferred_element_type=jnp.float32).astype(jnp.bfloat16)
        query_head_split = query.astype(jnp.float32).reshape(SEG, HEADS, DH)
        key_head_split = keys.astype(jnp.float32).reshape(SEG, HEADS, DH)
        value_head_split = values.astype(jnp.float32).reshape(SEG, HEADS, DH)
        valid_keys = (positions < valid_len).astype(jnp.float32)
        memory_write_scores = jnp.einsum('bia,sia->ibs', memory_head_split, key_head_split) * inverse_root_scale
        memory_write_weights = rounded(jax.nn.sigmoid(memory_write_scores - math.log(SEG)) * valid_keys[None, None, :])
        memory_written_keys = jnp.einsum('elz,zek->lek', memory_write_weights, key_head_split).reshape(MEMORY_ROWS, head_columns)
        memory_written_values = jnp.einsum('elz,zek->lek', memory_write_weights, value_head_split).reshape(MEMORY_ROWS, head_columns)
        written = jnp.stack([memory_written_keys, memory_written_values])
        memory_unit_rows = rounded(unit_rows(memory.reshape(2, MEMORY_ROWS, HEADS, DH)))
        memory_score_matrix = jnp.einsum('zul,rul->uzr', query_head_split, memory_unit_rows[0]) * head_scale_factors
        tok_scores = jnp.einsum('thd,shd->hts', query_head_split, key_head_split) * head_scale_factors
        allowed = causal * valid_keys[None, :]
        memory_attention_weights = rounded(jax.nn.sigmoid(memory_score_matrix - score_bias))
        token_attention_weights = rounded(jax.nn.sigmoid(tok_scores - score_bias) * allowed[None, :, :])
        attended_output = jnp.einsum('krf,fku->rku', memory_attention_weights, memory_unit_rows[1]) + jnp.einsum('ymo,oyl->myl', token_attention_weights, value_head_split)
        attended_output = rounded(attended_output * valid_keys[:, None, None]).reshape(SEG, N_HEAD, group_cols)
        partials = rounded(jnp.einsum('tgc,gcd->gtd', attended_output, out_groups))
        branch = lax.optimization_barrier(jnp.sum(partials, axis=0)).astype(jnp.bfloat16)
        new_memory = jnp.repeat(retain, DH)[None, None, :] * memory + written
        return (new_memory, branch)
    start = jnp.zeros((2, MEMORY_ROWS, head_columns), jnp.float32)
    segments_in = (tokens.reshape(LOG_PART_TOTAL, SEG, D), decay, seg_len.astype(jnp.int32))
    _, branches = lax.scan(segment, start, segments_in)
    return branches.reshape(LOG_PART_TOTAL * SEG, D)
```

```python
import math

import jax
import jax.numpy as jnp
from jax import lax
from jax.sharding import PartitionSpec as P

DH = 128


def pick(a, i):
    return lax.dynamic_index_in_dim(a, i, 0, False)


def body(tokens, gain, w_query, w_key, w_value, w_out, mem_query, score_scale, decay, seg_len):
    n_seq = lax.axis_size("seq")
    n_head = lax.axis_size("head")
    seg_rows, feat_local = tokens.shape
    width = gain.shape[0]
    w_rows, col_local = w_query.shape
    heads = col_local // DH
    slots = mem_query.shape[0]
    cn = 2 if heads % 2 == 0 else 1
    zn = heads // cn
    xn = n_seq // heads
    place = lax.axis_index("seq")
    y = lax.axis_index("head")
    c = place % cn
    x = place // cn % xn
    z = place // (cn * xn)

    def split(s):
        return s // (cn * xn), s // cn % xn, s % cn

    def join(a, b, d):
        return (a * xn + b) * cn + d

    def over_z(a, j):
        pairs = [(s, join(split(s)[0] ^ j, *split(s)[1:])) for s in range(n_seq)]
        return lax.ppermute(a, "seq", pairs)

    def over_x(a, k):
        pairs = []
        for s in range(n_seq):
            sz, sx, sc = split(s)
            pairs.append((s, join(sz, (sx + k) % xn, sc)))
        return lax.ppermute(a, "seq", pairs)

    def over_c(a, m):
        pairs = [(s, s ^ m) for s in range(n_seq)]
        return lax.ppermute(a, "seq", pairs)

    def over_y(a, k):
        return lax.ppermute(a, "head", [(h, (h + k) % n_head) for h in range(n_head)])

    def gather_z(a):
        got = {0: a}
        bit = zn // 2
        while bit:
            for j in sorted(got):
                got[j | bit] = over_z(got[j], bit)
            bit //= 2
        return [got[j] for j in range(zn)]

    normed = []
    for part in gather_z(tokens):
        own = [part] + [over_y(part, k) for k in range(1, n_head)]
        rows = []
        for m in range(cn):
            full = jnp.zeros((seg_rows, width), tokens.dtype)
            for k, piece in enumerate(own):
                piece = over_c(piece, m) if m else piece
                full = lax.dynamic_update_slice(full, piece, (0, (y - k) % n_head * feat_local))
            rows.append(full)
        wide = jnp.concatenate(rows).astype(jnp.float32)
        mean_squares = jnp.mean(wide * wide, axis=1, keepdims=True)
        normed.append((wide * lax.rsqrt(mean_squares + 1e-05) * gain).astype(jnp.bfloat16))

    blocks = jnp.concatenate(
        [
            w.reshape(w_rows, heads, DH).transpose(1, 0, 2)
            for w in (w_query, w_key, w_value)
        ],
        axis=2,
    ).reshape(zn, cn, w_rows, 3 * DH)
    weight = jnp.zeros((zn, xn, cn, w_rows, 3 * DH), w_query.dtype)
    for j in range(zn):
        block = pick(blocks, z ^ j)
        block = over_z(block, j) if j else block
        pair = jnp.zeros((cn, w_rows, 3 * DH), w_query.dtype)
        for m in range(cn):
            piece = pick(block, c ^ m)
            piece = over_c(piece, m) if m else piece
            pair = lax.dynamic_update_slice(pair, piece[None], (c ^ m, 0, 0))
        for k in range(xn):
            got = over_x(pair, k) if k else pair
            weight = lax.dynamic_update_slice(
                weight, got[None, None], (z ^ j, (x - k) % xn, 0, 0, 0)
            )
    weight = weight.reshape(width, 3 * DH)

    meta = jnp.concatenate([decay, seg_len.astype(jnp.float32)[:, None]], axis=1)
    table = jnp.zeros((zn, xn, cn, heads + 1), jnp.float32)
    for j, by_z in enumerate(gather_z(meta)):
        for k in range(xn):
            by_x = over_x(by_z, k) if k else by_z
            for m in range(cn):
                got = over_c(by_x, m) if m else by_x
                table = lax.dynamic_update_slice(
                    table, got[None, None], (z ^ j, (x - k) % xn, c ^ m, 0)
                )
    head = z * cn + c
    retain = lax.dynamic_index_in_dim(table, head, 3, False)
    lens = lax.dynamic_index_in_dim(table[..., heads], x, 1, False)
    retain_own = lax.dynamic_index_in_dim(retain, x, 1, False)

    sums = jnp.stack(
        [
            jnp.dot(rows, weight, preferred_element_type=jnp.float32)
            .astype(jnp.bfloat16)
            .reshape(cn, seg_rows, 3 * DH)
            for rows in normed
        ]
    )
    order = [pick(sums, z ^ i) for i in range(zn)]
    sums = jnp.stack([jnp.stack([pick(o, c ^ i) for i in range(cn)]) for o in order])
    query, keys, values = jnp.split(sums, 3, axis=3)

    inverse_root_scale = 1.0 / math.sqrt(DH)
    score_bias = math.log(slots + seg_rows)
    positions = jnp.arange(seg_rows, dtype=jnp.float32)
    valid = (positions < lens[..., None]).astype(jnp.float32)
    own_query = lax.dynamic_slice_in_dim(mem_query, head * DH, DH, 1)
    f32 = dict(preferred_element_type=jnp.float32)
    write_scores = jnp.einsum("md,zctd->zcmt", own_query, keys, **f32) * inverse_root_scale
    write_weights = (
        jax.nn.sigmoid(write_scores - math.log(seg_rows)) * valid[:, :, None, :]
    ).astype(jnp.bfloat16)
    written = jnp.einsum("zcmt,zctd->zcmd", write_weights, sums[..., DH:], **f32)

    group = written[:, 0]
    for i in range(1, cn):
        group = retain_own[:, i, None, None] * group + written[:, i]
    groups = jnp.zeros((xn,) + group.shape, jnp.float32)
    for k in range(xn):
        got = over_x(group.astype(jnp.bfloat16), k).astype(jnp.float32) if k else group
        groups = lax.dynamic_update_slice(groups, got[None], ((x - k) % xn, 0, 0, 0))
    group_retain = jnp.prod(retain, axis=2)
    memory = jnp.zeros_like(group[0])
    memory_in = []
    for i in range(zn):
        entry = memory
        for k in range(xn):
            if k:
                entry = jnp.where(x == k, memory, entry)
            memory = group_retain[i, k] * memory + groups[k, i]
        inner = []
        for m in range(cn):
            inner.append(entry)
            entry = retain_own[i, m] * entry + written[i, m]
        memory_in.append(jnp.stack(inner))
    memory_in = jnp.stack(memory_in).reshape(zn, cn, slots, 2, DH)
    unit = (
        memory_in * lax.rsqrt(jnp.mean(jnp.square(memory_in), axis=4, keepdims=True) + 1e-06)
    ).astype(jnp.bfloat16)

    scale = pick(score_scale, head) * inverse_root_scale
    mem_scores = jnp.einsum("zctd,zcmd->zctm", query, unit[:, :, :, 0], **f32) * scale
    tok_scores = jnp.einsum("zctd,zcsd->zcts", query, keys, **f32) * scale
    allowed = (positions[None, :] <= positions[:, None]).astype(jnp.float32) * valid[:, :, None, :]
    mem_weights = jax.nn.sigmoid(mem_scores - score_bias).astype(jnp.bfloat16)
    tok_weights = (jax.nn.sigmoid(tok_scores - score_bias) * allowed).astype(jnp.bfloat16)
    attended = jnp.einsum("zctm,zcmd->zctd", mem_weights, unit[:, :, :, 1], **f32)
    attended = attended + jnp.einsum("zcts,zcsd->zctd", tok_weights, values, **f32)
    attended = (attended * valid[..., None]).astype(jnp.bfloat16)

    rows = jnp.zeros((seg_rows, zn, cn, DH), jnp.bfloat16)
    for j in range(zn):
        block = pick(attended, z ^ j)
        block = over_z(block, j) if j else block
        for m in range(cn):
            piece = pick(block, c ^ m)
            piece = over_c(piece, m) if m else piece
            rows = lax.dynamic_update_slice(rows, piece[:, None, None], (0, z ^ j, c ^ m, 0))
    rows = rows.reshape(seg_rows, heads * DH)

    tied, _ = lax.optimization_barrier((w_out, weight))
    out_cols = w_out.shape[1]
    partial = jnp.zeros((seg_rows, n_seq * out_cols), jnp.bfloat16)
    for j, by_z in enumerate(gather_z(tied)):
        for k in range(xn):
            by_x = over_x(by_z, k) if k else by_z
            for m in range(cn):
                got = over_c(by_x, m) if m else by_x
                product = jnp.dot(rows, got, **f32).astype(jnp.bfloat16)
                source = join(z ^ j, (x - k) % xn, c ^ m)
                partial = lax.dynamic_update_slice(partial, product, (0, source * out_cols))
    branch = lax.dynamic_slice_in_dim(partial, y * feat_local, feat_local, 1).astype(jnp.float32)
    for k in range(1, n_head):
        share = lax.dynamic_slice_in_dim(partial, (y + k) % n_head * feat_local, feat_local, 1)
        branch = branch + over_y(share, k).astype(jnp.float32)
    return branch.astype(jnp.bfloat16)


def solution(mesh):
    return jax.shard_map(
        body,
        mesh=mesh,
        in_specs=(
            P("seq", "head"),
            P(),
            P("seq", "head"),
            P("seq", "head"),
            P("seq", "head"),
            P("head", "seq"),
            P(None, "head"),
            P("head"),
            P("seq", "head"),
            P("seq"),
        ),
        out_specs=P("seq", "head"),
        check_vma=False,
    )
```

```python
import functools
import math

import jax
import jax.numpy as jnp
from jax import lax
from jax.experimental import pallas as pl
from jax.experimental.pallas import tpu as pltpu
from jax.sharding import PartitionSpec as P

DH = 128
F32 = jnp.float32
BF16 = jnp.bfloat16
VMEM = pl.BlockSpec(memory_space=pltpu.VMEM)
SMEM = pl.BlockSpec(memory_space=pltpu.SMEM)


def dot(a, b, contract=(1, 0)):
    dims = (((contract[0],), (contract[1],)), ((), ()))
    return lax.dot_general(a, b, dims, preferred_element_type=F32)


def call(kernel, ins, outs, scratch=(), flops=0, scalars=1):
    moved = sum(math.prod(a.shape) * a.dtype.itemsize for a in (*ins, *outs))
    return pl.pallas_call(
        kernel,
        in_specs=[SMEM] * scalars + [VMEM] * (len(ins) - scalars),
        out_specs=[VMEM] * len(outs),
        out_shape=outs,
        scratch_shapes=scratch,
        compiler_params=pltpu.CompilerParams(vmem_limit_bytes=48 * 2**20),
        cost_estimate=pl.CostEstimate(flops=flops, bytes_accessed=moved, transcendentals=0),
    )(*ins)


def lanes(index, size):
    return pl.ds(pl.multiple_of(index * size, size), size)


def cut_kernel(zn, cn, at, *refs):
    weights, outs = refs[:3], refs[3:]
    z, c = at[0], at[2]
    for m, out in enumerate(outs):
        for j in range(zn):
            head = (z ^ j) * cn + (c ^ m)
            for i, w in enumerate(weights):
                out[j, :, i * DH : (i + 1) * DH] = w[:, lanes(head, DH)]


def pack_kernel(zn, cn, *refs):
    for j in range(zn):
        for m in range(cn):
            refs[cn + j][m] = refs[m][j]


def norm_kernel(n_head, at, gain, *refs):
    parts, out = refs[:n_head], refs[n_head]
    feat = parts[0].shape[1]
    wide = [part[...].astype(F32) for part in parts]
    squares = sum(jnp.sum(w * w, axis=1, keepdims=True) for w in wide)
    inverse = lax.rsqrt(squares / (feat * n_head) + 1e-05)
    for k, w in enumerate(wide):
        half = lanes(lax.rem(at[3] + n_head - k, n_head), feat)
        out[:, half] = (w * inverse * gain[:, half]).astype(BF16)


def project(zn, xn, cn, j, at, rows, weights, chunk, each):
    z, x, c = at[0], at[1], at[2]
    w_rows = weights[0].shape[1]
    for k, w in enumerate(weights):
        for m in range(cn):
            spot = lax.rem(x + xn - k, xn) * cn + (c ^ m)
            chunk[pl.ds(pl.multiple_of(spot * w_rows, w_rows), w_rows), :] = w[m]
    size = chunk.shape[0]
    for i in range(zn):
        left = jnp.concatenate([rows[i * cn + m][:, lanes(z ^ j, size)] for m in range(cn)])
        each(i, dot(left, chunk[...]))


def project_kernel(zn, xn, cn, steps, at, *refs):
    rows = refs[: zn * cn]
    weights = refs[zn * cn : zn * cn + len(steps) * xn]
    out, chunk = refs[-2:]
    for n, j in enumerate(steps):

        def each(i, sums):
            out[i] = sums if n == 0 else out[i] + sums

        project(zn, xn, cn, j, at, rows, weights[n * xn : (n + 1) * xn], chunk.at[n], each)


def segment_info(xn, cn, heads, at, table):
    width = heads + 1
    z, x, c = at[0], at[1], at[2]
    head = z * cn + c

    def row(zi, xi, ci):
        return (((z ^ zi) * xn + lax.rem(x + xn - xi, xn)) * cn + (c ^ ci)) * width

    def retain(zi, xi, ci):
        return table[row(zi, xi, ci) + head]

    def length(zi, ci):
        return table[row(zi, x, ci) + heads]

    return retain, length


def write_kernel(zn, xn, cn, heads, step, at, table, *refs):
    rows = refs[: zn * cn]
    weights = refs[zn * cn : zn * cn + xn]
    query = refs[zn * cn + xn]
    before = refs[zn * cn + xn + 1] if zn > 1 else None
    sums, written, group, group16, chunk = refs[-5:]
    z, x, c = at[0], at[1], at[2]
    retain, length = segment_info(xn, cn, heads, at, table)
    seg_rows = sums.shape[2]

    def each(i, add):
        add = add if before is None else add + before[i]
        add = add.astype(BF16).reshape(cn, seg_rows, 3 * DH)
        for m in range(cn):
            sums[z ^ i, c ^ m] = add[m]

    project(zn, xn, cn, step, at, rows, weights, chunk.at[0], each)
    own = query[:, lanes(z * cn + c, DH)]
    slots = own.shape[0]
    position = lax.broadcasted_iota(jnp.int32, (slots, seg_rows), 1).astype(F32)
    for i in range(zn):
        total = None
        for m in range(cn):
            keys = sums[i, m, :, DH : 2 * DH]
            scores = dot(own, keys, (1, 1)) * (1.0 / math.sqrt(DH))
            gate = jax.nn.sigmoid(scores - math.log(seg_rows))
            gate = jnp.where(position < length(i, m), gate, 0.0).astype(BF16)
            new = dot(gate, sums[i, m, :, DH:])
            written[i, m] = new
            total = new if total is None else retain(i, x, m) * total + new
        group[i] = total
        group16[i] = total.astype(BF16)


def token_kernel(zn, xn, cn, heads, slots, at, table, scale, sums, out):
    _, length = segment_info(xn, cn, heads, at, table)
    seg_rows = sums.shape[2]
    shape = (seg_rows, seg_rows)
    row = lax.broadcasted_iota(jnp.int32, shape, 0)
    column = lax.broadcasted_iota(jnp.int32, shape, 1)
    factor = scale[at[0] * cn + at[2]] * (1.0 / math.sqrt(DH))
    for i in range(zn):
        for m in range(cn):
            query, keys, values = (sums[i, m, :, n * DH : (n + 1) * DH] for n in range(3))
            scores = dot(query, keys, (1, 1)) * factor
            gate = jax.nn.sigmoid(scores - math.log(slots + seg_rows))
            allowed = (column <= row) & (column.astype(F32) < length(i, m))
            out[i, m] = dot(jnp.where(allowed, gate, 0.0).astype(BF16), values)


def memory_kernel(zn, xn, cn, heads, at, table, scale, sums, token, written, group, *refs):
    others = refs[: xn - 1]
    outs = refs[xn - 1 : xn - 1 + zn]
    groups, done = refs[-2:]
    z, x, c = at[0], at[1], at[2]
    retain, length = segment_info(xn, cn, heads, at, table)
    slots, seg_rows = group.shape[1], sums.shape[2]
    factor = scale[z * cn + c] * (1.0 / math.sqrt(DH))
    bias = math.log(slots + seg_rows)
    row = lax.broadcasted_iota(jnp.int32, (seg_rows, DH), 0).astype(F32)
    groups[x] = group[...]
    for k, other in enumerate(others, 1):
        groups[lax.rem(x + xn - k, xn)] = other[...].astype(F32)
    memory = jnp.zeros(group.shape[1:], F32)
    for i in range(zn):
        entry = memory
        for k in range(xn):
            if k:
                entry = jnp.where(x == k, memory, entry)
            kept = retain(i, k, 0)
            for m in range(1, cn):
                kept = kept * retain(i, k, m)
            memory = kept * memory + groups[k, i]
        for m in range(cn):
            units = []
            for n in range(2):
                part = entry[:, n * DH : (n + 1) * DH]
                mean = jnp.mean(part * part, axis=1, keepdims=True)
                units.append((part * lax.rsqrt(mean + 1e-06)).astype(BF16))
            scores = dot(sums[i, m, :, :DH], units[0], (1, 1)) * factor
            gate = jax.nn.sigmoid(scores - bias).astype(BF16)
            total = dot(gate, units[1]) + token[i, m]
            done[i, m] = jnp.where(row < length(i, m), total, 0.0).astype(BF16)
            if m + 1 < cn:
                entry = retain(i, x, m) * entry + written[i, m]
    for j in range(zn):
        for m in range(cn):
            outs[j][m] = done[z ^ j, c ^ m]


def out_kernel(zn, xn, cn, n_head, at, *refs):
    attended = refs[: zn * cn]
    weights = refs[zn * cn : zn * cn + zn * xn]
    outs, rows = refs[-1 - cn * n_head : -1], refs[-1]
    z, x, c, y = at[0], at[1], at[2], at[3]
    seg_rows = attended[0].shape[1]
    for j in range(zn):
        for e in range(cn):
            for m in range(cn):
                rows[m * seg_rows : (m + 1) * seg_rows, lanes((z ^ j) * cn + (c ^ e), DH)] = (
                    attended[j * cn + e][m ^ e]
                )
    blocks = outs[0].shape[0]
    for j in range(zn):
        for k in range(xn):
            product = dot(rows[...], weights[j * xn + k][...]).astype(BF16)
            spot = (z ^ j) * xn + lax.rem(x + xn - k, xn)
            turn = lax.rem(spot // blocks + n_head - y, n_head)
            for r in range(n_head):

                @pl.when(turn == r)
                def _():
                    for m in range(cn):
                        outs[r * cn + m][lax.rem(spot, blocks)] = product[
                            m * seg_rows : (m + 1) * seg_rows
                        ]


def sum_kernel(n_head, cn, at, *refs):
    out = refs[-1]
    blocks, _, size = refs[0].shape
    for b in range(blocks):
        totals = [
            sum(refs[r * cn + e][b].astype(F32) for r in range(n_head)).astype(BF16)
            for e in range(cn)
        ]
        for m in range(cn):
            total = totals[0]
            for e in range(1, cn):
                total = jnp.where((at[2] ^ e) == m, totals[e], total)
            first = (b * cn + m) * size
            out[:, first : first + size] = total


def body(tokens, gain, w_query, w_key, w_value, w_out, mem_query, score_scale, decay, seg_len):
    n_seq = lax.axis_size("seq")
    n_head = lax.axis_size("head")
    seg_rows, feat_local = tokens.shape
    width = gain.shape[0]
    w_rows, col_local = w_query.shape
    heads = col_local // DH
    slots = mem_query.shape[0]
    cn = 2 if heads % 2 == 0 else 1
    zn = heads // cn
    xn = n_seq // heads
    place = lax.axis_index("seq")
    y = lax.axis_index("head")
    at = jnp.stack([place // (cn * xn), place // cn % xn, place % cn, y]).astype(jnp.int32)

    def shape(dims, dtype=BF16):
        return jax.ShapeDtypeStruct(dims, dtype)

    def split(s):
        return s // (cn * xn), s // cn % xn, s % cn

    def join(a, b, d):
        return (a * xn + b) * cn + d

    def over_z(a, j):
        pairs = [(s, join(split(s)[0] ^ j, *split(s)[1:])) for s in range(n_seq)]
        return lax.ppermute(a, "seq", pairs)

    def over_x(a, k):
        pairs = []
        for s in range(n_seq):
            sz, sx, sc = split(s)
            pairs.append((s, join(sz, (sx + k) % xn, sc)))
        return lax.ppermute(a, "seq", pairs)

    def over_c(a, m):
        return lax.ppermute(a, "seq", [(s, s ^ m) for s in range(n_seq)])

    def over_y(a, k):
        return lax.ppermute(a, "head", [(h, (h + k) % n_head) for h in range(n_head)])

    def gather_z(a):
        got = {0: a}
        bit = zn // 2
        while bit:
            for j in sorted(got):
                got[j | bit] = over_z(got[j], bit)
            bit //= 2
        return [got[j] for j in range(zn)]

    def after(a, *done):
        return lax.optimization_barrier((a,) + done)[0]

    tok = gather_z(tokens)
    rows = []
    for part in tok:
        parts = [part] + [over_y(part, k) for k in range(1, n_head)]
        (normed,) = call(
            functools.partial(norm_kernel, n_head),
            (at, gain[None], *parts),
            [shape((seg_rows, width))],
        )
        rows += [over_c(normed, m) if m else normed for m in range(cn)]

    cuts = call(
        functools.partial(cut_kernel, zn, cn),
        (at, w_query, w_key, w_value),
        [shape((zn, w_rows, 3 * DH))] * cn,
    )
    cuts = [over_c(cut, m) if m else cut for m, cut in enumerate(cuts)]
    packs = call(
        functools.partial(pack_kernel, zn, cn),
        cuts,
        [shape((cn, w_rows, 3 * DH))] * zn,
        scalars=0,
    )
    pieces = []
    for j, pack in enumerate(packs):
        if j:
            pack = over_z(after(pack, tok[1 if j < 3 else 2]), j)
        pieces.append([over_x(pack, k) if k else pack for k in range(xn)])

    meta = after(jnp.concatenate([decay[0], seg_len.astype(F32)]), tok[zn // 2])
    meta = jnp.stack([over_c(meta, m) if m else meta for m in range(cn)])
    meta = jnp.stack([over_x(meta, k) if k else meta for k in range(xn)])
    table = jnp.stack(gather_z(meta)).reshape(-1)

    def chunks(count):
        return [pltpu.VMEM((count, xn * cn * w_rows, 3 * DH), BF16)]

    flops = 2 * zn * cn * seg_rows * width * 3 * DH
    last = zn - 1
    before = []
    if last:
        before = call(
            functools.partial(project_kernel, zn, xn, cn, range(last)),
            (at, *rows, *sum(pieces[:last], [])),
            [shape((zn, cn * seg_rows, 3 * DH), F32)],
            chunks(last),
            flops * last // zn,
        )
    sums, written, group, group16 = call(
        functools.partial(write_kernel, zn, xn, cn, heads, last),
        (at, table, *rows, *pieces[last], mem_query, *before),
        [
            shape((zn, cn, seg_rows, 3 * DH)),
            shape((zn, cn, slots, 2 * DH), F32),
            shape((zn, slots, 2 * DH), F32),
            shape((zn, slots, 2 * DH)),
        ],
        chunks(1),
        flops // zn,
        scalars=2,
    )
    others = [over_x(group16, k) for k in range(1, xn)]
    (token,) = call(
        functools.partial(token_kernel, zn, xn, cn, heads, slots),
        (at, table, score_scale, sums),
        [shape((zn, cn, seg_rows, DH), F32)],
        scalars=3,
    )
    attended = call(
        functools.partial(memory_kernel, zn, xn, cn, heads),
        (at, table, score_scale, sums, token, written, group, *others),
        [shape((cn, seg_rows, DH))] * zn,
        [
            pltpu.VMEM((xn, zn, slots, 2 * DH), F32),
            pltpu.VMEM((zn, cn, seg_rows, DH), BF16),
        ],
        scalars=3,
    )

    here = []
    for j, block in enumerate(attended):
        block = over_z(block, j) if j else block
        here += [over_c(block, m) if m else block for m in range(cn)]

    columns = []
    for part in gather_z(after(w_out, pieces[last][0])):
        columns += [over_x(part, k) if k else part for k in range(xn)]
    out_cols = w_out.shape[1]
    blocks = feat_local // (cn * out_cols)
    products = call(
        functools.partial(out_kernel, zn, xn, cn, n_head),
        (at, *here, *columns),
        [shape((blocks, seg_rows, out_cols))] * (cn * n_head),
        [pltpu.VMEM((cn * seg_rows, heads * DH), BF16)],
        2 * cn * seg_rows * heads * DH * zn * xn * out_cols,
    )
    mine = []
    for r in range(n_head):
        for m in range(cn):
            block = products[r * cn + m]
            block = over_c(block, m) if m else block
            mine.append(over_y(block, r) if r else block)
    (branch,) = call(
        functools.partial(sum_kernel, n_head, cn),
        (at, *mine),
        [shape((seg_rows, feat_local))],
    )
    return branch


def solution(mesh):
    return jax.shard_map(
        body,
        mesh=mesh,
        in_specs=(
            P("seq", "head"),
            P(),
            P("seq", "head"),
            P("seq", "head"),
            P("seq", "head"),
            P("head", "seq"),
            P(None, "head"),
            P("head"),
            P("seq", "head"),
            P("seq"),
        ),
        out_specs=P("seq", "head"),
        check_vma=False,
    )
```

```python
import functools
import math

import jax
import jax.numpy as jnp
from jax import lax
from jax.experimental import pallas as pl
from jax.experimental.pallas import tpu as pltpu
from jax.sharding import PartitionSpec as P

DH = 128
META = 16
F32 = jnp.float32
BF16 = jnp.bfloat16


def dot(a, b, contract=(1, 0)):
    dims = (((contract[0],), (contract[1],)), ((), ()))
    return lax.dot_general(a, b, dims, preferred_element_type=F32)


def call(kernel, ins, outs, scratch=(), flops=0, scalars=1, column=None, room=20):
    moved = sum(math.prod(a.shape) * a.dtype.itemsize for a in (*ins, *outs))

    def whole(a):
        return pl.BlockSpec(a.shape, lambda i, *_: (0,) * len(a.shape))

    def spec(a):
        if column and a.shape[-1] > column[0] and a.ndim == 2 and a.dtype == BF16:
            pick = column[1]
            return pl.BlockSpec((a.shape[0], column[0]), lambda i, at, *_: (0, pick(at)))
        return whole(a)

    return pl.pallas_call(
        kernel,
        grid_spec=pltpu.PrefetchScalarGridSpec(
            num_scalar_prefetch=scalars,
            grid=(1,),
            in_specs=[spec(a) for a in ins[scalars:]],
            out_specs=[whole(a) for a in outs],
            scratch_shapes=scratch,
        ),
        out_shape=outs,
        compiler_params=pltpu.CompilerParams(vmem_limit_bytes=room * 2**20),
        cost_estimate=pl.CostEstimate(flops=flops, bytes_accessed=moved, transcendentals=0),
    )(*ins)


def lanes(index, size):
    return pl.ds(pl.multiple_of(index * size, size), size)


def cut_kernel(cn, at, decay, seg_len, *refs):
    weights, outs = refs[:3], refs[3:]
    w_rows = weights[0].shape[0]
    row = lax.broadcasted_iota(jnp.int32, (META, DH), 0)
    length = jnp.full((META, DH), seg_len[0], jnp.int32).astype(F32)
    for j, out in enumerate(outs):
        for e in range(cn):
            head = (at[0] ^ j) * cn + e
            rest = jnp.full((META, DH), decay[head], F32)
            for i, w in enumerate(weights):
                first = (e * 3 + i) * DH
                out[:w_rows, first : first + DH] = w[:, lanes(head, DH)]
                term = rest.astype(BF16).astype(F32)
                rest = rest - term
                out[w_rows:, first : first + DH] = jnp.where(row < META // 2, term, length).astype(BF16)


def norm_kernel(n_head, at, gain, *refs):
    parts, out = refs[:n_head], refs[n_head]
    feat = parts[0].shape[1]
    wide = [part[...].astype(F32) for part in parts]
    squares = sum(jnp.sum(w * w, axis=1, keepdims=True) for w in wide)
    inverse = lax.rsqrt(squares / (feat * n_head) + 1e-05)
    for k, w in enumerate(wide):
        half = lanes(lax.rem(at[3] + n_head - k, n_head), feat)
        out[:, half] = (w * inverse * gain[:, half]).astype(BF16)


def project(xn, cn, at, rows, weights, chunk, meta, each):
    x, c = at[1], at[2]
    w_rows = weights[0].shape[0] - META
    row = lax.broadcasted_iota(jnp.int32, (META, DH), 0)
    for n, w in enumerate(weights):
        xi, ci = lax.rem(x + xn - n // cn, xn), c ^ (n % cn)
        chunk[pl.ds(pl.multiple_of((xi * cn + ci) * w_rows, w_rows), w_rows), :] = w[:w_rows]
        tail = w[w_rows:].astype(F32)
        terms = tail[:, : 3 * DH]
        for e in range(1, cn):
            terms = jnp.where(c == e, tail[:, e * 3 * DH : (e + 1) * 3 * DH], terms)
        total = terms[:, :DH] + terms[:, DH : 2 * DH] + terms[:, 2 * DH :]
        meta[xi, ci] = jnp.where(row < META // 2, total, terms[:, :DH])
    for first in range(0, len(rows), 2):
        pair = range(first, min(first + 2, len(rows)))
        sums = dot(jnp.concatenate([rows[i][...] for i in pair]), chunk[...])
        for n, i in enumerate(pair):
            size = sums.shape[0] // len(pair)
            each(i, sums[n * size : (n + 1) * size])


def project_kernel(zn, xn, cn, steps, at, *refs):
    rows = refs[:zn]
    weights = refs[zn : zn + len(steps) * xn * cn]
    out, meta, chunk = refs[-3:]
    size = chunk.shape[1]
    for n, j in enumerate(steps):

        def each(i, sums):
            out[i] = sums if n == 0 else out[i] + sums

        part = [row.at[:, lanes(at[0] ^ j, size)] for row in rows]
        few = weights[n * xn * cn : (n + 1) * xn * cn]
        project(xn, cn, at, part, few, chunk.at[n], meta.at[n], each)


def finish_kernel(zn, xn, cn, at, *refs):
    rows = refs[:zn]
    weights = refs[zn : zn + xn * cn]
    before = refs[zn + xn * cn] if zn > 1 else None
    outs, meta, chunk = refs[-2 - cn : -2], refs[-2], refs[-1]
    c = at[2]

    def each(i, sums):
        sums = (sums if before is None else sums + before[i]).astype(BF16)
        heads = [sums[:, e * 3 * DH : (e + 1) * 3 * DH] for e in range(cn)]
        for m, out in enumerate(outs):
            pick = heads[m]
            for e in range(cn):
                if e != m:
                    pick = jnp.where((c ^ m) == e, heads[e], pick)
            out[i] = pick

    project(xn, cn, at, rows, weights, chunk, meta.at[0], each)


def segment_info(table):
    def retain(zi, xi, ci):
        return table[zi, xi, ci, 0:1, 0:1]

    def length(zi, xi, ci):
        return table[zi, xi, ci, META // 2 : META // 2 + 1, 0:1]

    return retain, length


def write_kernel(zn, xn, cn, at, *refs):
    parts, query, metas = refs[:cn], refs[cn], refs[cn + 1 : -5]
    sums, written, group, group16, table = refs[-5:]
    z, x, c = at[0], at[1], at[2]
    j = 0
    for meta in metas:
        for n in range(meta.shape[0]):
            table[z ^ j] = meta[n]
            j += 1
    retain, length = segment_info(table)
    seg_rows = sums.shape[2]
    for i in range(zn):
        for m in range(cn):
            sums[z ^ i, c ^ m] = parts[m][i]
    own = query[:, lanes(z * cn + c, DH)]
    slots = own.shape[0]
    position = lax.broadcasted_iota(jnp.int32, (slots, seg_rows), 1).astype(F32)
    for i in range(zn):
        keys = sums[i, :, :, DH : 2 * DH].reshape(cn * seg_rows, DH)
        scores = dot(own, keys, (1, 1)) * (1.0 / math.sqrt(DH))
        gates = jax.nn.sigmoid(scores - math.log(seg_rows))
        total = None
        for m in range(cn):
            gate = gates[:, m * seg_rows : (m + 1) * seg_rows]
            gate = jnp.where(position < length(i, x, m), gate, 0.0).astype(BF16)
            new = dot(gate, sums[i, m, :, DH:])
            written[i, m] = new
            total = new if total is None else retain(i, x, m) * total + new
        group[i] = total
        group16[i] = total.astype(BF16)


def token_kernel(zn, cn, slots, at, scale, table, sums, out):
    _, length = segment_info(table)
    seg_rows = sums.shape[2]
    shape = (seg_rows, seg_rows)
    row = lax.broadcasted_iota(jnp.int32, shape, 0)
    column = lax.broadcasted_iota(jnp.int32, shape, 1)
    factor = scale[at[0] * cn + at[2]] * (1.0 / math.sqrt(DH))
    for i in range(zn):
        for m in range(cn):
            query, keys, values = (sums[i, m, :, n * DH : (n + 1) * DH] for n in range(3))
            scores = dot(query, keys, (1, 1)) * factor
            gate = jax.nn.sigmoid(scores - math.log(slots + seg_rows))
            allowed = (column <= row) & (column.astype(F32) < length(i, at[1], m))
            out[i, m] = dot(jnp.where(allowed, gate, 0.0).astype(BF16), values)


def memory_kernel(zn, xn, cn, at, scale, table, sums, token, written, group, *refs):
    others = refs[: xn - 1]
    outs = refs[xn - 1 : xn - 1 + zn]
    groups, done = refs[-2:]
    z, x, c = at[0], at[1], at[2]
    retain, length = segment_info(table)
    slots, seg_rows = group.shape[1], sums.shape[2]
    factor = scale[z * cn + c] * (1.0 / math.sqrt(DH))
    bias = math.log(slots + seg_rows)
    row = lax.broadcasted_iota(jnp.int32, (seg_rows, DH), 0).astype(F32)
    groups[x] = group[...]
    for k, other in enumerate(others, 1):
        groups[lax.rem(x + xn - k, xn)] = other[...].astype(F32)
    memory = jnp.zeros(group.shape[1:], F32)
    for i in range(zn):
        entry = memory
        for k in range(xn):
            if k:
                entry = jnp.where(x == k, memory, entry)
            kept = retain(i, k, 0)
            for m in range(1, cn):
                kept = kept * retain(i, k, m)
            memory = kept * memory + groups[k, i]
        for m in range(cn):
            units = []
            for n in range(2):
                part = entry[:, n * DH : (n + 1) * DH]
                mean = jnp.mean(part * part, axis=1, keepdims=True)
                units.append((part * lax.rsqrt(mean + 1e-06)).astype(BF16))
            scores = dot(sums[i, m, :, :DH], units[0], (1, 1)) * factor
            gate = jax.nn.sigmoid(scores - bias).astype(BF16)
            total = dot(gate, units[1]) + token[i, m]
            done[i, m] = jnp.where(row < length(i, x, m), total, 0.0).astype(BF16)
            if m + 1 < cn:
                entry = retain(i, x, m) * entry + written[i, m]
    for j in range(zn):
        for m in range(cn):
            outs[j][m] = done[z ^ j, c ^ m]


def out_kernel(zn, xn, cn, n_head, at, *refs):
    attended = refs[: zn * cn]
    weights = refs[zn * cn : zn * cn + zn * xn]
    outs, rows = refs[-1 - cn * n_head : -1], refs[-1]
    z, x, c, y = at[0], at[1], at[2], at[3]
    seg_rows = attended[0].shape[1]
    for j in range(zn):
        for e in range(cn):
            for m in range(cn):
                rows[m * seg_rows : (m + 1) * seg_rows, lanes((z ^ j) * cn + (c ^ e), DH)] = (
                    attended[j * cn + e][m ^ e]
                )
    blocks = outs[0].shape[0]
    for j in range(zn):
        for k in range(xn):
            product = dot(rows[...], weights[j * xn + k][...]).astype(BF16)
            spot = (z ^ j) * xn + lax.rem(x + xn - k, xn)
            turn = lax.rem(spot // blocks + n_head - y, n_head)
            for r in range(n_head):

                @pl.when(turn == r)
                def _():
                    for m in range(cn):
                        outs[r * cn + m][lax.rem(spot, blocks)] = product[
                            m * seg_rows : (m + 1) * seg_rows
                        ]


def sum_kernel(n_head, cn, at, *refs):
    out = refs[-1]
    blocks, _, size = refs[0].shape
    for b in range(blocks):
        totals = [
            sum(refs[r * cn + e][b].astype(F32) for r in range(n_head)).astype(BF16)
            for e in range(cn)
        ]
        for m in range(cn):
            total = totals[0]
            for e in range(1, cn):
                total = jnp.where((at[2] ^ e) == m, totals[e], total)
            first = (b * cn + m) * size
            out[:, first : first + size] = total


def body(tokens, gain, w_query, w_key, w_value, w_out, mem_query, score_scale, decay, seg_len):
    n_seq = lax.axis_size("seq")
    n_head = lax.axis_size("head")
    seg_rows, feat_local = tokens.shape
    width = gain.shape[0]
    w_rows, col_local = w_query.shape
    heads = col_local // DH
    slots = mem_query.shape[0]
    cn = 2 if heads % 2 == 0 else 1
    zn = heads // cn
    xn = n_seq // heads
    place = lax.axis_index("seq")
    y = lax.axis_index("head")
    at = jnp.stack([place // (cn * xn), place // cn % xn, place % cn, y]).astype(jnp.int32)

    def shape(dims, dtype=BF16):
        return jax.ShapeDtypeStruct(dims, dtype)

    def split(s):
        return s // (cn * xn), s // cn % xn, s % cn

    def join(a, b, d):
        return (a * xn + b) * cn + d

    def over_z(a, j):
        pairs = [(s, join(split(s)[0] ^ j, *split(s)[1:])) for s in range(n_seq)]
        return lax.ppermute(a, "seq", pairs)

    def over_x(a, k):
        pairs = []
        for s in range(n_seq):
            sz, sx, sc = split(s)
            pairs.append((s, join(sz, (sx + k) % xn, sc)))
        return lax.ppermute(a, "seq", pairs)

    def over_c(a, m):
        return lax.ppermute(a, "seq", [(s, s ^ m) for s in range(n_seq)])

    def over_y(a, k):
        return lax.ppermute(a, "head", [(h, (h + k) % n_head) for h in range(n_head)])

    chain = []

    def mark(a):
        chain[:] = [a]
        return a

    def done(a):
        return mark(lax.optimization_barrier((a, *chain))[0])

    def done_all(parts):
        parts = lax.optimization_barrier((*parts, *chain))[: len(parts)]
        mark(parts[-1])
        return parts

    def after(a, b):
        return lax.optimization_barrier((a, b))[0]

    last = zn - 1
    tok, packs, pieces, rows = {0: tokens}, {}, {}, {}
    started, columns, out_z = {}, {}, {0: w_out}

    def begin_tok(j):
        low = j & -j
        if j < zn and j not in started and j ^ low in tok:
            started[j] = over_z(tok[j ^ low], low)

    def begin_y(j):
        started["y", j] = [over_y(tok[j], k) for k in range(1, n_head)]

    def end_y(j):
        parts = [tok[j]] + [done(part) for part in started["y", j]]
        (rows[j],) = call(
            functools.partial(norm_kernel, n_head),
            (at, gain[None], *parts),
            [shape((seg_rows, width))],
        )
        mark(rows[j])

    def both(a):
        return [over_c(a, m) if m else a for m in range(cn)]

    def begin_x(j):
        started["x", j] = [over_x(packs[j], k) for k in range(1, xn)]
        pieces[j] = both(packs[j])

    def end_x(j):
        for part in started["x", j]:
            pieces[j] += both(done(part))

    def begin_out(j, source):
        started["o", j] = [over_x(source, k) for k in range(1, xn)]
        columns[j] = [source]

    def end_out(j):
        columns[j] += [done(part) for part in started["o", j]]

    for bit in range(zn.bit_length() - 2, -1, -1):
        begin_tok(1 << bit)
    begin_y(0)
    begin_out(0, w_out)
    sent = call(
        functools.partial(cut_kernel, cn),
        (at, decay[0], seg_len, w_query, w_key, w_value),
        [shape((w_rows + META, cn * 3 * DH))] * zn,
        scalars=3,
    )
    packs[0] = sent[0]
    begin_x(0)
    if last:
        started["w", 1] = over_z(sent[1], 1)

    bits = [1 << n for n in range(zn.bit_length() - 1)]
    more = [j for j in range(1, zn) if j not in bits]
    if bits:
        for b, part in zip(bits, done_all([started[b] for b in bits])):
            tok[b] = part
            begin_y(b)
    for j in more:
        begin_tok(j)
    for j in range(2, min(3, zn)):
        started["w", j] = over_z(after(sent[j], tok[1]), j)
    end_y(0)
    ready = []
    for j in range(1, zn):
        if j == 2:
            ready = done_all([started["w", 2], *(started[i] for i in more)])
            packs[2] = ready[0]
            for i, part in zip(more, ready[1:]):
                tok[i] = part
                begin_y(i)
        elif j == last:
            first = over_z(after(w_out, packs[j - 1]), 1)
            packs[j], out_z[1] = done_all([started["w", j], first])
        else:
            packs[j] = done(started["w", j])
        begin_x(j)
        if j > 1 and j + 1 < zn:
            started["w", j + 1] = over_z(after(sent[j + 1], packs[j]), j + 1)
        end_y(j)
        end_x(j - 1)
        if j == 1:
            end_out(0)
    for b in bits[1:]:
        started["oz", b] = over_z(after(w_out, packs[last]), b)
    if not last:
        end_out(0)
    rows = [rows[j] for j in range(zn)]

    chunk_rows = xn * cn * w_rows
    flops = 2 * zn * seg_rows * chunk_rows * cn * 3 * DH
    before = []
    if last:
        before = call(
            functools.partial(project_kernel, zn, xn, cn, range(last)),
            (at, *rows, *sum((pieces[j] for j in range(last)), [])),
            [
                shape((zn, seg_rows, cn * 3 * DH), F32),
                shape((last, xn, cn, META, DH), F32),
            ],
            [pltpu.VMEM((last, chunk_rows, cn * 3 * DH), BF16)],
            flops * last,
            room=48,
        )
        mark(before[0])
    end_x(last)
    *parts, meta = call(
        functools.partial(finish_kernel, zn, xn, cn),
        (at, *rows, *pieces[last], *before[:1]),
        [shape((zn, seg_rows, 3 * DH))] * cn + [shape((1, xn, cn, META, DH), F32)],
        [pltpu.VMEM((chunk_rows, cn * 3 * DH), BF16)],
        flops,
        column=(chunk_rows, lambda at: at[0] ^ last),
        room=32,
    )
    if last:
        begin_out(1, out_z[1])
    parts = [done(over_c(part, m)) if m else part for m, part in enumerate(parts)]
    sums, written, group, group16, table = call(
        functools.partial(write_kernel, zn, xn, cn),
        (at, *parts, mem_query, *before[1:], meta),
        [
            shape((zn, cn, seg_rows, 3 * DH)),
            shape((zn, cn, slots, 2 * DH), F32),
            shape((zn, slots, 2 * DH), F32),
            shape((zn, slots, 2 * DH)),
            shape((zn, xn, cn, META, DH), F32),
        ],
    )
    others = [over_x(group16, k) for k in range(1, xn)]
    (token,) = call(
        functools.partial(token_kernel, zn, cn, slots),
        (at, score_scale, table, sums),
        [shape((zn, cn, seg_rows, DH), F32)],
        scalars=2,
    )
    mark(token)
    others = [done(other) for other in others]
    attended = call(
        functools.partial(memory_kernel, zn, xn, cn),
        (at, score_scale, table, sums, token, written, group, *others),
        [shape((cn, seg_rows, DH))] * zn,
        [
            pltpu.VMEM((xn, zn, slots, 2 * DH), F32),
            pltpu.VMEM((zn, cn, seg_rows, DH), BF16),
        ],
        scalars=2,
    )

    here = [over_z(block, j) if j else block for j, block in enumerate(attended)]
    swapped = {}
    for j in range(zn):
        here[j] = done(here[j]) if j else here[j]
        swapped[j] = [over_c(here[j], m) for m in range(1, cn)]
    for b in bits[1:]:
        out_z[b] = done(started["oz", b])
        begin_out(b, out_z[b])
    for j in range(1, zn):
        if j not in out_z:
            low = j & -j
            out_z[j] = done(over_z(out_z[j ^ low], low))
            begin_out(j, out_z[j])
    here = sum(([here[j]] + [done(a) for a in swapped[j]] for j in range(zn)), [])

    for j in range(1, zn):
        end_out(j)
    columns = sum((columns[j] for j in range(zn)), [])
    out_cols = w_out.shape[1]
    blocks = feat_local // (cn * out_cols)
    products = call(
        functools.partial(out_kernel, zn, xn, cn, n_head),
        (at, *here, *columns),
        [shape((blocks, seg_rows, out_cols))] * (cn * n_head),
        [pltpu.VMEM((cn * seg_rows, heads * DH), BF16)],
        2 * cn * seg_rows * heads * DH * zn * xn * out_cols,
        room=32,
    )
    mine = []
    for r in range(n_head):
        for m in range(cn):
            block = products[r * cn + m]
            block = over_c(block, m) if m else block
            mine.append(over_y(block, r) if r else block)
    (branch,) = call(
        functools.partial(sum_kernel, n_head, cn),
        (at, *mine),
        [shape((seg_rows, feat_local))],
    )
    return branch


def solution(mesh):
    return jax.shard_map(
        body,
        mesh=mesh,
        in_specs=(
            P("seq", "head"),
            P(),
            P("seq", "head"),
            P("seq", "head"),
            P("seq", "head"),
            P("head", "seq"),
            P(None, "head"),
            P("head"),
            P("seq", "head"),
            P("seq"),
        ),
        out_specs=P("seq", "head"),
        check_vma=False,
    )
```

```python
import functools
import math

import jax
import jax.numpy as jnp
from jax import lax
from jax.experimental import pallas as pl
from jax.experimental.pallas import tpu as pltpu
from jax.sharding import PartitionSpec as P

DH = 128
META = 16
F32 = jnp.float32
BF16 = jnp.bfloat16


def dot(a, b, contract=(1, 0)):
    dims = (((contract[0],), (contract[1],)), ((), ()))
    return lax.dot_general(a, b, dims, preferred_element_type=F32)


def call(kernel, ins, outs, scratch=(), flops=0, scalars=1, column=None, room=20):
    moved = sum(math.prod(a.shape) * a.dtype.itemsize for a in (*ins, *outs))

    def whole(a):
        return pl.BlockSpec(a.shape, lambda i, *_: (0,) * len(a.shape))

    def spec(a):
        if column and a.shape[-1] > column[0] and a.ndim == 2 and a.dtype == BF16:
            pick = column[1]
            return pl.BlockSpec((a.shape[0], column[0]), lambda i, at, *_: (0, pick(at)))
        return whole(a)

    return pl.pallas_call(
        kernel,
        grid_spec=pltpu.PrefetchScalarGridSpec(
            num_scalar_prefetch=scalars,
            grid=(1,),
            in_specs=[spec(a) for a in ins[scalars:]],
            out_specs=[whole(a) for a in outs],
            scratch_shapes=scratch,
        ),
        out_shape=outs,
        compiler_params=pltpu.CompilerParams(vmem_limit_bytes=room * 2**20),
        cost_estimate=pl.CostEstimate(flops=flops, bytes_accessed=moved, transcendentals=0),
    )(*ins)


def lanes(index, size):
    return pl.ds(pl.multiple_of(index * size, size), size)


def cut_kernel(cn, at, decay, seg_len, *refs):
    weights, outs = refs[:3], refs[3:]
    w_rows = weights[0].shape[0]
    row = lax.broadcasted_iota(jnp.int32, (META, DH), 0)
    length = jnp.full((META, DH), seg_len[0], jnp.int32).astype(F32)
    for j, out in enumerate(outs):
        for e in range(cn):
            head = (at[0] ^ j) * cn + e
            rest = jnp.full((META, DH), decay[head], F32)
            for i, w in enumerate(weights):
                first = (e * 3 + i) * DH
                out[:w_rows, first : first + DH] = w[:, lanes(head, DH)]
                term = rest.astype(BF16).astype(F32)
                rest = rest - term
                out[w_rows:, first : first + DH] = jnp.where(row < META // 2, term, length).astype(BF16)


def norm_kernel(n_head, at, gain, *refs):
    parts, out = refs[:n_head], refs[n_head]
    feat = parts[0].shape[1]
    wide = [part[...].astype(F32) for part in parts]
    squares = sum(jnp.sum(w * w, axis=1, keepdims=True) for w in wide)
    inverse = lax.rsqrt(squares / (feat * n_head) + 1e-05)
    for k, w in enumerate(wide):
        half = lanes(lax.rem(at[3] + n_head - k, n_head), feat)
        out[:, half] = (w * inverse * gain[:, half]).astype(BF16)


def project(xn, cn, at, rows, weights, chunk, meta, each):
    x, c = at[1], at[2]
    w_rows = weights[0].shape[0] - META
    row = lax.broadcasted_iota(jnp.int32, (META, DH), 0)
    for n, w in enumerate(weights):
        xi, ci = lax.rem(x + xn - n // cn, xn), c ^ (n % cn)
        chunk[pl.ds(pl.multiple_of((xi * cn + ci) * w_rows, w_rows), w_rows), :] = w[:w_rows]
        tail = w[w_rows:].astype(F32)
        terms = tail[:, : 3 * DH]
        for e in range(1, cn):
            terms = jnp.where(c == e, tail[:, e * 3 * DH : (e + 1) * 3 * DH], terms)
        total = terms[:, :DH] + terms[:, DH : 2 * DH] + terms[:, 2 * DH :]
        meta[xi, ci] = jnp.where(row < META // 2, total, terms[:, :DH])
    for first in range(0, len(rows), 2):
        pair = range(first, min(first + 2, len(rows)))
        sums = dot(jnp.concatenate([rows[i][...] for i in pair]), chunk[...])
        for n, i in enumerate(pair):
            size = sums.shape[0] // len(pair)
            each(i, sums[n * size : (n + 1) * size])


def project_kernel(zn, xn, cn, steps, at, *refs):
    rows = refs[:zn]
    weights = refs[zn : zn + len(steps) * xn * cn]
    out, meta, chunk = refs[-3:]
    size = chunk.shape[1]
    for n, j in enumerate(steps):

        def each(i, sums):
            out[i] = sums if n == 0 else out[i] + sums

        part = [row.at[:, lanes(at[0] ^ j, size)] for row in rows]
        few = weights[n * xn * cn : (n + 1) * xn * cn]
        project(xn, cn, at, part, few, chunk.at[n], meta.at[n], each)


def finish_kernel(zn, xn, cn, at, *refs):
    rows = refs[:zn]
    weights = refs[zn : zn + xn * cn]
    before = refs[zn + xn * cn] if zn > 1 else None
    outs, meta, chunk = refs[-2 - cn : -2], refs[-2], refs[-1]
    c = at[2]

    def each(i, sums):
        sums = (sums if before is None else sums + before[i]).astype(BF16)
        heads = [sums[:, e * 3 * DH : (e + 1) * 3 * DH] for e in range(cn)]
        for m, out in enumerate(outs):
            pick = heads[m]
            for e in range(cn):
                if e != m:
                    pick = jnp.where((c ^ m) == e, heads[e], pick)
            out[i] = pick

    project(xn, cn, at, rows, weights, chunk, meta.at[0], each)


def segment_info(table):
    def retain(zi, xi, ci):
        return table[zi, xi, ci, 0:1, 0:1]

    def length(zi, xi, ci):
        return table[zi, xi, ci, META // 2 : META // 2 + 1, 0:1]

    return retain, length


def write_kernel(zn, xn, cn, at, *refs):
    parts, query, metas = refs[:cn], refs[cn], refs[cn + 1 : -5]
    sums, written, group, group16, table = refs[-5:]
    z, x, c = at[0], at[1], at[2]
    j = 0
    for meta in metas:
        for n in range(meta.shape[0]):
            table[z ^ j] = meta[n]
            j += 1
    retain, length = segment_info(table)
    seg_rows = sums.shape[2]
    for i in range(zn):
        for m in range(cn):
            sums[z ^ i, c ^ m] = parts[m][i]
    own = query[:, lanes(z * cn + c, DH)]
    slots = own.shape[0]
    position = lax.broadcasted_iota(jnp.int32, (slots, seg_rows), 1).astype(F32)
    for i in range(zn):
        keys = sums[i, :, :, DH : 2 * DH].reshape(cn * seg_rows, DH)
        scores = dot(own, keys, (1, 1)) * (1.0 / math.sqrt(DH))
        gates = jax.nn.sigmoid(scores - math.log(seg_rows))
        total = None
        for m in range(cn):
            gate = gates[:, m * seg_rows : (m + 1) * seg_rows]
            gate = jnp.where(position < length(i, x, m), gate, 0.0).astype(BF16)
            new = dot(gate, sums[i, m, :, DH:])
            written[i, m] = new
            total = new if total is None else retain(i, x, m) * total + new
        group[i] = total
        group16[i] = total.astype(BF16)


def token_kernel(zn, cn, slots, at, scale, table, sums, out):
    _, length = segment_info(table)
    seg_rows = sums.shape[2]
    shape = (seg_rows, seg_rows)
    row = lax.broadcasted_iota(jnp.int32, shape, 0)
    column = lax.broadcasted_iota(jnp.int32, shape, 1)
    factor = scale[at[0] * cn + at[2]] * (1.0 / math.sqrt(DH))
    for i in range(zn):
        for m in range(cn):
            query, keys, values = (sums[i, m, :, n * DH : (n + 1) * DH] for n in range(3))
            scores = dot(query, keys, (1, 1)) * factor
            gate = jax.nn.sigmoid(scores - math.log(slots + seg_rows))
            allowed = (column <= row) & (column.astype(F32) < length(i, at[1], m))
            out[i, m] = dot(jnp.where(allowed, gate, 0.0).astype(BF16), values)


def memory_kernel(zn, xn, cn, at, scale, table, sums, token, written, group, *refs):
    others = refs[: xn - 1]
    outs = refs[xn - 1 : xn - 1 + zn]
    groups, done = refs[-2:]
    z, x, c = at[0], at[1], at[2]
    retain, length = segment_info(table)
    slots, seg_rows = group.shape[1], sums.shape[2]
    factor = scale[z * cn + c] * (1.0 / math.sqrt(DH))
    bias = math.log(slots + seg_rows)
    row = lax.broadcasted_iota(jnp.int32, (seg_rows, DH), 0).astype(F32)
    groups[x] = group[...]
    for k, other in enumerate(others, 1):
        groups[lax.rem(x + xn - k, xn)] = other[...].astype(F32)
    memory = jnp.zeros(group.shape[1:], F32)
    for i in range(zn):
        entry = memory
        for k in range(xn):
            if k:
                entry = jnp.where(x == k, memory, entry)
            kept = retain(i, k, 0)
            for m in range(1, cn):
                kept = kept * retain(i, k, m)
            memory = kept * memory + groups[k, i]
        for m in range(cn):
            units = []
            for n in range(2):
                part = entry[:, n * DH : (n + 1) * DH]
                mean = jnp.mean(part * part, axis=1, keepdims=True)
                units.append((part * lax.rsqrt(mean + 1e-06)).astype(BF16))
            scores = dot(sums[i, m, :, :DH], units[0], (1, 1)) * factor
            gate = jax.nn.sigmoid(scores - bias).astype(BF16)
            total = dot(gate, units[1]) + token[i, m]
            done[i, m] = jnp.where(row < length(i, x, m), total, 0.0).astype(BF16)
            if m + 1 < cn:
                entry = retain(i, x, m) * entry + written[i, m]
    for j in range(zn):
        for m in range(cn):
            outs[j][m] = done[z ^ j, c ^ m]


def out_kernel(zn, xn, cn, n_head, at, *refs):
    attended = refs[: zn * cn]
    weights = refs[zn * cn : zn * cn + zn * xn]
    outs, rows = refs[-1 - cn * n_head : -1], refs[-1]
    z, x, c, y = at[0], at[1], at[2], at[3]
    seg_rows = attended[0].shape[1]
    for j in range(zn):
        for e in range(cn):
            for m in range(cn):
                rows[m * seg_rows : (m + 1) * seg_rows, lanes((z ^ j) * cn + (c ^ e), DH)] = (
                    attended[j * cn + e][m ^ e]
                )
    blocks = outs[0].shape[0]
    for j in range(zn):
        for k in range(xn):
            product = dot(rows[...], weights[j * xn + k][...]).astype(BF16)
            spot = (z ^ j) * xn + lax.rem(x + xn - k, xn)
            turn = lax.rem(spot // blocks + n_head - y, n_head)
            for r in range(n_head):

                @pl.when(turn == r)
                def _():
                    for m in range(cn):
                        outs[r * cn + m][lax.rem(spot, blocks)] = product[
                            m * seg_rows : (m + 1) * seg_rows
                        ]


def sum_kernel(n_head, cn, at, *refs):
    out = refs[-1]
    blocks, _, size = refs[0].shape
    for b in range(blocks):
        totals = [
            sum(refs[r * cn + e][b].astype(F32) for r in range(n_head)).astype(BF16)
            for e in range(cn)
        ]
        for m in range(cn):
            total = totals[0]
            for e in range(1, cn):
                total = jnp.where((at[2] ^ e) == m, totals[e], total)
            first = (b * cn + m) * size
            out[:, first : first + size] = total


def body(tokens, gain, w_query, w_key, w_value, w_out, mem_query, score_scale, decay, seg_len):
    n_seq = lax.axis_size("seq")
    n_head = lax.axis_size("head")
    seg_rows, feat_local = tokens.shape
    width = gain.shape[0]
    w_rows, col_local = w_query.shape
    heads = col_local // DH
    slots = mem_query.shape[0]
    cn = 2 if heads % 2 == 0 else 1
    zn = heads // cn
    xn = n_seq // heads
    place = lax.axis_index("seq")
    y = lax.axis_index("head")
    at = jnp.stack([place // (cn * xn), place // cn % xn, place % cn, y]).astype(jnp.int32)

    def shape(dims, dtype=BF16):
        return jax.ShapeDtypeStruct(dims, dtype)

    def split(s):
        return s // (cn * xn), s // cn % xn, s % cn

    def join(a, b, d):
        return (a * xn + b) * cn + d

    def over_z(a, j):
        pairs = [(s, join(split(s)[0] ^ j, *split(s)[1:])) for s in range(n_seq)]
        return lax.ppermute(a, "seq", pairs)

    def over_x(a, k):
        pairs = []
        for s in range(n_seq):
            sz, sx, sc = split(s)
            pairs.append((s, join(sz, (sx + k) % xn, sc)))
        return lax.ppermute(a, "seq", pairs)

    def over_c(a, m):
        return lax.ppermute(a, "seq", [(s, s ^ m) for s in range(n_seq)])

    def over_y(a, k):
        return lax.ppermute(a, "head", [(h, (h + k) % n_head) for h in range(n_head)])

    chain = []

    def mark(a):
        chain[:] = [a]
        return a

    def done(a):
        return mark(lax.optimization_barrier((a, *chain))[0])

    def done_all(*lists):
        flat = [part for parts in lists for part in parts]
        if flat:
            flat = lax.optimization_barrier((*flat, *chain))[: len(flat)]
            mark(flat[-1])
        flat = iter(flat)
        return [[next(flat) for _ in parts] for parts in lists]

    def after(a, b):
        return lax.optimization_barrier((a, b))[0]

    last = zn - 1
    tok, packs, pieces, rows = {0: tokens}, {}, {}, {}
    started, columns, out_z = {}, {}, {0: w_out}

    def begin_tok(j):
        low = j & -j
        if j < zn and j not in started and j ^ low in tok:
            started[j] = over_z(tok[j ^ low], low)

    def begin_y(j):
        started["y", j] = [over_y(tok[j], k) for k in range(1, n_head)]

    def end_y(j, others):
        (rows[j],) = call(
            functools.partial(norm_kernel, n_head),
            (at, gain[None], tok[j], *others),
            [shape((seg_rows, width))],
        )
        mark(rows[j])

    def both(a):
        return [over_c(a, m) if m else a for m in range(cn)]

    def begin_x(j):
        started["x", j] = [over_x(packs[j], k) for k in range(1, xn)]
        pieces[j] = both(packs[j])

    def end_x(j, others):
        for part in others:
            pieces[j] += both(part)

    def begin_out(j, source):
        started["o", j] = [over_x(source, k) for k in range(1, xn)]
        columns[j] = [source]

    def end_out(j):
        columns[j] += [done(part) for part in started["o", j]]

    for bit in range(zn.bit_length() - 2, -1, -1):
        begin_tok(1 << bit)
    begin_y(0)
    begin_out(0, w_out)
    sent = call(
        functools.partial(cut_kernel, cn),
        (at, decay[0], seg_len, w_query, w_key, w_value),
        [shape((w_rows + META, cn * 3 * DH))] * zn,
        scalars=3,
    )
    packs[0] = sent[0]
    begin_x(0)
    if last:
        started["w", 1] = over_z(sent[1], 1)

    bits = [1 << n for n in range(zn.bit_length() - 1)]
    more = [j for j in range(1, zn) if j not in bits]
    parts, first, whole, columns[0][1:] = done_all(
        [started[b] for b in bits], started["y", 0], started["x", 0], started["o", 0]
    )
    tok.update(zip(bits, parts))
    end_x(0, whole)
    for b in bits:
        begin_y(b)
    for j in more:
        begin_tok(j)
    early = range(1, min(3, zn))
    for j in early[1:]:
        started["w", j] = over_z(after(sent[j], tok[1]), j)
    end_y(0, first)
    parts, far, *near = done_all(
        [started["w", j] for j in early],
        [started[j] for j in more],
        *(started["y", b] for b in bits),
    )
    packs.update(zip(early, parts))
    tok.update(zip(more, far))
    for j in range(len(early) + 1, zn):
        started["w", j] = over_z(after(sent[j], packs[j - 1]), j)
    for j in more:
        begin_y(j)
    for j in early:
        begin_x(j)
    if last:
        started["oz", 1] = over_z(after(w_out, packs[early[-1]]), 1)
    for b, others in zip(bits, near):
        end_y(b, others)
    for j in more:
        end_y(j, done_all(started["y", j])[0])
    for j in range(len(early) + 1, zn):
        packs[j] = done(started["w", j])
        begin_x(j)
    for b in bits[1:]:
        started["oz", b] = over_z(after(w_out, packs[last]), b)
    for j in range(1, last):
        end_x(j, done_all(started["x", j])[0])
    if last:
        out_z[1] = done(started["oz", 1])
        begin_out(1, out_z[1])
    rows = [rows[j] for j in range(zn)]

    chunk_rows = xn * cn * w_rows
    flops = 2 * zn * seg_rows * chunk_rows * cn * 3 * DH
    before = []
    if last:
        before = call(
            functools.partial(project_kernel, zn, xn, cn, range(last)),
            (at, *rows, *sum((pieces[j] for j in range(last)), [])),
            [
                shape((zn, seg_rows, cn * 3 * DH), F32),
                shape((last, xn, cn, META, DH), F32),
            ],
            [pltpu.VMEM((last, chunk_rows, cn * 3 * DH), BF16)],
            flops * last,
            room=48,
        )
        mark(before[0])
    if last:
        parts, others, columns[1][1:] = done_all(
            [started["oz", b] for b in bits[1:]], started["x", last], started["o", 1]
        )
        end_x(last, others)
        out_z.update(zip(bits[1:], parts))
        for b in bits[1:]:
            begin_out(b, out_z[b])
        for j in more:
            started["oz", j] = over_z(out_z[j ^ (j & -j)], j & -j)
    *parts, meta = call(
        functools.partial(finish_kernel, zn, xn, cn),
        (at, *rows, *pieces[last], *before[:1]),
        [shape((zn, seg_rows, 3 * DH))] * cn + [shape((1, xn, cn, META, DH), F32)],
        [pltpu.VMEM((chunk_rows, cn * 3 * DH), BF16)],
        flops,
        column=(chunk_rows, lambda at: at[0] ^ last),
        room=32,
    )
    parts = [done(over_c(part, m)) if m else part for m, part in enumerate(parts)]
    sums, written, group, group16, table = call(
        functools.partial(write_kernel, zn, xn, cn),
        (at, *parts, mem_query, *before[1:], meta),
        [
            shape((zn, cn, seg_rows, 3 * DH)),
            shape((zn, cn, slots, 2 * DH), F32),
            shape((zn, slots, 2 * DH), F32),
            shape((zn, slots, 2 * DH)),
            shape((zn, xn, cn, META, DH), F32),
        ],
    )
    others = [over_x(group16, k) for k in range(1, xn)]
    (token,) = call(
        functools.partial(token_kernel, zn, cn, slots),
        (at, score_scale, table, sums),
        [shape((zn, cn, seg_rows, DH), F32)],
        scalars=2,
    )
    mark(token)
    others, parts = done_all(others, [started["oz", j] for j in more])
    for j, part in zip(more, parts):
        begin_out(j, part)
    attended = call(
        functools.partial(memory_kernel, zn, xn, cn),
        (at, score_scale, table, sums, token, written, group, *others),
        [shape((cn, seg_rows, DH))] * zn,
        [
            pltpu.VMEM((xn, zn, slots, 2 * DH), F32),
            pltpu.VMEM((zn, cn, seg_rows, DH), BF16),
        ],
        scalars=2,
    )

    here = [over_z(block, j) if j else block for j, block in enumerate(attended)]
    for j in range(1, zn):
        here[j] = done(here[j])
    swapped = [[over_c(here[j], m) for m in range(1, cn)] for j in range(zn)]
    here = sum(([here[j]] + [done(a) for a in swapped[j]] for j in range(zn)), [])

    for j in range(2, zn):
        end_out(j)
    columns = sum((columns[j] for j in range(zn)), [])
    out_cols = w_out.shape[1]
    blocks = feat_local // (cn * out_cols)
    products = call(
        functools.partial(out_kernel, zn, xn, cn, n_head),
        (at, *here, *columns),
        [shape((blocks, seg_rows, out_cols))] * (cn * n_head),
        [pltpu.VMEM((cn * seg_rows, heads * DH), BF16)],
        2 * cn * seg_rows * heads * DH * zn * xn * out_cols,
        room=32,
    )
    mine = []
    for r in range(n_head):
        for m in range(cn):
            block = products[r * cn + m]
            block = over_c(block, m) if m else block
            mine.append(over_y(block, r) if r else block)
    (branch,) = call(
        functools.partial(sum_kernel, n_head, cn),
        (at, *mine),
        [shape((seg_rows, feat_local))],
    )
    return branch


def solution(mesh):
    return jax.shard_map(
        body,
        mesh=mesh,
        in_specs=(
            P("seq", "head"),
            P(),
            P("seq", "head"),
            P("seq", "head"),
            P("seq", "head"),
            P("head", "seq"),
            P(None, "head"),
            P("head"),
            P("seq", "head"),
            P("seq"),
        ),
        out_specs=P("seq", "head"),
        check_vma=False,
    )
```

```python
import functools
import math

import jax
import jax.numpy as jnp
from jax import lax
from jax.experimental import pallas as pl
from jax.experimental.pallas import tpu as pltpu
from jax.sharding import PartitionSpec as P

DH = 128
META = 16
F32 = jnp.float32
BF16 = jnp.bfloat16


def dot(a, b, contract=(1, 0)):
    dims = (((contract[0],), (contract[1],)), ((), ()))
    return lax.dot_general(a, b, dims, preferred_element_type=F32)


def call(kernel, ins, outs, scratch=(), flops=0, scalars=1, column=None, room=12):
    moved = sum(math.prod(a.shape) * a.dtype.itemsize for a in (*ins, *outs))

    def whole(a):
        return pl.BlockSpec(a.shape, lambda i, *_: (0,) * len(a.shape))

    def spec(a):
        if column and a.shape[-1] > column[0] and a.ndim == 2 and a.dtype == BF16:
            pick = column[1]
            return pl.BlockSpec((a.shape[0], column[0]), lambda i, at, *_: (0, pick(at)))
        return whole(a)

    return pl.pallas_call(
        kernel,
        grid_spec=pltpu.PrefetchScalarGridSpec(
            num_scalar_prefetch=scalars,
            grid=(1,),
            in_specs=[spec(a) for a in ins[scalars:]],
            out_specs=[whole(a) for a in outs],
            scratch_shapes=scratch,
        ),
        out_shape=outs,
        compiler_params=pltpu.CompilerParams(vmem_limit_bytes=room * 2**20),
        cost_estimate=pl.CostEstimate(flops=flops, bytes_accessed=moved, transcendentals=0),
    )(*ins)


def lanes(index, size):
    return pl.ds(pl.multiple_of(index * size, size), size)


def cut_kernel(cn, at, decay, seg_len, *refs):
    weights, outs = refs[:3], refs[3:]
    w_rows = weights[0].shape[0]
    row = lax.broadcasted_iota(jnp.int32, (META, DH), 0)
    length = jnp.full((META, DH), seg_len[0], jnp.int32).astype(F32)
    for j, out in enumerate(outs):
        for e in range(cn):
            head = (at[0] ^ j) * cn + e
            rest = jnp.full((META, DH), decay[head], F32)
            for i, w in enumerate(weights):
                first = (e * 3 + i) * DH
                out[:w_rows, first : first + DH] = w[:, lanes(head, DH)]
                term = rest.astype(BF16).astype(F32)
                rest = rest - term
                out[w_rows:, first : first + DH] = jnp.where(row < META // 2, term, length).astype(BF16)


def norm_kernel(n_head, at, gain, *refs):
    parts, out = refs[:n_head], refs[n_head]
    feat = parts[0].shape[1]
    wide = [part[...].astype(F32) for part in parts]
    squares = sum(jnp.sum(w * w, axis=1, keepdims=True) for w in wide)
    inverse = lax.rsqrt(squares / (feat * n_head) + 1e-05)
    for k, w in enumerate(wide):
        half = lanes(lax.rem(at[3] + n_head - k, n_head), feat)
        out[:, half] = (w * inverse * gain[:, half]).astype(BF16)


def project(xn, cn, at, rows, weights, chunk, meta, each):
    x, c = at[1], at[2]
    w_rows = weights[0].shape[0] - META
    row = lax.broadcasted_iota(jnp.int32, (META, DH), 0)
    for n, w in enumerate(weights):
        xi, ci = lax.rem(x + xn - n // cn, xn), c ^ (n % cn)
        chunk[pl.ds(pl.multiple_of((xi * cn + ci) * w_rows, w_rows), w_rows), :] = w[:w_rows]
        tail = w[w_rows:].astype(F32)
        terms = tail[:, : 3 * DH]
        for e in range(1, cn):
            terms = jnp.where(c == e, tail[:, e * 3 * DH : (e + 1) * 3 * DH], terms)
        total = terms[:, :DH] + terms[:, DH : 2 * DH] + terms[:, 2 * DH :]
        meta[xi, ci] = jnp.where(row < META // 2, total, terms[:, :DH])
    for first in range(0, len(rows), 2):
        pair = range(first, min(first + 2, len(rows)))
        sums = dot(jnp.concatenate([rows[i][...] for i in pair]), chunk[...])
        for n, i in enumerate(pair):
            size = sums.shape[0] // len(pair)
            each(i, sums[n * size : (n + 1) * size])


def project_kernel(zn, xn, cn, steps, at, *refs):
    rows = refs[:zn]
    weights = refs[zn : zn + len(steps) * xn * cn]
    out, meta, chunk = refs[-3:]
    size = chunk.shape[1]
    for n, j in enumerate(steps):

        def each(i, sums):
            out[i] = sums if n == 0 else out[i] + sums

        part = [row.at[:, lanes(at[0] ^ j, size)] for row in rows]
        few = weights[n * xn * cn : (n + 1) * xn * cn]
        project(xn, cn, at, part, few, chunk.at[n], meta.at[n], each)


def finish_kernel(zn, xn, cn, at, *refs):
    rows = refs[:zn]
    weights = refs[zn : zn + xn * cn]
    before = refs[zn + xn * cn] if zn > 1 else None
    outs, meta, chunk = refs[-2 - cn : -2], refs[-2], refs[-1]
    c = at[2]

    def each(i, sums):
        sums = (sums if before is None else sums + before[i]).astype(BF16)
        heads = [sums[:, e * 3 * DH : (e + 1) * 3 * DH] for e in range(cn)]
        for m, out in enumerate(outs):
            pick = heads[m]
            for e in range(cn):
                if e != m:
                    pick = jnp.where((c ^ m) == e, heads[e], pick)
            out[i] = pick

    project(xn, cn, at, rows, weights, chunk, meta.at[0], each)


def segment_info(table):
    def retain(zi, xi, ci):
        return table[zi, xi, ci, 0:1, 0:1]

    def length(zi, xi, ci):
        return table[zi, xi, ci, META // 2 : META // 2 + 1, 0:1]

    return retain, length


def write_kernel(zn, xn, cn, at, *refs):
    parts, query, metas = refs[:cn], refs[cn], refs[cn + 1 : -5]
    sums, written, group, group16, table = refs[-5:]
    z, x, c = at[0], at[1], at[2]
    j = 0
    for meta in metas:
        for n in range(meta.shape[0]):
            table[z ^ j] = meta[n]
            j += 1
    retain, length = segment_info(table)
    seg_rows = sums.shape[2]
    for i in range(zn):
        for m in range(cn):
            sums[z ^ i, c ^ m] = parts[m][i]
    own = query[:, lanes(z * cn + c, DH)]
    slots = own.shape[0]
    position = lax.broadcasted_iota(jnp.int32, (slots, seg_rows), 1).astype(F32)
    for i in range(zn):
        keys = sums[i, :, :, DH : 2 * DH].reshape(cn * seg_rows, DH)
        scores = dot(own, keys, (1, 1)) * (1.0 / math.sqrt(DH))
        gates = jax.nn.sigmoid(scores - math.log(seg_rows))
        total = None
        for m in range(cn):
            gate = gates[:, m * seg_rows : (m + 1) * seg_rows]
            gate = jnp.where(position < length(i, x, m), gate, 0.0).astype(BF16)
            new = dot(gate, sums[i, m, :, DH:])
            written[i, m] = new
            total = new if total is None else retain(i, x, m) * total + new
        group[i] = total
        group16[i] = total.astype(BF16)


def token_kernel(zn, cn, slots, at, scale, table, sums, out):
    _, length = segment_info(table)
    seg_rows = sums.shape[2]
    shape = (seg_rows, seg_rows)
    row = lax.broadcasted_iota(jnp.int32, shape, 0)
    column = lax.broadcasted_iota(jnp.int32, shape, 1)
    factor = scale[at[0] * cn + at[2]] * (1.0 / math.sqrt(DH))
    for i in range(zn):
        for m in range(cn):
            query, keys, values = (sums[i, m, :, n * DH : (n + 1) * DH] for n in range(3))
            scores = dot(query, keys, (1, 1)) * factor
            gate = jax.nn.sigmoid(scores - math.log(slots + seg_rows))
            allowed = (column <= row) & (column.astype(F32) < length(i, at[1], m))
            out[i, m] = dot(jnp.where(allowed, gate, 0.0).astype(BF16), values)


def memory_kernel(zn, xn, cn, at, scale, table, sums, token, written, group, *refs):
    others = refs[: xn - 1]
    outs = refs[xn - 1 : xn - 1 + zn]
    groups, done = refs[-2:]
    z, x, c = at[0], at[1], at[2]
    retain, length = segment_info(table)
    slots, seg_rows = group.shape[1], sums.shape[2]
    factor = scale[z * cn + c] * (1.0 / math.sqrt(DH))
    bias = math.log(slots + seg_rows)
    row = lax.broadcasted_iota(jnp.int32, (seg_rows, DH), 0).astype(F32)
    groups[x] = group[...]
    for k, other in enumerate(others, 1):
        groups[lax.rem(x + xn - k, xn)] = other[...].astype(F32)
    memory = jnp.zeros(group.shape[1:], F32)
    for i in range(zn):
        entry = memory
        for k in range(xn):
            if k:
                entry = jnp.where(x == k, memory, entry)
            kept = retain(i, k, 0)
            for m in range(1, cn):
                kept = kept * retain(i, k, m)
            memory = kept * memory + groups[k, i]
        for m in range(cn):
            units = []
            for n in range(2):
                part = entry[:, n * DH : (n + 1) * DH]
                mean = jnp.mean(part * part, axis=1, keepdims=True)
                units.append((part * lax.rsqrt(mean + 1e-06)).astype(BF16))
            scores = dot(sums[i, m, :, :DH], units[0], (1, 1)) * factor
            gate = jax.nn.sigmoid(scores - bias).astype(BF16)
            total = dot(gate, units[1]) + token[i, m]
            done[i, m] = jnp.where(row < length(i, x, m), total, 0.0).astype(BF16)
            if m + 1 < cn:
                entry = retain(i, x, m) * entry + written[i, m]
    for j in range(zn):
        for m in range(cn):
            outs[j][m] = done[z ^ j, c ^ m]


def out_kernel(zn, xn, cn, n_head, slots, at, *refs):
    attended = refs[: zn * cn]
    weights = refs[zn * cn : zn * cn + len(slots) * xn]
    outs, rows = refs[-1 - cn * n_head : -1], refs[-1]
    z, x, c, y = at[0], at[1], at[2], at[3]
    seg_rows = attended[0].shape[1]
    for j in range(zn):
        for e in range(cn):
            for m in range(cn):
                rows[m * seg_rows : (m + 1) * seg_rows, lanes((z ^ j) * cn + (c ^ e), DH)] = (
                    attended[j * cn + e][m ^ e]
                )
    blocks = outs[0].shape[0]
    share = zn * xn // n_head
    for n, j in enumerate(slots):
        for k in range(xn):
            product = dot(rows[...], weights[n * xn + k][...]).astype(BF16)
            spot = (z ^ j) * xn + lax.rem(x + xn - k, xn)
            turn = lax.rem(spot // share + n_head - y, n_head)
            for r in range(n_head):

                @pl.when(turn == r)
                def _():
                    for m in range(cn):
                        outs[r * cn + m][lax.rem(spot, blocks)] = product[
                            m * seg_rows : (m + 1) * seg_rows
                        ]


def sum_kernel(n_head, cn, phases, at, *refs):
    out = refs[-1]
    blocks, seg_rows, size = refs[0].shape
    for p in range(phases):
        few = refs[p * n_head * cn : (p + 1) * n_head * cn]
        places = []
        for b in range(blocks):
            totals = [
                sum(few[r * cn + e][b].astype(F32) for r in range(n_head)).astype(BF16)
                for e in range(cn)
            ]
            for m in range(cn):
                total = totals[0]
                for e in range(1, cn):
                    total = jnp.where((at[2] ^ e) == m, totals[e], total)
                places.append(total)
        out[:, lanes(lax.rem(at[0] ^ p, phases), blocks * cn * size)] = jnp.concatenate(places, 1)


def body(tokens, gain, w_query, w_key, w_value, w_out, mem_query, score_scale, decay, seg_len):
    n_seq = lax.axis_size("seq")
    n_head = lax.axis_size("head")
    seg_rows, feat_local = tokens.shape
    width = gain.shape[0]
    w_rows, col_local = w_query.shape
    heads = col_local // DH
    slots = mem_query.shape[0]
    cn = 2 if heads % 2 == 0 else 1
    zn = heads // cn
    xn = n_seq // heads
    place = lax.axis_index("seq")
    y = lax.axis_index("head")
    at = jnp.stack([place // (cn * xn), place // cn % xn, place % cn, y]).astype(jnp.int32)

    def shape(dims, dtype=BF16):
        return jax.ShapeDtypeStruct(dims, dtype)

    def split(s):
        return s // (cn * xn), s // cn % xn, s % cn

    def join(a, b, d):
        return (a * xn + b) * cn + d

    def over_z(a, j):
        pairs = [(s, join(split(s)[0] ^ j, *split(s)[1:])) for s in range(n_seq)]
        return lax.ppermute(a, "seq", pairs)

    def over_x(a, k):
        pairs = []
        for s in range(n_seq):
            sz, sx, sc = split(s)
            pairs.append((s, join(sz, (sx + k) % xn, sc)))
        return lax.ppermute(a, "seq", pairs)

    def over_c(a, m):
        return lax.ppermute(a, "seq", [(s, s ^ m) for s in range(n_seq)])

    def over_y(a, k):
        return lax.ppermute(a, "head", [(h, (h + k) % n_head) for h in range(n_head)])

    chain = []

    def mark(a):
        chain[:] = [a]
        return a

    def done(a):
        return mark(lax.optimization_barrier((a, *chain))[0])

    def done_all(*lists):
        flat = [part for parts in lists for part in parts]
        if flat:
            flat = lax.optimization_barrier((*flat, *chain))[: len(flat)]
            mark(flat[-1])
        flat = iter(flat)
        return [[next(flat) for _ in parts] for parts in lists]

    def after(a, b):
        return lax.optimization_barrier((a, b))[0]

    last = zn - 1
    tok, packs, pieces, rows = {0: tokens}, {}, {}, {}
    started, columns, out_z = {}, {}, {0: w_out}

    def begin_tok(j):
        low = j & -j
        if j < zn and j not in started and j ^ low in tok:
            started[j] = over_z(tok[j ^ low], low)

    def begin_y(j):
        started["y", j] = [over_y(tok[j], k) for k in range(1, n_head)]

    def end_y(j, others):
        (rows[j],) = call(
            functools.partial(norm_kernel, n_head),
            (at, gain[None], tok[j], *others),
            [shape((seg_rows, width))],
        )
        mark(rows[j])

    def both(a):
        return [over_c(a, m) if m else a for m in range(cn)]

    def begin_x(j):
        started["x", j] = [over_x(packs[j], k) for k in range(1, xn)]
        pieces[j] = both(packs[j])

    def end_x(j, others):
        for part in others:
            pieces[j] += both(part)

    def begin_out(j, source):
        started["o", j] = [over_x(source, k) for k in range(1, xn)]
        columns[j] = [source]

    def end_out(j):
        columns[j] += [done(part) for part in started["o", j]]

    for bit in range(zn.bit_length() - 2, -1, -1):
        begin_tok(1 << bit)
    begin_y(0)
    begin_out(0, w_out)
    sent = call(
        functools.partial(cut_kernel, cn),
        (at, decay[0], seg_len, w_query, w_key, w_value),
        [shape((w_rows + META, cn * 3 * DH))] * zn,
        scalars=3,
    )
    packs[0] = sent[0]
    begin_x(0)
    if last:
        started["w", 1] = over_z(sent[1], 1)

    bits = [1 << n for n in range(zn.bit_length() - 1)]
    more = [j for j in range(1, zn) if j not in bits]
    parts, first, whole = done_all([started[b] for b in bits], started["y", 0], started["x", 0])
    tok.update(zip(bits, parts))
    end_x(0, whole)
    for b in bits:
        begin_y(b)
    for j in more:
        begin_tok(j)
    early = range(1, min(3, zn))
    for j in early[1:]:
        started["w", j] = over_z(after(sent[j], tok[1]), j)
    end_y(0, first)
    parts, far, columns[0][1:], *near = done_all(
        [started["w", j] for j in early],
        [started[j] for j in more],
        started["o", 0],
        *(started["y", b] for b in bits),
    )
    packs.update(zip(early, parts))
    tok.update(zip(more, far))
    for j in range(len(early) + 1, zn):
        started["w", j] = over_z(after(sent[j], packs[j - 1]), j)
    for j in more:
        begin_y(j)
    if last:
        begin_x(1)
        started["oz", 1] = over_z(after(w_out, packs[early[-1]]), 1)
    for b, others in zip(bits, near):
        end_y(b, others)
    for j in early[1:]:
        packs[j] = lax.optimization_barrier((packs[j], *(rows[b] for b in bits)))[0]
        begin_x(j)
    for j in range(len(early) + 1, zn):
        packs[j] = done(started["w", j])
        begin_x(j)
    for b in bits[1:]:
        started["oz", b] = over_z(after(w_out, packs[last]), b)
    for j in more:
        end_y(j, done_all(started["y", j])[0])
    for j in range(1, last):
        end_x(j, done_all(started["x", j])[0])
    if last:
        out_z[1] = done(started["oz", 1])
        begin_out(1, out_z[1])
    rows = [rows[j] for j in range(zn)]

    chunk_rows = xn * cn * w_rows
    flops = 2 * zn * seg_rows * chunk_rows * cn * 3 * DH
    before = []
    if last:
        before = call(
            functools.partial(project_kernel, zn, xn, cn, range(last)),
            (at, *rows, *sum((pieces[j] for j in range(last)), [])),
            [
                shape((zn, seg_rows, cn * 3 * DH), F32),
                shape((last, xn, cn, META, DH), F32),
            ],
            [pltpu.VMEM((last, chunk_rows, cn * 3 * DH), BF16)],
            flops * last,
            room=30,
        )
        mark(before[0])
    if last:
        parts, others, columns[1][1:] = done_all(
            [started["oz", b] for b in bits[1:]], started["x", last], started["o", 1]
        )
        end_x(last, others)
        out_z.update(zip(bits[1:], parts))
        for b in bits[1:]:
            begin_out(b, out_z[b])
        for j in more:
            started["oz", j] = over_z(out_z[j ^ (j & -j)], j & -j)
    *parts, meta = call(
        functools.partial(finish_kernel, zn, xn, cn),
        (at, *rows, *pieces[last], *before[:1]),
        [shape((zn, seg_rows, 3 * DH))] * cn + [shape((1, xn, cn, META, DH), F32)],
        [pltpu.VMEM((chunk_rows, cn * 3 * DH), BF16)],
        flops,
        column=(chunk_rows, lambda at: at[0] ^ last),
        room=20,
    )
    parts = [done(over_c(part, m)) if m else part for m, part in enumerate(parts)]
    sums, written, group, group16, table = call(
        functools.partial(write_kernel, zn, xn, cn),
        (at, *parts, mem_query, *before[1:], meta),
        [
            shape((zn, cn, seg_rows, 3 * DH)),
            shape((zn, cn, slots, 2 * DH), F32),
            shape((zn, slots, 2 * DH), F32),
            shape((zn, slots, 2 * DH)),
            shape((zn, xn, cn, META, DH), F32),
        ],
    )
    others = [over_x(group16, k) for k in range(1, xn)]
    (token,) = call(
        functools.partial(token_kernel, zn, cn, slots),
        (at, score_scale, table, sums),
        [shape((zn, cn, seg_rows, DH), F32)],
        scalars=2,
    )
    mark(token)
    others, parts = done_all(others, [started["oz", j] for j in more])
    for j, part in zip(more, parts):
        begin_out(j, part)
    attended = call(
        functools.partial(memory_kernel, zn, xn, cn),
        (at, score_scale, table, sums, token, written, group, *others),
        [shape((cn, seg_rows, DH))] * zn,
        [
            pltpu.VMEM((xn, zn, slots, 2 * DH), F32),
            pltpu.VMEM((zn, cn, seg_rows, DH), BF16),
        ],
        scalars=2,
    )

    here = [over_z(block, j) if j else block for j, block in enumerate(attended)]
    for j in range(1, zn):
        here[j] = done(here[j])
    swapped = [[over_c(here[j], m) for m in range(1, cn)] for j in range(zn)]
    here = sum(([here[j]] + [done(a) for a in swapped[j]] for j in range(zn)), [])

    for j in range(2, zn):
        end_out(j)
    out_cols = w_out.shape[1]
    phases = zn // n_head if zn % n_head == 0 else 1
    blocks = feat_local // (cn * out_cols * phases)
    mine = []
    for p in range(phases):
        few = range(p, zn, phases)
        products = call(
            functools.partial(out_kernel, zn, xn, cn, n_head, few),
            (at, *here, *sum((columns[j] for j in few), [])),
            [shape((blocks, seg_rows, out_cols))] * (cn * n_head),
            [pltpu.VMEM((cn * seg_rows, heads * DH), BF16)],
            2 * cn * seg_rows * heads * DH * len(few) * xn * out_cols,
            room=20,
        )
        for r in range(n_head):
            for m in range(cn):
                block = products[r * cn + m]
                block = over_c(block, m) if m else block
                mine.append(over_y(block, r) if r else block)
    (branch,) = call(
        functools.partial(sum_kernel, n_head, cn, phases),
        (at, *mine),
        [shape((seg_rows, feat_local))],
    )
    return branch


def solution(mesh):
    return jax.shard_map(
        body,
        mesh=mesh,
        in_specs=(
            P("seq", "head"),
            P(),
            P("seq", "head"),
            P("seq", "head"),
            P("seq", "head"),
            P("head", "seq"),
            P(None, "head"),
            P("head"),
            P("seq", "head"),
            P("seq"),
        ),
        out_specs=P("seq", "head"),
        check_vma=False,
    )
```

```python
import functools
import math

import jax
import jax.numpy as jnp
from jax import lax
from jax.experimental import pallas as pl
from jax.experimental.pallas import tpu as pltpu
from jax.sharding import PartitionSpec as P

DH = 128
META = 16
F32 = jnp.float32
BF16 = jnp.bfloat16


def dot(a, b, contract=(1, 0)):
    dims = (((contract[0],), (contract[1],)), ((), ()))
    return lax.dot_general(a, b, dims, preferred_element_type=F32)


def call(kernel, ins, outs, scratch=(), flops=0, scalars=1, column=None, room=12):
    moved = sum(math.prod(a.shape) * a.dtype.itemsize for a in (*ins, *outs))

    def whole(a):
        return pl.BlockSpec(a.shape, lambda i, *_: (0,) * len(a.shape))

    def spec(a):
        if column and a.shape[-1] > column[0] and a.ndim == 2 and a.dtype == BF16:
            pick = column[1]
            return pl.BlockSpec((a.shape[0], column[0]), lambda i, at, *_: (0, pick(at)))
        return whole(a)

    return pl.pallas_call(
        kernel,
        grid_spec=pltpu.PrefetchScalarGridSpec(
            num_scalar_prefetch=scalars,
            grid=(1,),
            in_specs=[spec(a) for a in ins[scalars:]],
            out_specs=[whole(a) for a in outs],
            scratch_shapes=scratch,
        ),
        out_shape=outs,
        compiler_params=pltpu.CompilerParams(vmem_limit_bytes=room * 2**20),
        cost_estimate=pl.CostEstimate(flops=flops, bytes_accessed=moved, transcendentals=0),
    )(*ins)


def lanes(index, size):
    return pl.ds(pl.multiple_of(index * size, size), size)


def cut_kernel(cn, at, decay, seg_len, *refs):
    weights, outs = refs[:3], refs[3:]
    w_rows = weights[0].shape[0]
    row = lax.broadcasted_iota(jnp.int32, (META, DH), 0)
    length = jnp.full((META, DH), seg_len[0], jnp.int32).astype(F32)
    for j, out in enumerate(outs):
        for e in range(cn):
            head = (at[0] ^ j) * cn + e
            rest = jnp.full((META, DH), decay[head], F32)
            for i, w in enumerate(weights):
                first = (e * 3 + i) * DH
                out[:w_rows, first : first + DH] = w[:, lanes(head, DH)]
                term = rest.astype(BF16).astype(F32)
                rest = rest - term
                out[w_rows:, first : first + DH] = jnp.where(row < META // 2, term, length).astype(BF16)


def norm_kernel(n_head, at, gain, *refs):
    parts, out = refs[:n_head], refs[n_head]
    feat = parts[0].shape[1]
    wide = [part[...].astype(F32) for part in parts]
    squares = sum(jnp.sum(w * w, axis=1, keepdims=True) for w in wide)
    inverse = lax.rsqrt(squares / (feat * n_head) + 1e-05)
    for k, w in enumerate(wide):
        half = lanes(lax.rem(at[3] + n_head - k, n_head), feat)
        out[:, half] = (w * inverse * gain[:, half]).astype(BF16)


def project(xn, cn, at, rows, weights, chunk, meta, each):
    x, c = at[1], at[2]
    w_rows = weights[0].shape[0] - META
    row = lax.broadcasted_iota(jnp.int32, (META, DH), 0)
    for n, w in enumerate(weights):
        xi, ci = lax.rem(x + xn - n // cn, xn), c ^ (n % cn)
        chunk[pl.ds(pl.multiple_of((xi * cn + ci) * w_rows, w_rows), w_rows), :] = w[:w_rows]
        tail = w[w_rows:].astype(F32)
        terms = tail[:, : 3 * DH]
        for e in range(1, cn):
            terms = jnp.where(c == e, tail[:, e * 3 * DH : (e + 1) * 3 * DH], terms)
        total = terms[:, :DH] + terms[:, DH : 2 * DH] + terms[:, 2 * DH :]
        meta[xi, ci] = jnp.where(row < META // 2, total, terms[:, :DH])
    for first in range(0, len(rows), 2):
        pair = range(first, min(first + 2, len(rows)))
        sums = dot(jnp.concatenate([rows[i][...] for i in pair]), chunk[...])
        for n, i in enumerate(pair):
            size = sums.shape[0] // len(pair)
            each(i, sums[n * size : (n + 1) * size])


def project_kernel(zn, xn, cn, steps, at, *refs):
    rows = refs[:zn]
    weights = refs[zn : zn + len(steps) * xn * cn]
    out, meta, chunk = refs[-3:]
    size = chunk.shape[1]
    for n, j in enumerate(steps):

        def each(i, sums):
            out[i] = sums if n == 0 else out[i] + sums

        part = [row.at[:, lanes(at[0] ^ j, size)] for row in rows]
        few = weights[n * xn * cn : (n + 1) * xn * cn]
        project(xn, cn, at, part, few, chunk.at[n], meta.at[n], each)


def finish_kernel(zn, xn, cn, at, *refs):
    rows = refs[:zn]
    weights = refs[zn : zn + xn * cn]
    before = refs[zn + xn * cn] if zn > 1 else None
    meta, chunk = refs[-2:]
    outs = refs[zn + xn * cn + (before is not None) : -2]
    c = at[2]

    def each(i, sums):
        sums = (sums if before is None else sums + before[i]).astype(BF16)
        heads = [sums[:, e * 3 * DH : (e + 1) * 3 * DH] for e in range(cn)]
        half = outs[0].shape[0]
        for m in range(cn):
            pick = heads[m]
            for e in range(cn):
                if e != m:
                    pick = jnp.where((c ^ m) == e, heads[e], pick)
            outs[i // half * cn + m][i % half] = pick

    project(xn, cn, at, rows, weights, chunk, meta.at[0], each)


def segment_info(table):
    def retain(zi, xi, ci):
        return table[zi, xi, ci, 0:1, 0:1]

    def length(zi, xi, ci):
        return table[zi, xi, ci, META // 2 : META // 2 + 1, 0:1]

    return retain, length


def write_kernel(zn, xn, cn, halves, at, *refs):
    count = cn * halves
    parts, query, metas = refs[:count], refs[count], refs[count + 1 : -5]
    sums, written, group, group16, table = refs[-5:]
    z, x, c = at[0], at[1], at[2]
    j = 0
    for meta in metas:
        for n in range(meta.shape[0]):
            table[z ^ j] = meta[n]
            j += 1
    retain, length = segment_info(table)
    seg_rows = sums.shape[2]
    half = zn // halves
    for i in range(zn):
        for m in range(cn):
            sums[z ^ i, c ^ m] = parts[i // half * cn + m][i % half]
    own = query[:, lanes(z * cn + c, DH)]
    slots = own.shape[0]
    position = lax.broadcasted_iota(jnp.int32, (slots, seg_rows), 1).astype(F32)
    for i in range(zn):
        keys = sums[i, :, :, DH : 2 * DH].reshape(cn * seg_rows, DH)
        scores = dot(own, keys, (1, 1)) * (1.0 / math.sqrt(DH))
        gates = jax.nn.sigmoid(scores - math.log(seg_rows))
        total = None
        for m in range(cn):
            gate = gates[:, m * seg_rows : (m + 1) * seg_rows]
            gate = jnp.where(position < length(i, x, m), gate, 0.0).astype(BF16)
            new = dot(gate, sums[i, m, :, DH:])
            written[i, m] = new
            total = new if total is None else retain(i, x, m) * total + new
        group[i] = total
        group16[i] = total.astype(BF16)


def token_kernel(zn, cn, slots, at, scale, table, sums, out):
    _, length = segment_info(table)
    seg_rows = sums.shape[2]
    shape = (seg_rows, seg_rows)
    row = lax.broadcasted_iota(jnp.int32, shape, 0)
    column = lax.broadcasted_iota(jnp.int32, shape, 1)
    factor = scale[at[0] * cn + at[2]] * (1.0 / math.sqrt(DH))
    for i in range(zn):
        for m in range(cn):
            query, keys, values = (sums[i, m, :, n * DH : (n + 1) * DH] for n in range(3))
            scores = dot(query, keys, (1, 1)) * factor
            gate = jax.nn.sigmoid(scores - math.log(slots + seg_rows))
            allowed = (column <= row) & (column.astype(F32) < length(i, at[1], m))
            out[i, m] = dot(jnp.where(allowed, gate, 0.0).astype(BF16), values)


def memory_kernel(zn, xn, cn, at, scale, table, sums, token, written, group, *refs):
    others = refs[: xn - 1]
    outs = refs[xn - 1 : xn - 1 + zn]
    groups, done = refs[-2:]
    z, x, c = at[0], at[1], at[2]
    retain, length = segment_info(table)
    slots, seg_rows = group.shape[1], sums.shape[2]
    factor = scale[z * cn + c] * (1.0 / math.sqrt(DH))
    bias = math.log(slots + seg_rows)
    row = lax.broadcasted_iota(jnp.int32, (seg_rows, DH), 0).astype(F32)
    groups[x] = group[...]
    for k, other in enumerate(others, 1):
        groups[lax.rem(x + xn - k, xn)] = other[...].astype(F32)
    memory = jnp.zeros(group.shape[1:], F32)
    for i in range(zn):
        entry = memory
        for k in range(xn):
            if k:
                entry = jnp.where(x == k, memory, entry)
            kept = retain(i, k, 0)
            for m in range(1, cn):
                kept = kept * retain(i, k, m)
            memory = kept * memory + groups[k, i]
        for m in range(cn):
            units = []
            for n in range(2):
                part = entry[:, n * DH : (n + 1) * DH]
                mean = jnp.mean(part * part, axis=1, keepdims=True)
                units.append((part * lax.rsqrt(mean + 1e-06)).astype(BF16))
            scores = dot(sums[i, m, :, :DH], units[0], (1, 1)) * factor
            gate = jax.nn.sigmoid(scores - bias).astype(BF16)
            total = dot(gate, units[1]) + token[i, m]
            done[i, m] = jnp.where(row < length(i, x, m), total, 0.0).astype(BF16)
            if m + 1 < cn:
                entry = retain(i, x, m) * entry + written[i, m]
    for j in range(zn):
        for m in range(cn):
            outs[j][m] = done[z ^ j, c ^ m]


def out_kernel(zn, xn, cn, n_head, slots, turns, phases, at, *refs):
    attended = refs[: zn * cn]
    weights = refs[zn * cn : zn * cn + len(slots) * xn]
    outs, rows = refs[zn * cn + len(weights) : -1], refs[-1]
    z, x, c, y = at[0], at[1], at[2], at[3]
    seg_rows = attended[0].shape[1]
    for j in range(zn):
        for e in range(cn):
            for m in range(cn):
                rows[m * seg_rows : (m + 1) * seg_rows, lanes((z ^ j) * cn + (c ^ e), DH)] = (
                    attended[j * cn + e][m ^ e]
                )
    blocks = outs[0].shape[0]
    share = zn * xn // n_head
    for n, j in enumerate(slots):
        for k in range(xn):
            spot = (z ^ j) * xn + lax.rem(x + xn - k, xn)
            turn = lax.rem(spot // share + n_head - y, n_head)
            for i, r in enumerate(turns):

                @pl.when(turn == r)
                def _():
                    product = dot(rows[...], weights[n * xn + k][...]).astype(BF16)
                    for m in range(cn):
                        out = outs[(j % phases * len(turns) + i) * cn + m if len(slots) == zn else i * cn + m]
                        out[lax.rem(spot, blocks)] = product[m * seg_rows : (m + 1) * seg_rows]


def sum_kernel(n_head, cn, phases, at, *refs):
    out = refs[-1]
    blocks, seg_rows, size = refs[0].shape
    for p in range(phases):
        count = (n_head - 1) * cn
        few = refs[(phases * (n_head - 1) + p) * cn :][:cn] + refs[p * count : (p + 1) * count]
        places = []
        for b in range(blocks):
            totals = [
                sum(few[r * cn + e][b].astype(F32) for r in range(n_head)).astype(BF16)
                for e in range(cn)
            ]
            for m in range(cn):
                total = totals[0]
                for e in range(1, cn):
                    total = jnp.where((at[2] ^ e) == m, totals[e], total)
                places.append(total)
        out[:, lanes(lax.rem(at[0] ^ p, phases), blocks * cn * size)] = jnp.concatenate(places, 1)


def body(tokens, gain, w_query, w_key, w_value, w_out, mem_query, score_scale, decay, seg_len):
    n_seq = lax.axis_size("seq")
    n_head = lax.axis_size("head")
    seg_rows, feat_local = tokens.shape
    width = gain.shape[0]
    w_rows, col_local = w_query.shape
    heads = col_local // DH
    slots = mem_query.shape[0]
    cn = 2 if heads % 2 == 0 else 1
    zn = heads // cn
    xn = n_seq // heads
    place = lax.axis_index("seq")
    y = lax.axis_index("head")
    at = jnp.stack([place // (cn * xn), place // cn % xn, place % cn, y]).astype(jnp.int32)

    def shape(dims, dtype=BF16):
        return jax.ShapeDtypeStruct(dims, dtype)

    def split(s):
        return s // (cn * xn), s // cn % xn, s % cn

    def join(a, b, d):
        return (a * xn + b) * cn + d

    def over_z(a, j):
        pairs = [(s, join(split(s)[0] ^ j, *split(s)[1:])) for s in range(n_seq)]
        return lax.ppermute(a, "seq", pairs)

    def over_x(a, k):
        pairs = []
        for s in range(n_seq):
            sz, sx, sc = split(s)
            pairs.append((s, join(sz, (sx + k) % xn, sc)))
        return lax.ppermute(a, "seq", pairs)

    def over_c(a, m):
        return lax.ppermute(a, "seq", [(s, s ^ m) for s in range(n_seq)])

    def over_y(a, k):
        return lax.ppermute(a, "head", [(h, (h + k) % n_head) for h in range(n_head)])

    chain = []

    def mark(a):
        chain[:] = [a]
        return a

    def done(a):
        return mark(lax.optimization_barrier((a, *chain))[0])

    def done_all(*lists):
        flat = [part for parts in lists for part in parts]
        if flat:
            flat = lax.optimization_barrier((*flat, *chain))[: len(flat)]
            mark(flat[-1])
        flat = iter(flat)
        return [[next(flat) for _ in parts] for parts in lists]

    def after(a, b):
        return lax.optimization_barrier((a, b))[0]

    last = zn - 1
    tok, packs, pieces, rows = {0: tokens}, {}, {}, {}
    started, columns, out_z = {}, {}, {0: w_out}

    def begin_tok(j):
        low = j & -j
        if j < zn and j not in started and j ^ low in tok:
            started[j] = over_z(tok[j ^ low], low)

    def begin_y(j):
        started["y", j] = [over_y(tok[j], k) for k in range(1, n_head)]

    def end_y(j, others):
        (rows[j],) = call(
            functools.partial(norm_kernel, n_head),
            (at, gain[None], tok[j], *others),
            [shape((seg_rows, width))],
        )
        mark(rows[j])

    def both(a):
        return [over_c(a, m) if m else a for m in range(cn)]

    def begin_x(j):
        started["x", j] = [over_x(packs[j], k) for k in range(1, xn)]
        pieces[j] = both(packs[j])

    def end_x(j, others):
        for part in others:
            pieces[j] += both(part)

    def begin_out(j, source):
        started["o", j] = [over_x(source, k) for k in range(1, xn)]
        columns[j] = [source]

    def end_out(j):
        columns[j] += [done(part) for part in started["o", j]]

    for bit in range(zn.bit_length() - 2, -1, -1):
        begin_tok(1 << bit)
    begin_y(0)
    begin_out(0, w_out)
    sent = call(
        functools.partial(cut_kernel, cn),
        (at, decay[0], seg_len, w_query, w_key, w_value),
        [shape((w_rows + META, cn * 3 * DH))] * zn,
        scalars=3,
    )
    packs[0] = sent[0]
    begin_x(0)
    if last:
        started["w", 1] = over_z(sent[1], 1)

    bits = [1 << n for n in range(zn.bit_length() - 1)]
    more = [j for j in range(1, zn) if j not in bits]
    parts, first, whole = done_all([started[b] for b in bits], started["y", 0], started["x", 0])
    tok.update(zip(bits, parts))
    end_x(0, whole)
    for b in bits:
        begin_y(b)
    for j in more:
        begin_tok(j)
    early = range(1, min(3, zn))
    for j in early[1:]:
        started["w", j] = over_z(after(sent[j], tok[1]), j)
    end_y(0, first)
    parts, far, columns[0][1:], *near = done_all(
        [started["w", j] for j in early],
        [started[j] for j in more],
        started["o", 0],
        *(started["y", b] for b in bits),
    )
    packs.update(zip(early, parts))
    tok.update(zip(more, far))
    for j in range(len(early) + 1, zn):
        started["w", j] = over_z(after(sent[j], packs[j - 1]), j)
    for j in more:
        begin_y(j)
    if last:
        begin_x(1)
        started["oz", 1] = over_z(after(w_out, packs[early[-1]]), 1)
    for b, others in zip(bits, near):
        end_y(b, others)
    for j in early[1:]:
        packs[j] = lax.optimization_barrier((packs[j], *(rows[b] for b in bits)))[0]
        begin_x(j)
    for j in range(len(early) + 1, zn):
        packs[j] = done(started["w", j])
        begin_x(j)
    for b in bits[1:]:
        started["oz", b] = over_z(after(w_out, packs[last]), b)
    for j in more:
        end_y(j, done_all(started["y", j])[0])
    if last:
        out_z[1] = done(started["oz", 1])
        begin_out(1, out_z[1])
    for j in range(1, last):
        end_x(j, done_all(started["x", j])[0])
    rows = [rows[j] for j in range(zn)]

    chunk_rows = xn * cn * w_rows
    flops = 2 * zn * seg_rows * chunk_rows * cn * 3 * DH
    before = []
    if last:
        before = call(
            functools.partial(project_kernel, zn, xn, cn, range(last)),
            (at, *rows, *sum((pieces[j] for j in range(last)), [])),
            [
                shape((zn, seg_rows, cn * 3 * DH), F32),
                shape((last, xn, cn, META, DH), F32),
            ],
            [pltpu.VMEM((last, chunk_rows, cn * 3 * DH), BF16)],
            flops * last,
            room=30,
        )
        mark(before[0])
    if last:
        end_x(last, done_all(started["x", last])[0])
        parts, columns[1][1:], held = done_all(
            [started["oz", b] for b in bits[1:]], started["o", 1], before[:1]
        )
        before = [*held, *before[1:]]
        out_z.update(zip(bits[1:], parts))
        for b in bits[1:]:
            begin_out(b, out_z[b])
        for j in more:
            started["oz", j] = over_z(out_z[j ^ (j & -j)], j & -j)
    halves = 2 if zn % 2 == 0 else 1
    *parts, meta = call(
        functools.partial(finish_kernel, zn, xn, cn),
        (at, *rows, *pieces[last], *before[:1]),
        [shape((zn // halves, seg_rows, 3 * DH))] * (cn * halves)
        + [shape((1, xn, cn, META, DH), F32)],
        [pltpu.VMEM((chunk_rows, cn * 3 * DH), BF16)],
        flops,
        column=(chunk_rows, lambda at: at[0] ^ last),
        room=20,
    )
    parts = [over_c(part, n % cn) if n % cn else part for n, part in enumerate(parts)]
    (parts,) = done_all(parts)
    sums, written, group, group16, table = call(
        functools.partial(write_kernel, zn, xn, cn, halves),
        (at, *parts, mem_query, *before[1:], meta),
        [
            shape((zn, cn, seg_rows, 3 * DH)),
            shape((zn, cn, slots, 2 * DH), F32),
            shape((zn, slots, 2 * DH), F32),
            shape((zn, slots, 2 * DH)),
            shape((zn, xn, cn, META, DH), F32),
        ],
    )
    others = [over_x(group16, k) for k in range(1, xn)]
    (token,) = call(
        functools.partial(token_kernel, zn, cn, slots),
        (at, score_scale, table, sums),
        [shape((zn, cn, seg_rows, DH), F32)],
        scalars=2,
    )
    mark(token)
    others, parts, *shares = done_all(
        others, [started["oz", j] for j in more], *(started["o", b] for b in bits[1:])
    )
    for b, share in zip(bits[1:], shares):
        columns[b] += share
    for j, part in zip(more, parts):
        begin_out(j, part)
    attended = call(
        functools.partial(memory_kernel, zn, xn, cn),
        (at, score_scale, table, sums, token, written, group, *others),
        [shape((cn, seg_rows, DH))] * zn,
        [
            pltpu.VMEM((xn, zn, slots, 2 * DH), F32),
            pltpu.VMEM((zn, cn, seg_rows, DH), BF16),
        ],
        scalars=2,
    )

    here = [over_z(block, j) if j else block for j, block in enumerate(attended)]
    for j in range(1, zn):
        here[j] = done(here[j])
    swapped = [[over_c(here[j], m) for m in range(1, cn)] for j in range(zn)]
    here = sum(([here[j]] + [done(a) for a in swapped[j]] for j in range(zn)), [])

    for j in more:
        end_out(j)
    out_cols = w_out.shape[1]
    phases = zn // n_head if zn % n_head == 0 else 1
    blocks = feat_local // (cn * out_cols * phases)
    def multiply(few, turns, outs):
        return call(
            functools.partial(out_kernel, zn, xn, cn, n_head, few, turns, phases),
            (at, *here, *sum((columns[j] for j in few), [])),
            [shape((blocks, seg_rows, out_cols))] * outs,
            [pltpu.VMEM((cn * seg_rows, heads * DH), BF16)],
            2 * cn * seg_rows * heads * DH * len(few) * xn * out_cols,
            room=20,
        )

    mine = []
    others = range(1, n_head)
    for p in range(phases):
        products = multiply(range(p, zn, phases), others, cn * len(others))
        for n, block in enumerate(products):
            block = over_c(block, n % cn) if n % cn else block
            mine.append(over_y(block, others[n // cn]))
    products = multiply(range(zn), (0,), cn * phases)
    for n, block in enumerate(products):
        mine.append(over_c(block, n % cn) if n % cn else block)
    (branch,) = call(
        functools.partial(sum_kernel, n_head, cn, phases),
        (at, *mine),
        [shape((seg_rows, feat_local))],
    )
    return branch


def solution(mesh):
    return jax.shard_map(
        body,
        mesh=mesh,
        in_specs=(
            P("seq", "head"),
            P(),
            P("seq", "head"),
            P("seq", "head"),
            P("seq", "head"),
            P("head", "seq"),
            P(None, "head"),
            P("head"),
            P("seq", "head"),
            P("seq"),
        ),
        out_specs=P("seq", "head"),
        check_vma=False,
    )
```

```python
import functools
import math

import jax
import jax.numpy as jnp
from jax import lax
from jax.experimental import pallas as pl
from jax.experimental.pallas import tpu as pltpu
from jax.sharding import PartitionSpec as P

DH = 128
META = 16
F32 = jnp.float32
BF16 = jnp.bfloat16


def dot(a, b, contract=(1, 0)):
    dims = (((contract[0],), (contract[1],)), ((), ()))
    return lax.dot_general(a, b, dims, preferred_element_type=F32)


def call(kernel, ins, outs, scratch=(), flops=0, scalars=1, column=None, room=12):
    moved = sum(math.prod(a.shape) * a.dtype.itemsize for a in (*ins, *outs))

    def whole(a):
        return pl.BlockSpec(a.shape, lambda i, *_: (0,) * len(a.shape))

    def spec(a):
        if column and a.shape[-1] > column[0] and a.ndim == 2 and a.dtype == BF16:
            pick = column[1]
            return pl.BlockSpec((a.shape[0], column[0]), lambda i, at, *_: (0, pick(at)))
        return whole(a)

    return pl.pallas_call(
        kernel,
        grid_spec=pltpu.PrefetchScalarGridSpec(
            num_scalar_prefetch=scalars,
            grid=(1,),
            in_specs=[spec(a) for a in ins[scalars:]],
            out_specs=[whole(a) for a in outs],
            scratch_shapes=scratch,
        ),
        out_shape=outs,
        compiler_params=pltpu.CompilerParams(vmem_limit_bytes=room * 2**20),
        cost_estimate=pl.CostEstimate(flops=flops, bytes_accessed=moved, transcendentals=0),
    )(*ins)


def lanes(index, size):
    return pl.ds(pl.multiple_of(index * size, size), size)


def cut_kernel(cn, at, decay, seg_len, *refs):
    weights, outs = refs[:3], refs[3:]
    w_rows = weights[0].shape[0]
    row = lax.broadcasted_iota(jnp.int32, (META, DH), 0)
    length = jnp.full((META, DH), seg_len[0], jnp.int32).astype(F32)
    for j, out in enumerate(outs):
        for e in range(cn):
            head = (at[0] ^ j) * cn + e
            rest = jnp.full((META, DH), decay[head], F32)
            for i, w in enumerate(weights):
                first = (e * 3 + i) * DH
                out[:w_rows, first : first + DH] = w[:, lanes(head, DH)]
                term = rest.astype(BF16).astype(F32)
                rest = rest - term
                out[w_rows:, first : first + DH] = jnp.where(row < META // 2, term, length).astype(BF16)


def norm_kernel(n_head, at, gain, *refs):
    parts, out = refs[:n_head], refs[n_head]
    feat = parts[0].shape[1]
    wide = [part[...].astype(F32) for part in parts]
    squares = sum(jnp.sum(w * w, axis=1, keepdims=True) for w in wide)
    inverse = lax.rsqrt(squares / (feat * n_head) + 1e-05)
    for k, w in enumerate(wide):
        half = lanes(lax.rem(at[3] + n_head - k, n_head), feat)
        out[:, half] = (w * inverse * gain[:, half]).astype(BF16)


def project(xn, cn, at, rows, weights, chunk, meta, each):
    x, c = at[1], at[2]
    w_rows = weights[0].shape[0] - META
    row = lax.broadcasted_iota(jnp.int32, (META, DH), 0)
    for n, w in enumerate(weights):
        xi, ci = lax.rem(x + xn - n // cn, xn), c ^ (n % cn)
        chunk[pl.ds(pl.multiple_of((xi * cn + ci) * w_rows, w_rows), w_rows), :] = w[:w_rows]
        tail = w[w_rows:].astype(F32)
        terms = tail[:, : 3 * DH]
        for e in range(1, cn):
            terms = jnp.where(c == e, tail[:, e * 3 * DH : (e + 1) * 3 * DH], terms)
        total = terms[:, :DH] + terms[:, DH : 2 * DH] + terms[:, 2 * DH :]
        meta[xi, ci] = jnp.where(row < META // 2, total, terms[:, :DH])
    for first in range(0, len(rows), 2):
        pair = range(first, min(first + 2, len(rows)))
        sums = dot(jnp.concatenate([rows[i][...] for i in pair]), chunk[...])
        for n, i in enumerate(pair):
            size = sums.shape[0] // len(pair)
            each(i, sums[n * size : (n + 1) * size])


def project_kernel(zn, xn, cn, steps, at, *refs):
    rows = refs[:zn]
    weights = refs[zn : zn + len(steps) * xn * cn]
    out, meta, chunk = refs[-3:]
    size = chunk.shape[1]
    for n, j in enumerate(steps):

        def each(i, sums):
            out[i] = sums if n == 0 else out[i] + sums

        part = [row.at[:, lanes(at[0] ^ j, size)] for row in rows]
        few = weights[n * xn * cn : (n + 1) * xn * cn]
        project(xn, cn, at, part, few, chunk.at[n], meta.at[n], each)


def finish_kernel(zn, xn, cn, at, *refs):
    rows = refs[:zn]
    weights = refs[zn : zn + xn * cn]
    before = refs[zn + xn * cn] if zn > 1 else None
    meta, chunk = refs[-2:]
    outs = refs[zn + xn * cn + (before is not None) : -2]
    c = at[2]

    def each(i, sums):
        sums = (sums if before is None else sums + before[i]).astype(BF16)
        heads = [sums[:, e * 3 * DH : (e + 1) * 3 * DH] for e in range(cn)]
        half = outs[0].shape[0]
        for m in range(cn):
            pick = heads[m]
            for e in range(cn):
                if e != m:
                    pick = jnp.where((c ^ m) == e, heads[e], pick)
            outs[i // half * cn + m][i % half] = pick

    project(xn, cn, at, rows, weights, chunk, meta.at[0], each)


def segment_info(table):
    def retain(zi, xi, ci):
        return table[zi, xi, ci, 0:1, 0:1]

    def length(zi, xi, ci):
        return table[zi, xi, ci, META // 2 : META // 2 + 1, 0:1]

    return retain, length


def write_kernel(zn, xn, cn, halves, at, *refs):
    count = cn * halves
    parts, query, metas = refs[:count], refs[count], refs[count + 1 : -5]
    sums, written, group, group16, table = refs[-5:]
    z, x, c = at[0], at[1], at[2]
    j = 0
    for meta in metas:
        for n in range(meta.shape[0]):
            table[z ^ j] = meta[n]
            j += 1
    retain, length = segment_info(table)
    seg_rows = sums.shape[2]
    half = zn // halves
    for i in range(zn):
        for m in range(cn):
            sums[z ^ i, c ^ m] = parts[i // half * cn + m][i % half]
    own = query[:, lanes(z * cn + c, DH)]
    slots = own.shape[0]
    position = lax.broadcasted_iota(jnp.int32, (slots, seg_rows), 1).astype(F32)
    for i in range(zn):
        keys = sums[i, :, :, DH : 2 * DH].reshape(cn * seg_rows, DH)
        scores = dot(own, keys, (1, 1)) * (1.0 / math.sqrt(DH))
        gates = jax.nn.sigmoid(scores - math.log(seg_rows))
        total = None
        for m in range(cn):
            gate = gates[:, m * seg_rows : (m + 1) * seg_rows]
            gate = jnp.where(position < length(i, x, m), gate, 0.0).astype(BF16)
            new = dot(gate, sums[i, m, :, DH:])
            written[i, m] = new
            total = new if total is None else retain(i, x, m) * total + new
        group[i] = total
        group16[i] = total.astype(BF16)


def token_kernel(zn, cn, slots, at, scale, table, sums, out):
    _, length = segment_info(table)
    seg_rows = sums.shape[2]
    shape = (seg_rows, seg_rows)
    row = lax.broadcasted_iota(jnp.int32, shape, 0)
    column = lax.broadcasted_iota(jnp.int32, shape, 1)
    factor = scale[at[0] * cn + at[2]] * (1.0 / math.sqrt(DH))
    for i in range(zn):
        for m in range(cn):
            query, keys, values = (sums[i, m, :, n * DH : (n + 1) * DH] for n in range(3))
            scores = dot(query, keys, (1, 1)) * factor
            gate = jax.nn.sigmoid(scores - math.log(slots + seg_rows))
            allowed = (column <= row) & (column.astype(F32) < length(i, at[1], m))
            out[i, m] = dot(jnp.where(allowed, gate, 0.0).astype(BF16), values)


def memory_kernel(zn, xn, cn, at, scale, table, sums, token, written, group, *refs):
    others = refs[: xn - 1]
    outs = refs[xn - 1 : xn - 1 + zn]
    groups, done = refs[-2:]
    z, x, c = at[0], at[1], at[2]
    retain, length = segment_info(table)
    slots, seg_rows = group.shape[1], sums.shape[2]
    factor = scale[z * cn + c] * (1.0 / math.sqrt(DH))
    bias = math.log(slots + seg_rows)
    row = lax.broadcasted_iota(jnp.int32, (seg_rows, DH), 0).astype(F32)
    groups[x] = group[...]
    for k, other in enumerate(others, 1):
        groups[lax.rem(x + xn - k, xn)] = other[...].astype(F32)
    memory = jnp.zeros(group.shape[1:], F32)
    for i in range(zn):
        entry = memory
        for k in range(xn):
            if k:
                entry = jnp.where(x == k, memory, entry)
            kept = retain(i, k, 0)
            for m in range(1, cn):
                kept = kept * retain(i, k, m)
            memory = kept * memory + groups[k, i]
        for m in range(cn):
            units = []
            for n in range(2):
                part = entry[:, n * DH : (n + 1) * DH]
                mean = jnp.mean(part * part, axis=1, keepdims=True)
                units.append((part * lax.rsqrt(mean + 1e-06)).astype(BF16))
            scores = dot(sums[i, m, :, :DH], units[0], (1, 1)) * factor
            gate = jax.nn.sigmoid(scores - bias).astype(BF16)
            total = dot(gate, units[1]) + token[i, m]
            done[i, m] = jnp.where(row < length(i, x, m), total, 0.0).astype(BF16)
            if m + 1 < cn:
                entry = retain(i, x, m) * entry + written[i, m]
    for j in range(zn):
        for m in range(cn):
            outs[j][m] = done[z ^ j, c ^ m]


def out_kernel(zn, xn, cn, n_head, slots, turns, phases, forms, at, *refs):
    attended = refs[: zn * cn]
    rest = iter(refs[zn * cn : -1])
    weights = [[next(rest) for _ in range(form)] for form in forms]
    outs, rows = list(rest), refs[-1]
    z, x, c, y = at[0], at[1], at[2], at[3]
    seg_rows = attended[0].shape[1]
    for j in range(zn):
        for e in range(cn):
            for m in range(cn):
                rows[m * seg_rows : (m + 1) * seg_rows, lanes((z ^ j) * cn + (c ^ e), DH)] = (
                    attended[j * cn + e][m ^ e]
                )
    blocks = outs[0].shape[0]
    share = zn * xn // n_head
    for n, j in enumerate(slots):
        for k in range(xn):
            spot = (z ^ j) * xn + lax.rem(x + xn - k, xn)
            turn = lax.rem(spot // share + n_head - y, n_head)
            for i, r in enumerate(turns):
                for e, weight in enumerate(weights[n * xn + k]):
                    here = turn == r
                    if len(weights[n * xn + k]) > 1:
                        here = here & (c == e)

                    @pl.when(here)
                    def _():
                        product = dot(rows[...], weight[...]).astype(BF16)
                        group = j % phases * len(turns) if len(slots) == zn else 0
                        for m in range(cn):
                            out = outs[(group + i) * cn + m]
                            out[lax.rem(spot, blocks)] = product[m * seg_rows : (m + 1) * seg_rows]


def sum_kernel(n_head, cn, phases, at, *refs):
    out = refs[-1]
    blocks, seg_rows, size = refs[0].shape
    for p in range(phases):
        count = (n_head - 1) * cn
        few = refs[(phases * (n_head - 1) + p) * cn :][:cn] + refs[p * count : (p + 1) * count]
        places = []
        for b in range(blocks):
            totals = [
                sum(few[r * cn + e][b].astype(F32) for r in range(n_head)).astype(BF16)
                for e in range(cn)
            ]
            for m in range(cn):
                total = totals[0]
                for e in range(1, cn):
                    total = jnp.where((at[2] ^ e) == m, totals[e], total)
                places.append(total)
        out[:, lanes(lax.rem(at[0] ^ p, phases), blocks * cn * size)] = jnp.concatenate(places, 1)


def body(tokens, gain, w_query, w_key, w_value, w_out, mem_query, score_scale, decay, seg_len):
    n_seq = lax.axis_size("seq")
    n_head = lax.axis_size("head")
    seg_rows, feat_local = tokens.shape
    width = gain.shape[0]
    w_rows, col_local = w_query.shape
    heads = col_local // DH
    slots = mem_query.shape[0]
    cn = 2 if heads % 2 == 0 else 1
    zn = heads // cn
    xn = n_seq // heads
    place = lax.axis_index("seq")
    y = lax.axis_index("head")
    at = jnp.stack([place // (cn * xn), place // cn % xn, place % cn, y]).astype(jnp.int32)

    def shape(dims, dtype=BF16):
        return jax.ShapeDtypeStruct(dims, dtype)

    def split(s):
        return s // (cn * xn), s // cn % xn, s % cn

    def join(a, b, d):
        return (a * xn + b) * cn + d

    def over_z(a, j):
        pairs = [(s, join(split(s)[0] ^ j, *split(s)[1:])) for s in range(n_seq)]
        return lax.ppermute(a, "seq", pairs)

    def over_x(a, k, cores=None):
        pairs = []
        for s in range(n_seq):
            sz, sx, sc = split(s)
            if cores is None or sc in cores:
                pairs.append((s, join(sz, (sx + k) % xn, sc)))
        return lax.ppermute(a, "seq", pairs)

    def over_c(a, m):
        return lax.ppermute(a, "seq", [(s, s ^ m) for s in range(n_seq)])

    def over_y(a, k):
        return lax.ppermute(a, "head", [(h, (h + k) % n_head) for h in range(n_head)])

    chain = []

    def mark(a):
        chain[:] = [a]
        return a

    def done(a):
        return mark(lax.optimization_barrier((a, *chain))[0])

    def done_all(*lists):
        flat = [part for parts in lists for part in parts]
        if flat:
            flat = lax.optimization_barrier((*flat, *chain))[: len(flat)]
            mark(flat[-1])
        flat = iter(flat)
        return [[next(flat) for _ in parts] for parts in lists]

    def after(a, b):
        return lax.optimization_barrier((a, b))[0]

    last = zn - 1
    tok, packs, pieces, rows = {0: tokens}, {}, {}, {}
    started, columns, out_z = {}, {}, {0: w_out}

    def begin_tok(j):
        low = j & -j
        if j < zn and j not in started and j ^ low in tok:
            started[j] = over_z(tok[j ^ low], low)

    def begin_y(j):
        started["y", j] = [over_y(tok[j], k) for k in range(1, n_head)]

    def end_y(j, others):
        (rows[j],) = call(
            functools.partial(norm_kernel, n_head),
            (at, gain[None], tok[j], *others),
            [shape((seg_rows, width))],
        )
        mark(rows[j])

    def both(a):
        return [over_c(a, m) if m else a for m in range(cn)]

    def begin_x(j):
        started["x", j] = [over_x(packs[j], k) for k in range(1, xn)]
        pieces[j] = both(packs[j])

    def end_x(j, others):
        for part in others:
            pieces[j] += both(part)

    def begin_out(j, source):
        started["o", j] = [over_x(source, k) for k in range(1, xn)]
        columns[j] = [source]

    def end_out(j):
        columns[j] += [done(part) for part in started["o", j]]

    for bit in range(zn.bit_length() - 2, -1, -1):
        begin_tok(1 << bit)
    begin_y(0)
    begin_out(0, w_out)
    sent = call(
        functools.partial(cut_kernel, cn),
        (at, decay[0], seg_len, w_query, w_key, w_value),
        [shape((w_rows + META, cn * 3 * DH))] * zn,
        scalars=3,
    )
    packs[0] = sent[0]
    begin_x(0)
    if last:
        started["w", 1] = over_z(sent[1], 1)

    bits = [1 << n for n in range(zn.bit_length() - 1)]
    more = [j for j in range(1, zn) if j not in bits]
    parts, first, whole = done_all([started[b] for b in bits], started["y", 0], started["x", 0])
    tok.update(zip(bits, parts))
    end_x(0, whole)
    for b in bits:
        begin_y(b)
    for j in more:
        begin_tok(j)
    early = range(1, min(3, zn))
    for j in early[1:]:
        started["w", j] = over_z(after(sent[j], tok[1]), j)
    end_y(0, first)
    parts, far, columns[0][1:], *near = done_all(
        [started["w", j] for j in early],
        [started[j] for j in more],
        started["o", 0],
        *(started["y", b] for b in bits),
    )
    packs.update(zip(early, parts))
    tok.update(zip(more, far))
    for j in range(len(early) + 1, zn):
        started["w", j] = over_z(after(sent[j], packs[j - 1]), j)
    for j in more:
        begin_y(j)
    if last:
        begin_x(1)
        started["oz", 1] = over_z(after(w_out, packs[early[-1]]), 1)
    for b, others in zip(bits, near):
        end_y(b, others)
    for j in early[1:]:
        packs[j] = lax.optimization_barrier((packs[j], *(rows[b] for b in bits)))[0]
        begin_x(j)
    for j in range(len(early) + 1, zn):
        packs[j] = done(started["w", j])
        begin_x(j)
    for b in bits[1:]:
        started["oz", b] = over_z(after(w_out, packs[last]), b)
    for j in more:
        end_y(j, done_all(started["y", j])[0])
    if last:
        out_z[1] = done(started["oz", 1])
        begin_out(1, out_z[1])
    for j in range(1, last):
        end_x(j, done_all(started["x", j])[0])
    rows = [rows[j] for j in range(zn)]

    chunk_rows = xn * cn * w_rows
    flops = 2 * zn * seg_rows * chunk_rows * cn * 3 * DH
    before = []
    if last:
        before = call(
            functools.partial(project_kernel, zn, xn, cn, range(last)),
            (at, *rows, *sum((pieces[j] for j in range(last)), [])),
            [
                shape((zn, seg_rows, cn * 3 * DH), F32),
                shape((last, xn, cn, META, DH), F32),
            ],
            [pltpu.VMEM((last, chunk_rows, cn * 3 * DH), BF16)],
            flops * last,
            room=30,
        )
        mark(before[0])
    if last:
        end_x(last, done_all(started["x", last])[0])
        parts, columns[1][1:], held = done_all(
            [started["oz", b] for b in bits[1:]], started["o", 1], before[:1]
        )
        before = [*held, *before[1:]]
        out_z.update(zip(bits[1:], parts))
        for b in bits[1:]:
            columns[b] = [out_z[b]]
            started["o", b] = [
                over_x(out_z[b], k, (e,)) for e in range(cn) for k in range(1, xn)
            ]
        for j in more:
            started["oz", j] = over_z(out_z[j ^ (j & -j)], j & -j)
    halves = 2 if zn % 2 == 0 else 1
    *parts, meta = call(
        functools.partial(finish_kernel, zn, xn, cn),
        (at, *rows, *pieces[last], *before[:1]),
        [shape((zn // halves, seg_rows, 3 * DH))] * (cn * halves)
        + [shape((1, xn, cn, META, DH), F32)],
        [pltpu.VMEM((chunk_rows, cn * 3 * DH), BF16)],
        flops,
        column=(chunk_rows, lambda at: at[0] ^ last),
        room=20,
    )
    parts = [over_c(part, n % cn) if n % cn else part for n, part in enumerate(parts)]
    (parts,) = done_all(parts)
    sums, written, group, group16, table = call(
        functools.partial(write_kernel, zn, xn, cn, halves),
        (at, *parts, mem_query, *before[1:], meta),
        [
            shape((zn, cn, seg_rows, 3 * DH)),
            shape((zn, cn, slots, 2 * DH), F32),
            shape((zn, slots, 2 * DH), F32),
            shape((zn, slots, 2 * DH)),
            shape((zn, xn, cn, META, DH), F32),
        ],
    )
    others = [over_x(group16, k) for k in range(1, xn)]
    (token,) = call(
        functools.partial(token_kernel, zn, cn, slots),
        (at, score_scale, table, sums),
        [shape((zn, cn, seg_rows, DH), F32)],
        scalars=2,
    )
    mark(token)
    count = xn - 1
    others, parts, *early_x = done_all(
        others, [started["oz", j] for j in more], *(started["o", b][:count] for b in bits[1:])
    )
    for j, part in zip(more, parts):
        begin_out(j, part)
    attended = call(
        functools.partial(memory_kernel, zn, xn, cn),
        (at, score_scale, table, sums, token, written, group, *others),
        [shape((cn, seg_rows, DH))] * zn,
        [
            pltpu.VMEM((xn, zn, slots, 2 * DH), F32),
            pltpu.VMEM((zn, cn, seg_rows, DH), BF16),
        ],
        scalars=2,
    )

    here = [over_z(block, j) if j else block for j, block in enumerate(attended)]
    for j in reversed(range(1, zn)):
        here[j] = done(here[j])
    for b, ready in zip(bits[1:], early_x):
        ready = ready + done_all(started["o", b][count:])[0]
        columns[b] += [ready[k::count] for k in range(count)]
    swapped = [[over_c(here[j], m) for m in range(1, cn)] for j in range(zn)]
    here = sum(([here[j]] + [done(a) for a in swapped[j]] for j in range(zn)), [])

    for j in more:
        end_out(j)
    out_cols = w_out.shape[1]
    phases = zn // n_head if zn % n_head == 0 else 1
    blocks = feat_local // (cn * out_cols * phases)
    def multiply(few, turns, outs):
        arrays = sum((columns[j] for j in few), [])
        arrays = [a if isinstance(a, list) else [a] for a in arrays]
        forms = tuple(len(a) for a in arrays)
        return call(
            functools.partial(out_kernel, zn, xn, cn, n_head, few, turns, phases, forms),
            (at, *here, *sum(arrays, [])),
            [shape((blocks, seg_rows, out_cols))] * outs,
            [pltpu.VMEM((cn * seg_rows, heads * DH), BF16)],
            2 * cn * seg_rows * heads * DH * len(few) * xn * out_cols,
            room=20,
        )

    mine = []
    others = range(1, n_head)
    for p in range(phases):
        products = multiply(range(p, zn, phases), others, cn * len(others))
        for n, block in enumerate(products):
            block = over_c(block, n % cn) if n % cn else block
            mine.append(over_y(block, others[n // cn]))
    products = multiply(range(zn), (0,), cn * phases)
    for n, block in enumerate(products):
        mine.append(over_c(block, n % cn) if n % cn else block)
    (branch,) = call(
        functools.partial(sum_kernel, n_head, cn, phases),
        (at, *mine),
        [shape((seg_rows, feat_local))],
    )
    return branch


def solution(mesh):
    return jax.shard_map(
        body,
        mesh=mesh,
        in_specs=(
            P("seq", "head"),
            P(),
            P("seq", "head"),
            P("seq", "head"),
            P("seq", "head"),
            P("head", "seq"),
            P(None, "head"),
            P("head"),
            P("seq", "head"),
            P("seq"),
        ),
        out_specs=P("seq", "head"),
        check_vma=False,
    )
```

```python
import functools
import math

import jax
import jax.numpy as jnp
from jax import lax
from jax.experimental import pallas as pl
from jax.experimental.pallas import tpu as pltpu
from jax.sharding import PartitionSpec as P

DH = 128
META = 16
F32 = jnp.float32
BF16 = jnp.bfloat16


def dot(a, b, contract=(1, 0)):
    dims = (((contract[0],), (contract[1],)), ((), ()))
    return lax.dot_general(a, b, dims, preferred_element_type=F32)


def call(kernel, ins, outs, scratch=(), flops=0, scalars=1, column=None, room=12):
    moved = sum(math.prod(a.shape) * a.dtype.itemsize for a in (*ins, *outs))

    def whole(a):
        return pl.BlockSpec(a.shape, lambda i, *_: (0,) * len(a.shape))

    def spec(a):
        if column and a.shape[-1] > column[0] and a.ndim == 2 and a.dtype == BF16:
            pick = column[1]
            return pl.BlockSpec((a.shape[0], column[0]), lambda i, at, *_: (0, pick(at)))
        return whole(a)

    return pl.pallas_call(
        kernel,
        grid_spec=pltpu.PrefetchScalarGridSpec(
            num_scalar_prefetch=scalars,
            grid=(1,),
            in_specs=[spec(a) for a in ins[scalars:]],
            out_specs=[whole(a) for a in outs],
            scratch_shapes=scratch,
        ),
        out_shape=outs,
        compiler_params=pltpu.CompilerParams(vmem_limit_bytes=room * 2**20),
        cost_estimate=pl.CostEstimate(flops=flops, bytes_accessed=moved, transcendentals=0),
    )(*ins)


def lanes(index, size):
    return pl.ds(pl.multiple_of(index * size, size), size)


def cut_kernel(cn, at, decay, seg_len, *refs):
    weights, outs = refs[:3], refs[3:]
    w_rows = weights[0].shape[0]
    row = lax.broadcasted_iota(jnp.int32, (META, DH), 0)
    length = jnp.full((META, DH), seg_len[0], jnp.int32).astype(F32)
    for j, out in enumerate(outs):
        for e in range(cn):
            head = (at[0] ^ j) * cn + e
            rest = jnp.full((META, DH), decay[head], F32)
            for i, w in enumerate(weights):
                first = (e * 3 + i) * DH
                out[:w_rows, first : first + DH] = w[:, lanes(head, DH)]
                term = rest.astype(BF16).astype(F32)
                rest = rest - term
                out[w_rows:, first : first + DH] = jnp.where(row < META // 2, term, length).astype(BF16)


def norm_kernel(n_head, at, gain, *refs):
    parts, out = refs[:n_head], refs[n_head]
    feat = parts[0].shape[1]
    wide = [part[...].astype(F32) for part in parts]
    squares = sum(jnp.sum(w * w, axis=1, keepdims=True) for w in wide)
    inverse = lax.rsqrt(squares / (feat * n_head) + 1e-05)
    for k, w in enumerate(wide):
        half = lanes(lax.rem(at[3] + n_head - k, n_head), feat)
        out[:, half] = (w * inverse * gain[:, half]).astype(BF16)


def project(xn, cn, at, rows, weights, chunk, meta, each):
    x, c = at[1], at[2]
    w_rows = weights[0].shape[0] - META
    row = lax.broadcasted_iota(jnp.int32, (META, DH), 0)
    for n, w in enumerate(weights):
        xi, ci = lax.rem(x + xn - n // cn, xn), c ^ (n % cn)
        chunk[pl.ds(pl.multiple_of((xi * cn + ci) * w_rows, w_rows), w_rows), :] = w[:w_rows]
        tail = w[w_rows:].astype(F32)
        terms = tail[:, : 3 * DH]
        for e in range(1, cn):
            terms = jnp.where(c == e, tail[:, e * 3 * DH : (e + 1) * 3 * DH], terms)
        total = terms[:, :DH] + terms[:, DH : 2 * DH] + terms[:, 2 * DH :]
        meta[xi, ci] = jnp.where(row < META // 2, total, terms[:, :DH])
    for first in range(0, len(rows), 2):
        pair = range(first, min(first + 2, len(rows)))
        sums = dot(jnp.concatenate([rows[i][...] for i in pair]), chunk[...])
        for n, i in enumerate(pair):
            size = sums.shape[0] // len(pair)
            each(i, sums[n * size : (n + 1) * size])


def project_kernel(zn, xn, cn, steps, at, *refs):
    rows = refs[:zn]
    weights = refs[zn : zn + len(steps) * xn * cn]
    out, meta, chunk = refs[-3:]
    size = chunk.shape[1]
    for n, j in enumerate(steps):

        def each(i, sums):
            out[i] = sums if n == 0 else out[i] + sums

        part = [row.at[:, lanes(at[0] ^ j, size)] for row in rows]
        few = weights[n * xn * cn : (n + 1) * xn * cn]
        project(xn, cn, at, part, few, chunk.at[n], meta.at[n], each)


def finish_kernel(zn, xn, cn, at, *refs):
    rows = refs[:zn]
    weights = refs[zn : zn + xn * cn]
    before = refs[zn + xn * cn] if zn > 1 else None
    meta, chunk = refs[-2:]
    outs = refs[zn + xn * cn + (before is not None) : -2]
    c = at[2]

    def each(i, sums):
        sums = (sums if before is None else sums + before[i]).astype(BF16)
        heads = [sums[:, e * 3 * DH : (e + 1) * 3 * DH] for e in range(cn)]
        half = outs[0].shape[0]
        for m in range(cn):
            pick = heads[m]
            for e in range(cn):
                if e != m:
                    pick = jnp.where((c ^ m) == e, heads[e], pick)
            outs[i // half * cn + m][i % half] = pick

    project(xn, cn, at, rows, weights, chunk, meta.at[0], each)


def segment_info(table):
    def retain(zi, xi, ci):
        return table[zi, xi, ci, 0:1, 0:1]

    def length(zi, xi, ci):
        return table[zi, xi, ci, META // 2 : META // 2 + 1, 0:1]

    return retain, length


def write_kernel(zn, xn, cn, halves, at, *refs):
    count = cn * halves
    parts, query, metas = refs[:count], refs[count], refs[count + 1 : -5]
    sums, written, group, group16, table = refs[-5:]
    z, x, c = at[0], at[1], at[2]
    j = 0
    for meta in metas:
        for n in range(meta.shape[0]):
            table[z ^ j] = meta[n]
            j += 1
    retain, length = segment_info(table)
    seg_rows = sums.shape[2]
    half = zn // halves
    for i in range(zn):
        for m in range(cn):
            sums[z ^ i, c ^ m] = parts[i // half * cn + m][i % half]
    own = query[:, lanes(z * cn + c, DH)]
    slots = own.shape[0]
    position = lax.broadcasted_iota(jnp.int32, (slots, seg_rows), 1).astype(F32)
    for i in range(zn):
        keys = sums[i, :, :, DH : 2 * DH].reshape(cn * seg_rows, DH)
        scores = dot(own, keys, (1, 1)) * (1.0 / math.sqrt(DH))
        gates = jax.nn.sigmoid(scores - math.log(seg_rows))
        total = None
        for m in range(cn):
            gate = gates[:, m * seg_rows : (m + 1) * seg_rows]
            gate = jnp.where(position < length(i, x, m), gate, 0.0).astype(BF16)
            new = dot(gate, sums[i, m, :, DH:])
            written[i, m] = new
            total = new if total is None else retain(i, x, m) * total + new
        group[i] = total
        group16[i] = total.astype(BF16)


def token_kernel(zn, cn, slots, at, scale, table, sums, out):
    _, length = segment_info(table)
    seg_rows = sums.shape[2]
    shape = (seg_rows, seg_rows)
    row = lax.broadcasted_iota(jnp.int32, shape, 0)
    column = lax.broadcasted_iota(jnp.int32, shape, 1)
    factor = scale[at[0] * cn + at[2]] * (1.0 / math.sqrt(DH))
    for i in range(zn):
        for m in range(cn):
            query, keys, values = (sums[i, m, :, n * DH : (n + 1) * DH] for n in range(3))
            scores = dot(query, keys, (1, 1)) * factor
            gate = jax.nn.sigmoid(scores - math.log(slots + seg_rows))
            allowed = (column <= row) & (column.astype(F32) < length(i, at[1], m))
            out[i, m] = dot(jnp.where(allowed, gate, 0.0).astype(BF16), values)


def memory_kernel(zn, xn, cn, at, scale, table, sums, token, written, group, *refs):
    others = refs[: xn - 1]
    outs = refs[xn - 1 : xn - 1 + zn]
    groups, done = refs[-2:]
    z, x, c = at[0], at[1], at[2]
    retain, length = segment_info(table)
    slots, seg_rows = group.shape[1], sums.shape[2]
    factor = scale[z * cn + c] * (1.0 / math.sqrt(DH))
    bias = math.log(slots + seg_rows)
    row = lax.broadcasted_iota(jnp.int32, (seg_rows, DH), 0).astype(F32)
    groups[x] = group[...]
    for k, other in enumerate(others, 1):
        groups[lax.rem(x + xn - k, xn)] = other[...].astype(F32)
    memory = jnp.zeros(group.shape[1:], F32)
    for i in range(zn):
        entry = memory
        for k in range(xn):
            if k:
                entry = jnp.where(x == k, memory, entry)
            kept = retain(i, k, 0)
            for m in range(1, cn):
                kept = kept * retain(i, k, m)
            memory = kept * memory + groups[k, i]
        for m in range(cn):
            units = []
            for n in range(2):
                part = entry[:, n * DH : (n + 1) * DH]
                mean = jnp.mean(part * part, axis=1, keepdims=True)
                units.append((part * lax.rsqrt(mean + 1e-06)).astype(BF16))
            scores = dot(sums[i, m, :, :DH], units[0], (1, 1)) * factor
            gate = jax.nn.sigmoid(scores - bias).astype(BF16)
            total = dot(gate, units[1]) + token[i, m]
            done[i, m] = jnp.where(row < length(i, x, m), total, 0.0).astype(BF16)
            if m + 1 < cn:
                entry = retain(i, x, m) * entry + written[i, m]
    for j in range(zn):
        for m in range(cn):
            outs[j][m] = done[z ^ j, c ^ m]


def out_kernel(zn, xn, cn, n_head, slots, turns, phases, forms, at, *refs):
    attended = refs[: zn * cn]
    rest = iter(refs[zn * cn : -1])
    weights = [[next(rest) for _ in range(form)] for form in forms]
    outs, rows = list(rest), refs[-1]
    z, x, c, y = at[0], at[1], at[2], at[3]
    seg_rows = attended[0].shape[1]
    for j in range(zn):
        for e in range(cn):
            for m in range(cn):
                rows[m * seg_rows : (m + 1) * seg_rows, lanes((z ^ j) * cn + (c ^ e), DH)] = (
                    attended[j * cn + e][m ^ e]
                )
    blocks = outs[0].shape[0]
    share = zn * xn // n_head
    for n, j in enumerate(slots):
        for k in range(xn):
            spot = (z ^ j) * xn + lax.rem(x + xn - k, xn)
            turn = lax.rem(spot // share + n_head - y, n_head)
            for i, r in enumerate(turns):
                for e, weight in enumerate(weights[n * xn + k]):
                    here = turn == r
                    if len(weights[n * xn + k]) > 1:
                        here = here & (c == e)

                    @pl.when(here)
                    def _():
                        product = dot(rows[...], weight[...]).astype(BF16)
                        group = j % phases * len(turns) if len(slots) == zn else 0
                        for m in range(cn):
                            out = outs[(group + i) * cn + m]
                            out[lax.rem(spot, blocks)] = product[m * seg_rows : (m + 1) * seg_rows]


def sum_kernel(n_head, cn, phases, at, *refs):
    out = refs[-1]
    blocks, seg_rows, size = refs[0].shape
    for p in range(phases):
        count = (n_head - 1) * cn
        few = refs[(phases * (n_head - 1) + p) * cn :][:cn] + refs[p * count : (p + 1) * count]
        places = []
        for b in range(blocks):
            totals = [
                sum(few[r * cn + e][b].astype(F32) for r in range(n_head)).astype(BF16)
                for e in range(cn)
            ]
            for m in range(cn):
                total = totals[0]
                for e in range(1, cn):
                    total = jnp.where((at[2] ^ e) == m, totals[e], total)
                places.append(total)
        out[:, lanes(lax.rem(at[0] ^ p, phases), blocks * cn * size)] = jnp.concatenate(places, 1)


def body(tokens, gain, w_query, w_key, w_value, w_out, mem_query, score_scale, decay, seg_len):
    n_seq = lax.axis_size("seq")
    n_head = lax.axis_size("head")
    seg_rows, feat_local = tokens.shape
    width = gain.shape[0]
    w_rows, col_local = w_query.shape
    heads = col_local // DH
    slots = mem_query.shape[0]
    cn = 2 if heads % 2 == 0 else 1
    zn = heads // cn
    xn = n_seq // heads
    place = lax.axis_index("seq")
    y = lax.axis_index("head")
    at = jnp.stack([place // (cn * xn), place // cn % xn, place % cn, y]).astype(jnp.int32)

    def shape(dims, dtype=BF16):
        return jax.ShapeDtypeStruct(dims, dtype)

    def split(s):
        return s // (cn * xn), s // cn % xn, s % cn

    def join(a, b, d):
        return (a * xn + b) * cn + d

    def over_z(a, j):
        pairs = [(s, join(split(s)[0] ^ j, *split(s)[1:])) for s in range(n_seq)]
        return lax.ppermute(a, "seq", pairs)

    def over_x(a, k, cores=None):
        pairs = []
        for s in range(n_seq):
            sz, sx, sc = split(s)
            if cores is None or sc in cores:
                pairs.append((s, join(sz, (sx + k) % xn, sc)))
        return lax.ppermute(a, "seq", pairs)

    def over_c(a, m):
        return lax.ppermute(a, "seq", [(s, s ^ m) for s in range(n_seq)])

    def over_y(a, k):
        return lax.ppermute(a, "head", [(h, (h + k) % n_head) for h in range(n_head)])

    chain = []

    def mark(a):
        chain[:] = [a]
        return a

    def done(a):
        return mark(lax.optimization_barrier((a, *chain))[0])

    def done_all(*lists):
        flat = [part for parts in lists for part in parts]
        if flat:
            flat = lax.optimization_barrier((*flat, *chain))[: len(flat)]
            mark(flat[-1])
        flat = iter(flat)
        return [[next(flat) for _ in parts] for parts in lists]

    def after(a, b):
        return lax.optimization_barrier((a, b))[0]

    last = zn - 1
    tok, packs, pieces, rows = {0: tokens}, {}, {}, {}
    started, columns, out_z = {}, {}, {0: w_out}

    def begin_tok(j):
        low = j & -j
        if j < zn and j not in started and j ^ low in tok:
            started[j] = over_z(tok[j ^ low], low)

    def begin_y(j):
        started["y", j] = [over_y(tok[j], k) for k in range(1, n_head)]

    def end_y(j, others):
        (rows[j],) = call(
            functools.partial(norm_kernel, n_head),
            (at, gain[None], tok[j], *others),
            [shape((seg_rows, width))],
        )
        mark(rows[j])

    def both(a):
        return [over_c(a, m) if m else a for m in range(cn)]

    def begin_x(j):
        started["x", j] = [over_x(packs[j], k) for k in range(1, xn)]
        pieces[j] = both(packs[j])

    def end_x(j, others):
        for part in others:
            pieces[j] += both(part)

    def begin_out(j, source):
        started["o", j] = [over_x(source, k) for k in range(1, xn)]
        columns[j] = [source]

    def end_out(j):
        columns[j] += [done(part) for part in started["o", j]]

    for bit in range(zn.bit_length() - 2, -1, -1):
        begin_tok(1 << bit)
    begin_y(0)
    begin_out(0, w_out)
    sent = call(
        functools.partial(cut_kernel, cn),
        (at, decay[0], seg_len, w_query, w_key, w_value),
        [shape((w_rows + META, cn * 3 * DH))] * zn,
        scalars=3,
    )
    packs[0] = sent[0]
    begin_x(0)
    if last:
        started["w", 1] = over_z(sent[1], 1)

    bits = [1 << n for n in range(zn.bit_length() - 1)]
    more = [j for j in range(1, zn) if j not in bits]
    parts, first, whole = done_all([started[b] for b in bits], started["y", 0], started["x", 0])
    tok.update(zip(bits, parts))
    end_x(0, whole)
    for b in bits:
        begin_y(b)
    for j in more:
        begin_tok(j)
    early = range(1, min(3, zn))
    for j in early[1:]:
        started["w", j] = over_z(after(sent[j], tok[1]), j)
    end_y(0, first)
    parts, far, columns[0][1:], *near = done_all(
        [started["w", j] for j in early],
        [started[j] for j in more],
        started["o", 0],
        *(started["y", b] for b in bits),
    )
    packs.update(zip(early, parts))
    tok.update(zip(more, far))
    for j in range(len(early) + 1, zn):
        started["w", j] = over_z(after(sent[j], packs[j - 1]), j)
    for j in more:
        begin_y(j)
    if last:
        begin_x(1)
        started["oz", 1] = over_z(after(w_out, packs[early[-1]]), 1)
    for b, others in zip(bits, near):
        end_y(b, others)
    for j in early[1:]:
        packs[j] = lax.optimization_barrier((packs[j], *(rows[b] for b in bits)))[0]
        begin_x(j)
    for j in range(len(early) + 1, zn):
        packs[j] = done(started["w", j])
        begin_x(j)
    for b in bits[1:]:
        started["oz", b] = over_z(after(w_out, packs[last]), b)
    for j in more:
        end_y(j, done_all(started["y", j])[0])
    if last:
        out_z[1] = done(started["oz", 1])
        begin_out(1, out_z[1])
    for j in range(1, last):
        end_x(j, done_all(started["x", j])[0])
    rows = [rows[j] for j in range(zn)]

    chunk_rows = xn * cn * w_rows
    flops = 2 * zn * seg_rows * chunk_rows * cn * 3 * DH
    before = []
    if last:
        before = call(
            functools.partial(project_kernel, zn, xn, cn, range(last)),
            (at, *rows, *sum((pieces[j] for j in range(last)), [])),
            [
                shape((zn, seg_rows, cn * 3 * DH), F32),
                shape((last, xn, cn, META, DH), F32),
            ],
            [pltpu.VMEM((last, chunk_rows, cn * 3 * DH), BF16)],
            flops * last,
            room=30,
        )
        mark(before[0])
    if last:
        end_x(last, done_all(started["x", last])[0])
        parts, columns[1][1:], held = done_all(
            [started["oz", b] for b in bits[1:]], started["o", 1], before[:1]
        )
        before = [*held, *before[1:]]
        out_z.update(zip(bits[1:], parts))
        for b in bits[1:]:
            columns[b] = [out_z[b]]
            started["o", b] = [
                over_x(out_z[b], k, (e,)) for e in reversed(range(cn)) for k in range(1, xn)
            ]
        for j in more:
            started["oz", j] = over_z(out_z[j ^ (j & -j)], j & -j)
    halves = 2 if zn % 2 == 0 else 1
    *parts, meta = call(
        functools.partial(finish_kernel, zn, xn, cn),
        (at, *rows, *pieces[last], *before[:1]),
        [shape((zn // halves, seg_rows, 3 * DH))] * (cn * halves)
        + [shape((1, xn, cn, META, DH), F32)],
        [pltpu.VMEM((chunk_rows, cn * 3 * DH), BF16)],
        flops,
        column=(chunk_rows, lambda at: at[0] ^ last),
        room=20,
    )
    parts = [over_c(part, n % cn) if n % cn else part for n, part in enumerate(parts)]
    (parts,) = done_all(parts)
    sums, written, group, group16, table = call(
        functools.partial(write_kernel, zn, xn, cn, halves),
        (at, *parts, mem_query, *before[1:], meta),
        [
            shape((zn, cn, seg_rows, 3 * DH)),
            shape((zn, cn, slots, 2 * DH), F32),
            shape((zn, slots, 2 * DH), F32),
            shape((zn, slots, 2 * DH)),
            shape((zn, xn, cn, META, DH), F32),
        ],
    )
    others = [over_x(group16, k) for k in range(1, xn)]
    (token,) = call(
        functools.partial(token_kernel, zn, cn, slots),
        (at, score_scale, table, sums),
        [shape((zn, cn, seg_rows, DH), F32)],
        scalars=2,
    )
    mark(token)
    count = xn - 1
    others, parts, *early_x = done_all(
        others, [started["oz", j] for j in more], *(started["o", b][:count] for b in bits[1:])
    )
    for j, part in zip(more, parts):
        begin_out(j, part)
    attended = call(
        functools.partial(memory_kernel, zn, xn, cn),
        (at, score_scale, table, sums, token, written, group, *others),
        [shape((cn, seg_rows, DH))] * zn,
        [
            pltpu.VMEM((xn, zn, slots, 2 * DH), F32),
            pltpu.VMEM((zn, cn, seg_rows, DH), BF16),
        ],
        scalars=2,
    )

    here = [over_z(block, j) if j else block for j, block in enumerate(attended)]
    for j in reversed(range(1, zn)):
        here[j] = done(here[j])
    for b, ready in zip(bits[1:], early_x):
        ready = ready + done_all(started["o", b][count:])[0]
        columns[b] += [ready[k::count][::-1] for k in range(count)]
    swapped = [[over_c(here[j], m) for m in range(1, cn)] for j in range(zn)]
    here = sum(([here[j]] + [done(a) for a in swapped[j]] for j in range(zn)), [])

    for j in more:
        end_out(j)
    out_cols = w_out.shape[1]
    phases = zn // n_head if zn % n_head == 0 else 1
    blocks = feat_local // (cn * out_cols * phases)
    def multiply(few, turns, outs):
        arrays = sum((columns[j] for j in few), [])
        arrays = [a if isinstance(a, list) else [a] for a in arrays]
        forms = tuple(len(a) for a in arrays)
        return call(
            functools.partial(out_kernel, zn, xn, cn, n_head, few, turns, phases, forms),
            (at, *here, *sum(arrays, [])),
            [shape((blocks, seg_rows, out_cols))] * outs,
            [pltpu.VMEM((cn * seg_rows, heads * DH), BF16)],
            2 * cn * seg_rows * heads * DH * len(few) * xn * out_cols,
            room=20,
        )

    mine = []
    others = range(1, n_head)
    for p in range(phases):
        products = multiply(range(p, zn, phases), others, cn * len(others))
        for n, block in enumerate(products):
            block = over_c(block, n % cn) if n % cn else block
            mine.append(over_y(block, others[n // cn]))
    products = multiply(range(zn), (0,), cn * phases)
    for n, block in enumerate(products):
        mine.append(over_c(block, n % cn) if n % cn else block)
    (branch,) = call(
        functools.partial(sum_kernel, n_head, cn, phases),
        (at, *mine),
        [shape((seg_rows, feat_local))],
    )
    return branch


def solution(mesh):
    return jax.shard_map(
        body,
        mesh=mesh,
        in_specs=(
            P("seq", "head"),
            P(),
            P("seq", "head"),
            P("seq", "head"),
            P("seq", "head"),
            P("head", "seq"),
            P(None, "head"),
            P("head"),
            P("seq", "head"),
            P("seq"),
        ),
        out_specs=P("seq", "head"),
        check_vma=False,
    )
```

```python
import functools
import math

import jax
import jax.numpy as jnp
from jax import lax
from jax.experimental import pallas as pl
from jax.experimental.pallas import tpu as pltpu
from jax.sharding import PartitionSpec as P

DH = 128
META = 16
F32 = jnp.float32
BF16 = jnp.bfloat16


def dot(a, b, contract=(1, 0)):
    dims = (((contract[0],), (contract[1],)), ((), ()))
    return lax.dot_general(a, b, dims, preferred_element_type=F32)


def call(kernel, ins, outs, scratch=(), flops=0, scalars=1, column=None, room=12):
    moved = sum(math.prod(a.shape) * a.dtype.itemsize for a in (*ins, *outs))

    def whole(a):
        return pl.BlockSpec(a.shape, lambda i, *_: (0,) * len(a.shape))

    def spec(a):
        if column and a.shape[-1] > column[0] and a.ndim == 2 and a.dtype == BF16:
            pick = column[1]
            return pl.BlockSpec((a.shape[0], column[0]), lambda i, at, *_: (0, pick(at)))
        return whole(a)

    return pl.pallas_call(
        kernel,
        grid_spec=pltpu.PrefetchScalarGridSpec(
            num_scalar_prefetch=scalars,
            grid=(1,),
            in_specs=[spec(a) for a in ins[scalars:]],
            out_specs=[whole(a) for a in outs],
            scratch_shapes=scratch,
        ),
        out_shape=outs,
        compiler_params=pltpu.CompilerParams(vmem_limit_bytes=room * 2**20),
        cost_estimate=pl.CostEstimate(flops=flops, bytes_accessed=moved, transcendentals=0),
    )(*ins)


def lanes(index, size):
    return pl.ds(pl.multiple_of(index * size, size), size)


def cut_kernel(cn, at, decay, seg_len, *refs):
    weights, outs = refs[:3], refs[3:]
    w_rows = weights[0].shape[0]
    row = lax.broadcasted_iota(jnp.int32, (META, DH), 0)
    length = jnp.full((META, DH), seg_len[0], jnp.int32).astype(F32)
    for j, out in enumerate(outs):
        for e in range(cn):
            head = (at[0] ^ j) * cn + e
            rest = jnp.full((META, DH), decay[head], F32)
            for i, w in enumerate(weights):
                first = (e * 3 + i) * DH
                out[:w_rows, first : first + DH] = w[:, lanes(head, DH)]
                term = rest.astype(BF16).astype(F32)
                rest = rest - term
                out[w_rows:, first : first + DH] = jnp.where(row < META // 2, term, length).astype(BF16)


def norm_kernel(n_head, at, gain, *refs):
    parts, out = refs[:n_head], refs[n_head]
    feat = parts[0].shape[1]
    wide = [part[...].astype(F32) for part in parts]
    squares = sum(jnp.sum(w * w, axis=1, keepdims=True) for w in wide)
    inverse = lax.rsqrt(squares / (feat * n_head) + 1e-05)
    for k, w in enumerate(wide):
        half = lanes(lax.rem(at[3] + n_head - k, n_head), feat)
        out[:, half] = (w * inverse * gain[:, half]).astype(BF16)


def project(xn, cn, at, rows, weights, chunk, meta, each):
    x, c = at[1], at[2]
    w_rows = weights[0].shape[0] - META
    row = lax.broadcasted_iota(jnp.int32, (META, DH), 0)
    for n, w in enumerate(weights):
        xi, ci = lax.rem(x + xn - n // cn, xn), c ^ (n % cn)
        chunk[pl.ds(pl.multiple_of((xi * cn + ci) * w_rows, w_rows), w_rows), :] = w[:w_rows]
        tail = w[w_rows:].astype(F32)
        terms = tail[:, : 3 * DH]
        for e in range(1, cn):
            terms = jnp.where(c == e, tail[:, e * 3 * DH : (e + 1) * 3 * DH], terms)
        total = terms[:, :DH] + terms[:, DH : 2 * DH] + terms[:, 2 * DH :]
        meta[xi, ci] = jnp.where(row < META // 2, total, terms[:, :DH])
    for first in range(0, len(rows), 2):
        pair = range(first, min(first + 2, len(rows)))
        sums = dot(jnp.concatenate([rows[i][...] for i in pair]), chunk[...])
        for n, i in enumerate(pair):
            size = sums.shape[0] // len(pair)
            each(i, sums[n * size : (n + 1) * size])


def project_kernel(zn, xn, cn, steps, at, *refs):
    rows = refs[:zn]
    weights = refs[zn : zn + len(steps) * xn * cn]
    out, meta, chunk = refs[-3:]
    size = chunk.shape[1]
    for n, j in enumerate(steps):

        def each(i, sums):
            out[i] = sums if n == 0 else out[i] + sums

        part = [row.at[:, lanes(at[0] ^ j, size)] for row in rows]
        few = weights[n * xn * cn : (n + 1) * xn * cn]
        project(xn, cn, at, part, few, chunk.at[n], meta.at[j], each)


def finish_kernel(zn, xn, cn, at, *refs):
    rows = refs[:zn]
    weights = refs[zn : zn + xn * cn]
    before = refs[zn + xn * cn] if zn > 1 else None
    meta, chunk = refs[-2:]
    outs = refs[zn + xn * cn + (before is not None) : -2]
    c = at[2]

    def each(i, sums):
        sums = (sums if before is None else sums + before[i]).astype(BF16)
        heads = [sums[:, e * 3 * DH : (e + 1) * 3 * DH] for e in range(cn)]
        half = outs[0].shape[0]
        for m in range(cn):
            pick = heads[m]
            for e in range(cn):
                if e != m:
                    pick = jnp.where((c ^ m) == e, heads[e], pick)
            outs[i // half * cn + m][i % half] = pick

    project(xn, cn, at, rows, weights, chunk, meta.at[0], each)


def segment_info(table):
    def retain(zi, xi, ci):
        return table[zi, xi, ci, 0:1, 0:1]

    def length(zi, xi, ci):
        return table[zi, xi, ci, META // 2 : META // 2 + 1, 0:1]

    return retain, length


def write_kernel(zn, xn, cn, halves, at, *refs):
    count = cn * halves
    parts, query, metas = refs[:count], refs[count], refs[count + 1 : -5]
    sums, written, group, group16, table = refs[-5:]
    z, x, c = at[0], at[1], at[2]
    j = 0
    for meta in metas:
        for n in range(meta.shape[0]):
            table[z ^ j] = meta[n]
            j += 1
    retain, length = segment_info(table)
    seg_rows = sums.shape[2]
    half = zn // halves
    for i in range(zn):
        for m in range(cn):
            sums[z ^ i, c ^ m] = parts[i // half * cn + m][i % half]
    own = query[:, lanes(z * cn + c, DH)]
    slots = own.shape[0]
    position = lax.broadcasted_iota(jnp.int32, (slots, seg_rows), 1).astype(F32)
    for i in range(zn):
        keys = sums[i, :, :, DH : 2 * DH].reshape(cn * seg_rows, DH)
        scores = dot(own, keys, (1, 1)) * (1.0 / math.sqrt(DH))
        gates = jax.nn.sigmoid(scores - math.log(seg_rows))
        total = None
        for m in range(cn):
            gate = gates[:, m * seg_rows : (m + 1) * seg_rows]
            gate = jnp.where(position < length(i, x, m), gate, 0.0).astype(BF16)
            new = dot(gate, sums[i, m, :, DH:])
            written[i, m] = new
            total = new if total is None else retain(i, x, m) * total + new
        group[i] = total
        group16[i] = total.astype(BF16)


def token_kernel(zn, cn, slots, at, scale, table, sums, out):
    _, length = segment_info(table)
    seg_rows = sums.shape[2]
    shape = (seg_rows, seg_rows)
    row = lax.broadcasted_iota(jnp.int32, shape, 0)
    column = lax.broadcasted_iota(jnp.int32, shape, 1)
    factor = scale[at[0] * cn + at[2]] * (1.0 / math.sqrt(DH))
    for i in range(zn):
        for m in range(cn):
            query, keys, values = (sums[i, m, :, n * DH : (n + 1) * DH] for n in range(3))
            scores = dot(query, keys, (1, 1)) * factor
            gate = jax.nn.sigmoid(scores - math.log(slots + seg_rows))
            allowed = (column <= row) & (column.astype(F32) < length(i, at[1], m))
            out[i, m] = dot(jnp.where(allowed, gate, 0.0).astype(BF16), values)


def memory_kernel(zn, xn, cn, at, scale, table, sums, token, written, group, *refs):
    others = refs[: xn - 1]
    outs = refs[xn - 1 : xn - 1 + zn]
    groups, done = refs[-2:]
    z, x, c = at[0], at[1], at[2]
    retain, length = segment_info(table)
    slots, seg_rows = group.shape[1], sums.shape[2]
    factor = scale[z * cn + c] * (1.0 / math.sqrt(DH))
    bias = math.log(slots + seg_rows)
    row = lax.broadcasted_iota(jnp.int32, (seg_rows, DH), 0).astype(F32)
    groups[x] = group[...]
    for k, other in enumerate(others, 1):
        groups[lax.rem(x + xn - k, xn)] = other[...].astype(F32)
    memory = jnp.zeros(group.shape[1:], F32)
    for i in range(zn):
        entry = memory
        for k in range(xn):
            if k:
                entry = jnp.where(x == k, memory, entry)
            kept = retain(i, k, 0)
            for m in range(1, cn):
                kept = kept * retain(i, k, m)
            memory = kept * memory + groups[k, i]
        for m in range(cn):
            units = []
            for n in range(2):
                part = entry[:, n * DH : (n + 1) * DH]
                mean = jnp.mean(part * part, axis=1, keepdims=True)
                units.append((part * lax.rsqrt(mean + 1e-06)).astype(BF16))
            scores = dot(sums[i, m, :, :DH], units[0], (1, 1)) * factor
            gate = jax.nn.sigmoid(scores - bias).astype(BF16)
            total = dot(gate, units[1]) + token[i, m]
            done[i, m] = jnp.where(row < length(i, x, m), total, 0.0).astype(BF16)
            if m + 1 < cn:
                entry = retain(i, x, m) * entry + written[i, m]
    for j in range(zn):
        for m in range(cn):
            outs[j][m] = done[z ^ j, c ^ m]


def out_kernel(zn, xn, cn, n_head, slots, turns, phases, forms, at, *refs):
    attended = refs[: zn * cn]
    rest = iter(refs[zn * cn : -1])
    weights = [[next(rest) for _ in range(form)] for form in forms]
    outs, rows = list(rest), refs[-1]
    z, x, c, y = at[0], at[1], at[2], at[3]
    seg_rows = attended[0].shape[1]
    for j in range(zn):
        for e in range(cn):
            for m in range(cn):
                rows[m * seg_rows : (m + 1) * seg_rows, lanes((z ^ j) * cn + (c ^ e), DH)] = (
                    attended[j * cn + e][m ^ e]
                )
    blocks = outs[0].shape[0]
    share = zn * xn // n_head
    for n, j in enumerate(slots):
        for k in range(xn):
            spot = (z ^ j) * xn + lax.rem(x + xn - k, xn)
            turn = lax.rem(spot // share + n_head - y, n_head)
            for i, r in enumerate(turns):
                for e, weight in enumerate(weights[n * xn + k]):
                    here = turn == r
                    if len(weights[n * xn + k]) > 1:
                        here = here & (c == e)

                    @pl.when(here)
                    def _():
                        product = dot(rows[...], weight[...]).astype(BF16)
                        group = j % phases * len(turns) if len(slots) == zn else 0
                        for m in range(cn):
                            out = outs[(group + i) * cn + m]
                            out[lax.rem(spot, blocks)] = product[m * seg_rows : (m + 1) * seg_rows]


def sum_kernel(n_head, cn, phases, at, *refs):
    out = refs[-1]
    blocks, seg_rows, size = refs[0].shape
    for p in range(phases):
        count = (n_head - 1) * cn
        few = refs[(phases * (n_head - 1) + p) * cn :][:cn] + refs[p * count : (p + 1) * count]
        places = []
        for b in range(blocks):
            totals = [
                sum(few[r * cn + e][b].astype(F32) for r in range(n_head)).astype(BF16)
                for e in range(cn)
            ]
            for m in range(cn):
                total = totals[0]
                for e in range(1, cn):
                    total = jnp.where((at[2] ^ e) == m, totals[e], total)
                places.append(total)
        out[:, lanes(lax.rem(at[0] ^ p, phases), blocks * cn * size)] = jnp.concatenate(places, 1)


def body(tokens, gain, w_query, w_key, w_value, w_out, mem_query, score_scale, decay, seg_len):
    n_seq = lax.axis_size("seq")
    n_head = lax.axis_size("head")
    seg_rows, feat_local = tokens.shape
    width = gain.shape[0]
    w_rows, col_local = w_query.shape
    heads = col_local // DH
    slots = mem_query.shape[0]
    cn = 2 if heads % 2 == 0 else 1
    zn = heads // cn
    xn = n_seq // heads
    place = lax.axis_index("seq")
    y = lax.axis_index("head")
    at = jnp.stack([place // (cn * xn), place // cn % xn, place % cn, y]).astype(jnp.int32)

    def shape(dims, dtype=BF16):
        return jax.ShapeDtypeStruct(dims, dtype)

    def split(s):
        return s // (cn * xn), s // cn % xn, s % cn

    def join(a, b, d):
        return (a * xn + b) * cn + d

    def over_z(a, j):
        pairs = [(s, join(split(s)[0] ^ j, *split(s)[1:])) for s in range(n_seq)]
        return lax.ppermute(a, "seq", pairs)

    def over_x(a, k, cores=None):
        pairs = []
        for s in range(n_seq):
            sz, sx, sc = split(s)
            if cores is None or sc in cores:
                pairs.append((s, join(sz, (sx + k) % xn, sc)))
        return lax.ppermute(a, "seq", pairs)

    def over_c(a, m):
        return lax.ppermute(a, "seq", [(s, s ^ m) for s in range(n_seq)])

    def over_y(a, k):
        return lax.ppermute(a, "head", [(h, (h + k) % n_head) for h in range(n_head)])

    chain = []

    def mark(a):
        chain[:] = [a]
        return a

    def done(a):
        return mark(lax.optimization_barrier((a, *chain))[0])

    def done_all(*lists):
        flat = [part for parts in lists for part in parts]
        if flat:
            flat = lax.optimization_barrier((*flat, *chain))[: len(flat)]
            mark(flat[-1])
        flat = iter(flat)
        return [[next(flat) for _ in parts] for parts in lists]

    def after(a, b):
        return lax.optimization_barrier((a, b))[0]

    last = zn - 1
    tok, packs, pieces, rows = {0: tokens}, {}, {}, {}
    started, columns, out_z = {}, {}, {0: w_out}

    def begin_tok(j):
        low = j & -j
        if j < zn and j not in started and j ^ low in tok:
            started[j] = over_z(tok[j ^ low], low)

    def begin_y(j):
        started["y", j] = [over_y(tok[j], k) for k in range(1, n_head)]

    def end_y(j, others):
        (rows[j],) = call(
            functools.partial(norm_kernel, n_head),
            (at, gain[None], tok[j], *others),
            [shape((seg_rows, width))],
        )
        mark(rows[j])

    def both(a):
        return [over_c(a, m) if m else a for m in range(cn)]

    def begin_x(j):
        started["x", j] = [over_x(packs[j], k) for k in range(1, xn)]
        pieces[j] = both(packs[j])

    def end_x(j, others):
        for part in others:
            pieces[j] += both(part)

    def begin_out(j, source):
        started["o", j] = [over_x(source, k) for k in range(1, xn)]
        columns[j] = [source]

    def end_out(j):
        columns[j] += [done(part) for part in started["o", j]]

    for bit in range(zn.bit_length() - 2, -1, -1):
        begin_tok(1 << bit)
    begin_y(0)
    begin_out(0, w_out)
    sent = call(
        functools.partial(cut_kernel, cn),
        (at, decay[0], seg_len, w_query, w_key, w_value),
        [shape((w_rows + META, cn * 3 * DH))] * zn,
        scalars=3,
    )
    packs[0] = sent[0]
    begin_x(0)
    if last:
        started["w", 1] = over_z(sent[1], 1)

    bits = [1 << n for n in range(zn.bit_length() - 1)]
    more = [j for j in range(1, zn) if j not in bits]
    parts, first, whole = done_all([started[b] for b in bits], started["y", 0], started["x", 0])
    tok.update(zip(bits, parts))
    end_x(0, whole)
    for b in bits:
        begin_y(b)
    for j in more:
        begin_tok(j)
    early = range(1, min(3, zn))
    for j in early[1:]:
        started["w", j] = over_z(after(sent[j], tok[1]), j)
    end_y(0, first)
    if last:
        pieces[0] = done_all(pieces[0])[0]
    parts, far, columns[0][1:], *near = done_all(
        [started["w", j] for j in early],
        [started[j] for j in more],
        started["o", 0],
        *(started["y", b] for b in bits),
    )
    packs.update(zip(early, parts))
    tok.update(zip(more, far))
    for j in range(len(early) + 1, zn):
        started["w", j] = over_z(after(sent[j], packs[j - 1]), j)
    for j in more:
        begin_y(j)
    if last:
        begin_x(1)
        started["oz", 1] = over_z(after(w_out, packs[early[-1]]), 1)
    for b, others in zip(bits, near):
        end_y(b, others)
    for j in early[1:]:
        packs[j] = lax.optimization_barrier((packs[j], *(rows[b] for b in bits)))[0]
        begin_x(j)
    for j in range(len(early) + 1, zn):
        packs[j] = done(started["w", j])
        begin_x(j)
    for b in bits[1:]:
        started["oz", b] = over_z(after(w_out, packs[last]), b)
    for j in more:
        end_y(j, done_all(started["y", j])[0])
    if last:
        out_z[1] = done(started["oz", 1])
        begin_out(1, out_z[1])
    for j in range(1, last):
        end_x(j, done_all(started["x", j])[0])
    rows = [rows[j] for j in range(zn)]

    chunk_rows = xn * cn * w_rows
    flops = 2 * zn * seg_rows * chunk_rows * cn * 3 * DH
    before = []
    if last:
        before = call(
            functools.partial(project_kernel, zn, xn, cn, range(last)[::-1]),
            (at, *rows, *sum((pieces[j] for j in range(last)[::-1]), [])),
            [
                shape((zn, seg_rows, cn * 3 * DH), F32),
                shape((last, xn, cn, META, DH), F32),
            ],
            [pltpu.VMEM((last, chunk_rows, cn * 3 * DH), BF16)],
            flops * last,
            room=30,
        )
        mark(before[0])
    if last:
        parts, others, columns[1][1:] = done_all(
            [started["oz", b] for b in bits[1:]], started["x", last], started["o", 1]
        )
        end_x(last, others)
        out_z.update(zip(bits[1:], parts))
        for b in bits[1:]:
            columns[b] = [out_z[b]]
            started["o", b] = [
                over_x(out_z[b], k, (e,)) for e in reversed(range(cn)) for k in range(1, xn)
            ]
        for j in more:
            started["oz", j] = over_z(out_z[j ^ (j & -j)], j & -j)
    halves = 2 if zn % 2 == 0 else 1
    *parts, meta = call(
        functools.partial(finish_kernel, zn, xn, cn),
        (at, *rows, *pieces[last], *before[:1]),
        [shape((zn // halves, seg_rows, 3 * DH))] * (cn * halves)
        + [shape((1, xn, cn, META, DH), F32)],
        [pltpu.VMEM((chunk_rows, cn * 3 * DH), BF16)],
        flops,
        column=(chunk_rows, lambda at: at[0] ^ last),
        room=20,
    )
    parts = [over_c(part, n % cn) if n % cn else part for n, part in enumerate(parts)]
    (parts,) = done_all(parts)
    sums, written, group, group16, table = call(
        functools.partial(write_kernel, zn, xn, cn, halves),
        (at, *parts, mem_query, *before[1:], meta),
        [
            shape((zn, cn, seg_rows, 3 * DH)),
            shape((zn, cn, slots, 2 * DH), F32),
            shape((zn, slots, 2 * DH), F32),
            shape((zn, slots, 2 * DH)),
            shape((zn, xn, cn, META, DH), F32),
        ],
    )
    others = [over_x(group16, k) for k in range(1, xn)]
    (token,) = call(
        functools.partial(token_kernel, zn, cn, slots),
        (at, score_scale, table, sums),
        [shape((zn, cn, seg_rows, DH), F32)],
        scalars=2,
    )
    mark(token)
    count = xn - 1
    others, parts, *early_x = done_all(
        others, [started["oz", j] for j in more], *(started["o", b][:count] for b in bits[1:])
    )
    for j, part in zip(more, parts):
        begin_out(j, part)
    attended = call(
        functools.partial(memory_kernel, zn, xn, cn),
        (at, score_scale, table, sums, token, written, group, *others),
        [shape((cn, seg_rows, DH))] * zn,
        [
            pltpu.VMEM((xn, zn, slots, 2 * DH), F32),
            pltpu.VMEM((zn, cn, seg_rows, DH), BF16),
        ],
        scalars=2,
    )

    here = [over_z(block, j) if j else block for j, block in enumerate(attended)]
    for j in reversed(range(1, zn)):
        here[j] = done(here[j])
    for b, ready in zip(bits[1:], early_x):
        ready = ready + done_all(started["o", b][count:])[0]
        columns[b] += [ready[k::count][::-1] for k in range(count)]
    swapped = [[over_c(here[j], m) for m in range(1, cn)] for j in range(zn)]
    here = sum(([here[j]] + [done(a) for a in swapped[j]] for j in range(zn)), [])

    for j in more:
        end_out(j)
    out_cols = w_out.shape[1]
    phases = zn // n_head if zn % n_head == 0 else 1
    blocks = feat_local // (cn * out_cols * phases)
    def multiply(few, turns, outs):
        arrays = sum((columns[j] for j in few), [])
        arrays = [a if isinstance(a, list) else [a] for a in arrays]
        forms = tuple(len(a) for a in arrays)
        return call(
            functools.partial(out_kernel, zn, xn, cn, n_head, few, turns, phases, forms),
            (at, *here, *sum(arrays, [])),
            [shape((blocks, seg_rows, out_cols))] * outs,
            [pltpu.VMEM((cn * seg_rows, heads * DH), BF16)],
            2 * cn * seg_rows * heads * DH * len(few) * xn * out_cols,
            room=20,
        )

    mine = []
    others = range(1, n_head)
    for p in range(phases):
        products = multiply(range(p, zn, phases), others, cn * len(others))
        for n, block in enumerate(products):
            block = over_c(block, n % cn) if n % cn else block
            mine.append(over_y(block, others[n // cn]))
    products = multiply(range(zn), (0,), cn * phases)
    for n, block in enumerate(products):
        mine.append(over_c(block, n % cn) if n % cn else block)
    (branch,) = call(
        functools.partial(sum_kernel, n_head, cn, phases),
        (at, *mine),
        [shape((seg_rows, feat_local))],
    )
    return branch


def solution(mesh):
    return jax.shard_map(
        body,
        mesh=mesh,
        in_specs=(
            P("seq", "head"),
            P(),
            P("seq", "head"),
            P("seq", "head"),
            P("seq", "head"),
            P("head", "seq"),
            P(None, "head"),
            P("head"),
            P("seq", "head"),
            P("seq"),
        ),
        out_specs=P("seq", "head"),
        check_vma=False,
    )
```

```python
import functools
import math

import jax
import jax.numpy as jnp
from jax import lax
from jax.experimental import pallas as pl
from jax.experimental.pallas import tpu as pltpu
from jax.sharding import PartitionSpec as P

DH = 128
META = 16
F32 = jnp.float32
BF16 = jnp.bfloat16


def dot(a, b, contract=(1, 0)):
    dims = (((contract[0],), (contract[1],)), ((), ()))
    return lax.dot_general(a, b, dims, preferred_element_type=F32)


def call(kernel, ins, outs, scratch=(), flops=0, scalars=1, column=None, room=12):
    moved = sum(math.prod(a.shape) * a.dtype.itemsize for a in (*ins, *outs))

    def whole(a):
        return pl.BlockSpec(a.shape, lambda i, *_: (0,) * len(a.shape))

    def spec(a):
        if column and a.shape[-1] > column[0] and a.ndim == 2 and a.dtype == BF16:
            pick = column[1]
            return pl.BlockSpec((a.shape[0], column[0]), lambda i, at, *_: (0, pick(at)))
        return whole(a)

    return pl.pallas_call(
        kernel,
        grid_spec=pltpu.PrefetchScalarGridSpec(
            num_scalar_prefetch=scalars,
            grid=(1,),
            in_specs=[spec(a) for a in ins[scalars:]],
            out_specs=[whole(a) for a in outs],
            scratch_shapes=scratch,
        ),
        out_shape=outs,
        compiler_params=pltpu.CompilerParams(vmem_limit_bytes=room * 2**20),
        cost_estimate=pl.CostEstimate(flops=flops, bytes_accessed=moved, transcendentals=0),
    )(*ins)


def lanes(index, size):
    return pl.ds(pl.multiple_of(index * size, size), size)


def cut_kernel(cn, at, decay, seg_len, *refs):
    weights, outs = refs[:3], refs[3:]
    w_rows = weights[0].shape[0]
    row = lax.broadcasted_iota(jnp.int32, (META, DH), 0)
    length = jnp.full((META, DH), seg_len[0], jnp.int32).astype(F32)
    for j, out in enumerate(outs):
        for e in range(cn):
            head = (at[0] ^ j) * cn + e
            rest = jnp.full((META, DH), decay[head], F32)
            for i, w in enumerate(weights):
                first = (e * 3 + i) * DH
                out[:w_rows, first : first + DH] = w[:, lanes(head, DH)]
                term = rest.astype(BF16).astype(F32)
                rest = rest - term
                out[w_rows:, first : first + DH] = jnp.where(row < META // 2, term, length).astype(BF16)


def norm_kernel(n_head, at, gain, *refs):
    parts, out = refs[:n_head], refs[n_head]
    feat = parts[0].shape[1]
    wide = [part[...].astype(F32) for part in parts]
    squares = sum(jnp.sum(w * w, axis=1, keepdims=True) for w in wide)
    inverse = lax.rsqrt(squares / (feat * n_head) + 1e-05)
    for k, w in enumerate(wide):
        half = lanes(lax.rem(at[3] + n_head - k, n_head), feat)
        out[:, half] = (w * inverse * gain[:, half]).astype(BF16)


def project(xn, cn, at, rows, weights, chunk, meta, each):
    x, c = at[1], at[2]
    w_rows = weights[0].shape[0] - META
    row = lax.broadcasted_iota(jnp.int32, (META, DH), 0)
    for n, w in enumerate(weights):
        xi, ci = lax.rem(x + xn - n // cn, xn), c ^ (n % cn)
        chunk[pl.ds(pl.multiple_of((xi * cn + ci) * w_rows, w_rows), w_rows), :] = w[:w_rows]
        tail = w[w_rows:].astype(F32)
        terms = tail[:, : 3 * DH]
        for e in range(1, cn):
            terms = jnp.where(c == e, tail[:, e * 3 * DH : (e + 1) * 3 * DH], terms)
        total = terms[:, :DH] + terms[:, DH : 2 * DH] + terms[:, 2 * DH :]
        meta[xi, ci] = jnp.where(row < META // 2, total, terms[:, :DH])
    for first in range(0, len(rows), 2):
        pair = range(first, min(first + 2, len(rows)))
        sums = dot(jnp.concatenate([rows[i][...] for i in pair]), chunk[...])
        for n, i in enumerate(pair):
            size = sums.shape[0] // len(pair)
            each(i, sums[n * size : (n + 1) * size])


def project_kernel(zn, xn, cn, steps, at, *refs):
    rows = refs[:zn]
    weights = refs[zn : zn + len(steps) * xn * cn]
    out, meta, chunk = refs[-3:]
    size = chunk.shape[1]
    for n, j in enumerate(steps):

        def each(i, sums):
            out[i] = sums if n == 0 else out[i] + sums

        part = [row.at[:, lanes(at[0] ^ j, size)] for row in rows]
        few = weights[n * xn * cn : (n + 1) * xn * cn]
        project(xn, cn, at, part, few, chunk.at[n], meta.at[j], each)


def finish_kernel(zn, xn, cn, at, *refs):
    rows = refs[:zn]
    weights = refs[zn : zn + xn * cn]
    before = refs[zn + xn * cn] if zn > 1 else None
    meta, chunk = refs[-2:]
    outs = refs[zn + xn * cn + (before is not None) : -2]
    c = at[2]

    def each(i, sums):
        sums = (sums if before is None else sums + before[i]).astype(BF16)
        heads = [sums[:, e * 3 * DH : (e + 1) * 3 * DH] for e in range(cn)]
        half = outs[0].shape[0]
        for m in range(cn):
            pick = heads[m]
            for e in range(cn):
                if e != m:
                    pick = jnp.where((c ^ m) == e, heads[e], pick)
            outs[i // half * cn + m][i % half] = pick

    project(xn, cn, at, rows, weights, chunk, meta.at[0], each)


def segment_info(table):
    def retain(zi, xi, ci):
        return table[zi, xi, ci, 0:1, 0:1]

    def length(zi, xi, ci):
        return table[zi, xi, ci, META // 2 : META // 2 + 1, 0:1]

    return retain, length


def write_kernel(zn, xn, cn, halves, at, *refs):
    count = cn * halves
    parts, query, metas = refs[:count], refs[count], refs[count + 1 : -5]
    sums, written, group, group16, table = refs[-5:]
    z, x, c = at[0], at[1], at[2]
    j = 0
    for meta in metas:
        for n in range(meta.shape[0]):
            table[z ^ j] = meta[n]
            j += 1
    retain, length = segment_info(table)
    seg_rows = sums.shape[2]
    half = zn // halves
    for i in range(zn):
        for m in range(cn):
            sums[z ^ i, c ^ m] = parts[i // half * cn + m][i % half]
    own = query[:, lanes(z * cn + c, DH)]
    slots = own.shape[0]
    position = lax.broadcasted_iota(jnp.int32, (slots, seg_rows), 1).astype(F32)
    for i in range(zn):
        keys = sums[i, :, :, DH : 2 * DH].reshape(cn * seg_rows, DH)
        scores = dot(own, keys, (1, 1)) * (1.0 / math.sqrt(DH))
        gates = jax.nn.sigmoid(scores - math.log(seg_rows))
        total = None
        for m in range(cn):
            gate = gates[:, m * seg_rows : (m + 1) * seg_rows]
            gate = jnp.where(position < length(i, x, m), gate, 0.0).astype(BF16)
            new = dot(gate, sums[i, m, :, DH:])
            written[i, m] = new
            total = new if total is None else retain(i, x, m) * total + new
        group[i] = total
        group16[i] = total.astype(BF16)


def token_kernel(zn, cn, slots, at, scale, table, sums, out):
    _, length = segment_info(table)
    seg_rows = sums.shape[2]
    shape = (seg_rows, seg_rows)
    row = lax.broadcasted_iota(jnp.int32, shape, 0)
    column = lax.broadcasted_iota(jnp.int32, shape, 1)
    factor = scale[at[0] * cn + at[2]] * (1.0 / math.sqrt(DH))
    for i in range(zn):
        for m in range(cn):
            query, keys, values = (sums[i, m, :, n * DH : (n + 1) * DH] for n in range(3))
            scores = dot(query, keys, (1, 1)) * factor
            gate = jax.nn.sigmoid(scores - math.log(slots + seg_rows))
            allowed = (column <= row) & (column.astype(F32) < length(i, at[1], m))
            out[i, m] = dot(jnp.where(allowed, gate, 0.0).astype(BF16), values)


def memory_kernel(zn, xn, cn, at, scale, table, sums, token, written, group, *refs):
    others = refs[: xn - 1]
    outs = refs[xn - 1 : xn - 1 + zn]
    groups, done = refs[-2:]
    z, x, c = at[0], at[1], at[2]
    retain, length = segment_info(table)
    slots, seg_rows = group.shape[1], sums.shape[2]
    factor = scale[z * cn + c] * (1.0 / math.sqrt(DH))
    bias = math.log(slots + seg_rows)
    row = lax.broadcasted_iota(jnp.int32, (seg_rows, DH), 0).astype(F32)
    groups[x] = group[...]
    for k, other in enumerate(others, 1):
        groups[lax.rem(x + xn - k, xn)] = other[...].astype(F32)
    memory = jnp.zeros(group.shape[1:], F32)
    for i in range(zn):
        entry = memory
        for k in range(xn):
            if k:
                entry = jnp.where(x == k, memory, entry)
            kept = retain(i, k, 0)
            for m in range(1, cn):
                kept = kept * retain(i, k, m)
            memory = kept * memory + groups[k, i]
        for m in range(cn):
            units = []
            for n in range(2):
                part = entry[:, n * DH : (n + 1) * DH]
                mean = jnp.mean(part * part, axis=1, keepdims=True)
                units.append((part * lax.rsqrt(mean + 1e-06)).astype(BF16))
            scores = dot(sums[i, m, :, :DH], units[0], (1, 1)) * factor
            gate = jax.nn.sigmoid(scores - bias).astype(BF16)
            total = dot(gate, units[1]) + token[i, m]
            done[i, m] = jnp.where(row < length(i, x, m), total, 0.0).astype(BF16)
            if m + 1 < cn:
                entry = retain(i, x, m) * entry + written[i, m]
    for j in range(zn):
        for m in range(cn):
            outs[j][m] = done[z ^ j, c ^ m]


def out_kernel(zn, xn, cn, n_head, slots, turns, phases, forms, at, *refs):
    attended = refs[: zn * cn]
    rest = iter(refs[zn * cn : -1])
    weights = [[next(rest) for _ in range(form)] for form in forms]
    outs, rows = list(rest), refs[-1]
    z, x, c, y = at[0], at[1], at[2], at[3]
    seg_rows = attended[0].shape[1]
    for j in range(zn):
        for e in range(cn):
            for m in range(cn):
                rows[m * seg_rows : (m + 1) * seg_rows, lanes((z ^ j) * cn + (c ^ e), DH)] = (
                    attended[j * cn + e][m ^ e]
                )
    blocks = outs[0].shape[0]
    share = zn * xn // n_head
    for n, j in enumerate(slots):
        for k in range(xn):
            spot = (z ^ j) * xn + lax.rem(x + xn - k, xn)
            turn = lax.rem(spot // share + n_head - y, n_head)
            for i, r in enumerate(turns):
                for e, weight in enumerate(weights[n * xn + k]):
                    here = turn == r
                    if len(weights[n * xn + k]) > 1:
                        here = here & (c == e)

                    @pl.when(here)
                    def _():
                        product = dot(rows[...], weight[...]).astype(BF16)
                        group = j % phases * len(turns) if len(slots) == zn else 0
                        for m in range(cn):
                            out = outs[(group + i) * cn + m]
                            out[lax.rem(spot, blocks)] = product[m * seg_rows : (m + 1) * seg_rows]


def sum_kernel(n_head, cn, phases, at, *refs):
    out = refs[-1]
    blocks, seg_rows, size = refs[0].shape
    for p in range(phases):
        count = (n_head - 1) * cn
        few = refs[(phases * (n_head - 1) + p) * cn :][:cn] + refs[p * count : (p + 1) * count]
        places = []
        for b in range(blocks):
            totals = [
                sum(few[r * cn + e][b].astype(F32) for r in range(n_head)).astype(BF16)
                for e in range(cn)
            ]
            for m in range(cn):
                total = totals[0]
                for e in range(1, cn):
                    total = jnp.where((at[2] ^ e) == m, totals[e], total)
                places.append(total)
        out[:, lanes(lax.rem(at[0] ^ p, phases), blocks * cn * size)] = jnp.concatenate(places, 1)


def body(tokens, gain, w_query, w_key, w_value, w_out, mem_query, score_scale, decay, seg_len):
    n_seq = lax.axis_size("seq")
    n_head = lax.axis_size("head")
    seg_rows, feat_local = tokens.shape
    width = gain.shape[0]
    w_rows, col_local = w_query.shape
    heads = col_local // DH
    slots = mem_query.shape[0]
    cn = 2 if heads % 2 == 0 else 1
    zn = heads // cn
    xn = n_seq // heads
    place = lax.axis_index("seq")
    y = lax.axis_index("head")
    at = jnp.stack([place // (cn * xn), place // cn % xn, place % cn, y]).astype(jnp.int32)

    def shape(dims, dtype=BF16):
        return jax.ShapeDtypeStruct(dims, dtype)

    def split(s):
        return s // (cn * xn), s // cn % xn, s % cn

    def join(a, b, d):
        return (a * xn + b) * cn + d

    def over_z(a, j):
        pairs = [(s, join(split(s)[0] ^ j, *split(s)[1:])) for s in range(n_seq)]
        return lax.ppermute(a, "seq", pairs)

    def over_x(a, k, cores=None):
        pairs = []
        for s in range(n_seq):
            sz, sx, sc = split(s)
            if cores is None or sc in cores:
                pairs.append((s, join(sz, (sx + k) % xn, sc)))
        return lax.ppermute(a, "seq", pairs)

    def over_c(a, m):
        return lax.ppermute(a, "seq", [(s, s ^ m) for s in range(n_seq)])

    def over_y(a, k):
        return lax.ppermute(a, "head", [(h, (h + k) % n_head) for h in range(n_head)])

    chain = []

    def mark(a):
        chain[:] = [a]
        return a

    def done(a):
        return mark(lax.optimization_barrier((a, *chain))[0])

    def done_all(*lists):
        flat = [part for parts in lists for part in parts]
        if flat:
            flat = lax.optimization_barrier((*flat, *chain))[: len(flat)]
            mark(flat[-1])
        flat = iter(flat)
        return [[next(flat) for _ in parts] for parts in lists]

    def after(a, b):
        return lax.optimization_barrier((a, b))[0]

    last = zn - 1
    tok, packs, pieces, rows = {0: tokens}, {}, {}, {}
    started, columns, out_z = {}, {}, {0: w_out}

    def begin_tok(j):
        low = j & -j
        if j < zn and j not in started and j ^ low in tok:
            started[j] = over_z(tok[j ^ low], low)

    def begin_y(j):
        started["y", j] = [over_y(tok[j], k) for k in range(1, n_head)]

    def end_y(j, others):
        (rows[j],) = call(
            functools.partial(norm_kernel, n_head),
            (at, gain[None], tok[j], *others),
            [shape((seg_rows, width))],
        )
        mark(rows[j])

    def both(a):
        return [over_c(a, m) if m else a for m in range(cn)]

    def begin_x(j):
        started["x", j] = [over_x(packs[j], k) for k in range(1, xn)]
        pieces[j] = both(packs[j])

    def end_x(j, others):
        for part in others:
            pieces[j] += both(part)

    def begin_out(j, source):
        started["o", j] = [over_x(source, k) for k in range(1, xn)]
        columns[j] = [source]

    def end_out(j):
        columns[j] += [done(part) for part in started["o", j]]

    for bit in range(zn.bit_length() - 2, -1, -1):
        begin_tok(1 << bit)
    begin_y(0)
    begin_out(0, w_out)
    sent = call(
        functools.partial(cut_kernel, cn),
        (at, decay[0], seg_len, w_query, w_key, w_value),
        [shape((w_rows + META, cn * 3 * DH))] * zn,
        scalars=3,
        room=60,
    )
    packs[0] = sent[0]
    begin_x(0)
    if last:
        started["w", 1] = over_z(sent[1], 1)

    bits = [1 << n for n in range(zn.bit_length() - 1)]
    more = [j for j in range(1, zn) if j not in bits]
    parts, first, whole = done_all([started[b] for b in bits], started["y", 0], started["x", 0])
    tok.update(zip(bits, parts))
    end_x(0, whole)
    for b in bits:
        begin_y(b)
    for j in more:
        begin_tok(j)
    early = range(1, min(3, zn))
    for j in early[1:]:
        started["w", j] = over_z(after(sent[j], tok[1]), j)
    end_y(0, first)
    if last:
        pieces[0] = done_all(pieces[0])[0]
    parts, far, columns[0][1:], *near = done_all(
        [started["w", j] for j in early],
        [started[j] for j in more],
        started["o", 0],
        *(started["y", b] for b in bits),
    )
    packs.update(zip(early, parts))
    tok.update(zip(more, far))
    for j in range(len(early) + 1, zn):
        started["w", j] = over_z(after(sent[j], packs[j - 1]), j)
    for j in more:
        begin_y(j)
    if last:
        begin_x(1)
        started["oz", 1] = over_z(after(w_out, packs[early[-1]]), 1)
    for b, others in zip(bits, near):
        end_y(b, others)
    for j in early[1:]:
        packs[j] = lax.optimization_barrier((packs[j], *(rows[b] for b in bits)))[0]
        begin_x(j)
    for j in range(len(early) + 1, zn):
        packs[j] = done(started["w", j])
        begin_x(j)
    for b in bits[1:]:
        started["oz", b] = over_z(after(w_out, packs[last]), b)
    for j in more:
        end_y(j, done_all(started["y", j])[0])
    if last:
        out_z[1] = done(started["oz", 1])
        begin_out(1, out_z[1])
    for j in range(1, last):
        end_x(j, done_all(started["x", j])[0])
    rows = [rows[j] for j in range(zn)]

    chunk_rows = xn * cn * w_rows
    flops = 2 * zn * seg_rows * chunk_rows * cn * 3 * DH
    before = []
    if last:
        before = call(
            functools.partial(project_kernel, zn, xn, cn, range(last)[::-1]),
            (at, *rows, *sum((pieces[j] for j in range(last)[::-1]), [])),
            [
                shape((zn, seg_rows, cn * 3 * DH), F32),
                shape((last, xn, cn, META, DH), F32),
            ],
            [pltpu.VMEM((last, chunk_rows, cn * 3 * DH), BF16)],
            flops * last,
            room=30,
        )
        mark(before[0])
    if last:
        parts, others, columns[1][1:] = done_all(
            [started["oz", b] for b in bits[1:]], started["x", last], started["o", 1]
        )
        end_x(last, others)
        out_z.update(zip(bits[1:], parts))
        for b in bits[1:]:
            columns[b] = [out_z[b]]
            started["o", b] = [
                over_x(out_z[b], k, (e,)) for e in reversed(range(cn)) for k in range(1, xn)
            ]
        for j in more:
            started["oz", j] = over_z(out_z[j ^ (j & -j)], j & -j)
    halves = 2 if zn % 2 == 0 else 1
    *parts, meta = call(
        functools.partial(finish_kernel, zn, xn, cn),
        (at, *rows, *pieces[last], *before[:1]),
        [shape((zn // halves, seg_rows, 3 * DH))] * (cn * halves)
        + [shape((1, xn, cn, META, DH), F32)],
        [pltpu.VMEM((chunk_rows, cn * 3 * DH), BF16)],
        flops,
        column=(chunk_rows, lambda at: at[0] ^ last),
        room=20,
    )
    parts = [over_c(part, n % cn) if n % cn else part for n, part in enumerate(parts)]
    (parts,) = done_all(parts)
    sums, written, group, group16, table = call(
        functools.partial(write_kernel, zn, xn, cn, halves),
        (at, *parts, mem_query, *before[1:], meta),
        [
            shape((zn, cn, seg_rows, 3 * DH)),
            shape((zn, cn, slots, 2 * DH), F32),
            shape((zn, slots, 2 * DH), F32),
            shape((zn, slots, 2 * DH)),
            shape((zn, xn, cn, META, DH), F32),
        ],
    )
    others = [over_x(group16, k) for k in range(1, xn)]
    (token,) = call(
        functools.partial(token_kernel, zn, cn, slots),
        (at, score_scale, table, sums),
        [shape((zn, cn, seg_rows, DH), F32)],
        scalars=2,
    )
    mark(token)
    count = xn - 1
    others, parts, *early_x = done_all(
        others, [started["oz", j] for j in more], *(started["o", b][:count] for b in bits[1:])
    )
    for j, part in zip(more, parts):
        begin_out(j, part)
    attended = call(
        functools.partial(memory_kernel, zn, xn, cn),
        (at, score_scale, table, sums, token, written, group, *others),
        [shape((cn, seg_rows, DH))] * zn,
        [
            pltpu.VMEM((xn, zn, slots, 2 * DH), F32),
            pltpu.VMEM((zn, cn, seg_rows, DH), BF16),
        ],
        scalars=2,
    )

    here = [over_z(block, j) if j else block for j, block in enumerate(attended)]
    for j in reversed(range(1, zn)):
        here[j] = done(here[j])
    for b, ready in zip(bits[1:], early_x):
        ready = ready + done_all(started["o", b][count:])[0]
        columns[b] += [ready[k::count][::-1] for k in range(count)]
    swapped = [[over_c(here[j], m) for m in range(1, cn)] for j in range(zn)]
    here = sum(([here[j]] + [done(a) for a in swapped[j]] for j in range(zn)), [])

    for j in more:
        end_out(j)
    out_cols = w_out.shape[1]
    phases = zn // n_head if zn % n_head == 0 else 1
    blocks = feat_local // (cn * out_cols * phases)
    def multiply(few, turns, outs):
        arrays = sum((columns[j] for j in few), [])
        arrays = [a if isinstance(a, list) else [a] for a in arrays]
        forms = tuple(len(a) for a in arrays)
        return call(
            functools.partial(out_kernel, zn, xn, cn, n_head, few, turns, phases, forms),
            (at, *here, *sum(arrays, [])),
            [shape((blocks, seg_rows, out_cols))] * outs,
            [pltpu.VMEM((cn * seg_rows, heads * DH), BF16)],
            2 * cn * seg_rows * heads * DH * len(few) * xn * out_cols,
            room=20,
        )

    mine = []
    others = range(1, n_head)
    for p in range(phases):
        products = multiply(range(p, zn, phases), others, cn * len(others))
        for n, block in enumerate(products):
            block = over_c(block, n % cn) if n % cn else block
            mine.append(over_y(block, others[n // cn]))
    products = multiply(range(zn), (0,), cn * phases)
    for n, block in enumerate(products):
        mine.append(over_c(block, n % cn) if n % cn else block)
    (branch,) = call(
        functools.partial(sum_kernel, n_head, cn, phases),
        (at, *mine),
        [shape((seg_rows, feat_local))],
    )
    return branch


def solution(mesh):
    return jax.shard_map(
        body,
        mesh=mesh,
        in_specs=(
            P("seq", "head"),
            P(),
            P("seq", "head"),
            P("seq", "head"),
            P("seq", "head"),
            P("head", "seq"),
            P(None, "head"),
            P("head"),
            P("seq", "head"),
            P("seq"),
        ),
        out_specs=P("seq", "head"),
        check_vma=False,
    )
```
